32 devices in a mesh: gx: 4 (over y, core), gy: 8 (over z, x).
Axes of the slice: x: 2, y: 2, z: 4, core: 2. Of those that a mesh axis runs over, the one named last changes fastest.
Arguments:
- reference_image: bfloat16 [64, 64, 1024], P(None, 'gx', 'gy'), may hold values from -8 to 8
- deformed_image: bfloat16 [64, 64, 1024], P(None, 'gx', 'gy'), may hold values from -8 to 8
- route: int32 [4, 8, 32, 1], P('gx', 'gy'), may hold values from 0 to 4; in each aligned block of 32 rows (0 to 31, 32 to 63, ..., all dimensions but the last counted through in order) at most 8 rows name the same one
- within: int32 [4, 8, 32], P('gx', 'gy'), may hold values from 0 to 7
- xshift: int32 [4, 8, 32], P('gx', 'gy'), may hold values from 0 to 2
- fractions: int32 [4, 8, 32, 3], P('gx', 'gy'), may hold values from 0 to 15
Outputs:
- increment: float32 [3, 5, 4, 64], P(None, None, 'gx', 'gy')
- mismatch: float32 [64, 64, 1024], P(None, 'gx', 'gy')
The draws below stay inside these ranges and needn't reach their ends.
Inputs may be any that keep to these rules, and one draw needn't show every extreme that they name: `route`: among the 32 rows of one device (aligned blocks of rows along the first three dimensions taken together) no value occurs more than 8 times, and some value occurs exactly 8 times.
All inputs are finite; a program needn't handle non-finite values.
Results may differ from the reference program's by a relative error of at most 0.0006.
Values may be sent and summed in bfloat16 or wider, within the bound.
No kernel may reach another device: no remote copies, remote signals or barrier semaphores. Data moves between devices by JAX's collectives and lax.ppermute only.
A program may use at most 64 MiB of HBM per device.

```python
import math
import jax
import jax.numpy as jnp
import numpy as np
from jax import lax

EDGE = 16
EZ = 4
EXD = 1
EYD = 8
SPAN = 2
ITERS = 3
NEL = 32
CAP = 8
VOL = 4096
EX = 4
EY = 64
NZV = 64
NXV = 64
NYV = 1024
N_GX = 4
N_GY = 8


def wave_sum(key, amplitudes, periods):
    phases = jax.random.uniform(key, (3,), jnp.float32, 0.0, 2.0 * math.pi)
    depth_axis = jnp.arange(NZV, dtype=jnp.float32)[:, None, None]
    across = jnp.arange(NXV, dtype=jnp.float32)[None, :, None]
    height = jnp.arange(NYV, dtype=jnp.float32)[None, None, :]
    banding = amplitudes[0] * jnp.sin(2.0 * math.pi * depth_axis / periods[0] + phases[0])
    banding = banding + amplitudes[1] * jnp.sin(2.0 * math.pi * across / periods[1] + phases[1])
    return banding + amplitudes[2] * jnp.sin(2.0 * math.pi * height / periods[2] + phases[2])


def draw_reference_image(key, part):
    texture_key, phase_key = jax.random.split(jax.random.fold_in(key, 11))
    texture = jnp.clip(jax.random.normal(texture_key, (NZV, NXV, NYV), jnp.float32), -4.0, 4.0)
    banding = wave_sum(phase_key, (0.8, 1.2, 1.2), (24.0, 40.0, 56.0))
    return (texture + banding).astype(jnp.bfloat16)


def draw_deformed_image(key, part):
    texture_key, phase_key = jax.random.split(jax.random.fold_in(key, 23))
    texture = jnp.clip(jax.random.normal(texture_key, (NZV, NXV, NYV), jnp.float32), -4.0, 4.0)
    banding = wave_sum(phase_key, (0.6, 1.0, 1.5), (30.0, 52.0, 44.0))
    return (texture + banding).astype(jnp.bfloat16)


def plant(values, key, least, largest):
    spot = [jax.random.randint(jax.random.fold_in(key, axis), (), 0, length) for axis, length in enumerate(values.shape)]
    main_axis = values.shape.index(max(values.shape))
    beside = spot[:main_axis] + [(spot[main_axis] + 1) % values.shape[main_axis]] + spot[main_axis + 1:]
    return values.at[tuple(spot)].set(least).at[tuple(beside)].set(largest)


def routed_block(stream_key, own, number, rows, amount, top, most, slope):
    sequence = jax.random.permutation(stream_key, amount)
    heavy_load, common = shares(amount, rows * top, most, slope, True), shares(amount, rows * top, most, slope, False)
    places = jnp.arange(amount)

    def named(sizes, turn):
        used = int((sizes > 0).sum())
        fixed = max(1, used // 4)
        passed = fixed + (places - fixed + turn * (used - fixed)) % max(1, amount - fixed)
        return jnp.zeros((amount,), jnp.int32).at[sequence[jnp.where(places < fixed, places, passed)]].set(jnp.asarray(sizes, jnp.int32))

    sizes = jnp.where(number % 4 == 0, named(heavy_load, number // 4), named(common, number - number // 4 - 1))
    mixed = jax.random.permutation(jax.random.fold_in(own, 3), amount)
    source_of, taker = mixed[0:amount // 2 * 2:2], mixed[1:amount // 2 * 2:2]
    room = jnp.minimum(sizes[source_of] - 1, most - sizes[taker]) // 2
    room = jnp.where((source_of == sequence[0]) | (taker == sequence[0]) | (sizes[taker] == 0), 0, jnp.maximum(room, 0))
    passed = jax.random.randint(jax.random.fold_in(own, 4), (amount // 2,), 0, 1 << 20) % (room + 1)
    sizes = sizes.at[source_of].add(-passed).at[taker].add(passed)
    members = jnp.searchsorted(jnp.cumsum(sizes), jnp.arange(rows * top), side="right").astype(jnp.int32)
    grid = members.reshape(top, rows).T
    grid = grid[jax.random.permutation(jax.random.fold_in(own, 1), rows)]
    turn = jax.random.randint(jax.random.fold_in(own, 2), (rows, 1), 0, top)
    return jnp.take_along_axis(grid, (jnp.arange(top)[None, :] + turn) % top, axis=1)


def shares(count, total, most, skew, full):
    weights = [(1 << 20) // math.isqrt(standing ** skew) + 1 for standing in range(1, count + 1)]
    largest = most if full else min(most, max(-(-total // count), total * weights[0] // sum(weights)))
    least = 1 if total - largest >= count - 1 else 0
    given, surplus = [largest] + [least] * (count - 1), total - largest - least * (count - 1)
    while surplus > 0:
        candidates = [i for i in range(1, count) if given[i] < largest] or [i for i in range(1, count) if given[i] < most]
        whole, left = sum([weights[i] for i in candidates]), surplus
        for i in candidates:
            more = min(most - given[i], max(1, left * weights[i] // whole), surplus)
            given[i] = given[i] + more
            surplus = surplus - more
    return np.array(given)


def setup_inputs(seed: int = 0) -> dict:
    key_list = jax.random.split(jax.random.key(seed), 7)
    reference_image = draw_reference_image(jax.random.fold_in(key_list[6], 71), 0)
    deformed_image = draw_deformed_image(jax.random.fold_in(key_list[6], 71), 0)
    route_keys = jax.random.split(jax.random.fold_in(key_list[2], 1), N_GX * N_GY * NEL // NEL)
    route_turns = jax.random.permutation(jax.random.fold_in(key_list[2], 3), N_GX * N_GY * NEL // NEL)
    route = jax.vmap(lambda own, number: routed_block(jax.random.fold_in(key_list[2], 2), own, number, NEL, 2 * SPAN + 1, 1, CAP, 2))(route_keys, route_turns).reshape((N_GX, N_GY, NEL, 1))
    within = plant(jax.random.randint(key_list[3], (N_GX, N_GY, NEL), 0, EYD), jax.random.fold_in(key_list[3], 1), 0, EYD - 1).astype(jnp.int32)
    xshift = plant(jax.random.randint(key_list[4], (N_GX, N_GY, NEL), 0, 3), jax.random.fold_in(key_list[4], 1), 0, 2).astype(jnp.int32)
    fractions = plant(jax.random.randint(key_list[5], (N_GX, N_GY, NEL, 3), 0, EDGE), jax.random.fold_in(key_list[5], 1), 0, EDGE - 1).astype(jnp.int32)
    return dict(reference_image=reference_image, deformed_image=deformed_image, route=route, within=within, xshift=xshift, fractions=fractions)


LAMBDA = 0.05


def hat_positions(brick_edge, trailing):
    positions = (jnp.arange(brick_edge, dtype=jnp.float32) + 0.5) / brick_edge
    return positions.reshape((brick_edge,) + (1,) * trailing)


def spread_along(node_values, which_axis, brick_edge):
    node_count = node_values.shape[which_axis] - 1
    positions = hat_positions(brick_edge, node_values.ndim - which_axis - 1)
    lower_part = jnp.expand_dims(lax.slice_in_dim(node_values, 0, node_count, axis=which_axis), which_axis + 1)
    upper_part = jnp.expand_dims(lax.slice_in_dim(node_values, 1, node_count + 1, axis=which_axis), which_axis + 1)
    blended = lower_part * (1.0 - positions) + upper_part * positions
    new_shape = node_values.shape[:which_axis] + (node_count * brick_edge,) + node_values.shape[which_axis + 1:]
    return blended.reshape(new_shape)


def collect_along(voxel_values, which_axis, brick_edge):
    node_count = voxel_values.shape[which_axis] // brick_edge
    positions = hat_positions(brick_edge, voxel_values.ndim - which_axis - 1)
    blocks = voxel_values.reshape(voxel_values.shape[:which_axis] + (node_count, brick_edge) + voxel_values.shape[which_axis + 1:])
    lower_part = jnp.sum(blocks * (1.0 - positions), axis=which_axis + 1)
    upper_part = jnp.sum(blocks * positions, axis=which_axis + 1)
    zero_cap = jnp.zeros_like(lax.slice_in_dim(lower_part, 0, 1, axis=which_axis))
    return jnp.concatenate([lower_part, zero_cap], which_axis) + jnp.concatenate([zero_cap, upper_part], which_axis)


def clamp_shift(bricks, stride):
    advanced = jnp.concatenate([bricks[:, stride:], bricks[:, -stride:]], axis=1)
    places = jnp.arange(bricks.shape[1], dtype=jnp.int32)
    at_rim = (places // stride) % EDGE == EDGE - 1
    return jnp.where(at_rim[None, :], bricks, advanced)


def warp_bricks(bricks, fractions):
    weights = fractions.astype(jnp.float32) / EDGE
    blended = bricks
    for column, stride in ((2, 1), (1, EDGE), (0, EDGE * EDGE)):
        portion = weights[:, column:column + 1]
        blended = (1.0 - portion) * blended + portion * clamp_shift(blended, stride)
    return blended


def element_grid(values):
    trailing = values.shape[3:]
    shaped = values.reshape((N_GX, N_GY, EZ, EXD, EYD) + trailing)
    permuted_axes = (2, 0, 3, 1, 4) + tuple(range(5, 5 + len(trailing)))
    return shaped.transpose(permuted_axes).reshape((EZ, EX, EY) + trailing)


def brick_rows(image):
    shaped = image.reshape(EZ, EDGE, EX, EDGE, EY, EDGE)
    return shaped.transpose(0, 2, 4, 1, 3, 5).reshape(EZ, EX * EY, VOL)


def voxel_field(rows):
    shaped = rows.reshape(EZ, EX, EY, EDGE, EDGE, EDGE)
    return shaped.transpose(0, 3, 1, 4, 2, 5).reshape(NZV, NXV, NYV)


def compute_mismatch(reference_image, deformed_image, route, within, xshift, fractions):
    route_grid = element_grid(route)[..., 0]
    within_grid = element_grid(within)
    xshift_grid = element_grid(xshift)
    fraction_grid = element_grid(fractions).reshape(EZ, EX * EY, 3)
    column_x = jnp.arange(EX, dtype=jnp.int32)[:, None]
    column_y = jnp.arange(EY, dtype=jnp.int32)[None, :]
    source_x = jnp.clip(column_x + xshift_grid - 1, 0, EX - 1)
    source_y = ((column_y // EYD + route_grid - SPAN) % N_GY) * EYD + within_grid
    source_row = (source_x * EY + source_y).reshape(EZ, EX * EY).astype(jnp.int32)
    deformed_rows = brick_rows(deformed_image)
    reference_rows = brick_rows(reference_image)

    def slab_rows(inputs):
        rows_deformed, rows_reference, wanted, weights = inputs
        fetched = jnp.take(rows_deformed, wanted, axis=0)
        warped = warp_bricks(fetched.astype(jnp.float32), weights)
        return rows_reference.astype(jnp.float32) - warped

    mismatch_rows = lax.map(slab_rows, (deformed_rows, reference_rows, source_row, fraction_grid))
    return voxel_field(mismatch_rows)


def plane_gradient(padded, depth_index):
    slab = lax.dynamic_slice_in_dim(padded, depth_index, 3, 0).astype(jnp.float32)
    middle = slab[1]
    along_z = (slab[2] - slab[0])[1:-1, 1:-1] * 0.5
    along_x = (middle[2:, 1:-1] - middle[:-2, 1:-1]) * 0.5
    along_y = (middle[1:-1, 2:] - middle[1:-1, :-2]) * 0.5
    rounded = lax.optimization_barrier(jnp.stack([along_z, along_x, along_y]).astype(jnp.bfloat16))
    return rounded.astype(jnp.float32)


def layer_weights(depth_index):
    layer_index = depth_index // EDGE
    height = ((depth_index % EDGE).astype(jnp.float32) + 0.5) / EDGE
    levels = jnp.arange(EZ + 1, dtype=jnp.int32)
    return jnp.where(levels == layer_index, 1.0 - height, 0.0) + jnp.where(levels == layer_index + 1, height, 0.0)


def restrict_planes(padded, plane_terms):
    def visit_plane(running_total, depth_index):
        gradient = plane_gradient(padded, depth_index)
        voxel_terms = plane_terms(depth_index, gradient)
        plane_nodes = collect_along(collect_along(voxel_terms, 2, EDGE), 1, EDGE)
        weights = layer_weights(depth_index)
        return running_total + weights[None, :, None, None] * plane_nodes[:, None], None

    zero_nodes = jnp.zeros((3, EZ + 1, EX + 1, EY + 1), jnp.float32)
    running_total = lax.scan(visit_plane, zero_nodes, jnp.arange(NZV, dtype=jnp.int32))[0]
    return running_total[:, :, :EX, :EY] / VOL


def apply_hessian(unknown, padded):
    node_values = jnp.pad(unknown, ((0, 0), (0, 0), (0, 1), (0, 1)))

    def plane_terms(depth_index, gradient):
        weights = layer_weights(depth_index)
        plane_nodes = jnp.sum(weights[None, :, None, None] * node_values, axis=1)
        displaced = spread_along(spread_along(plane_nodes, 2, EDGE), 1, EDGE)
        normal_part = jnp.sum(gradient * displaced, axis=0)
        return gradient * normal_part

    return restrict_planes(padded, plane_terms) + LAMBDA * unknown


def reference(reference_image, deformed_image, route, within, xshift, fractions):
    mismatch = compute_mismatch(reference_image, deformed_image, route, within, xshift, fractions)
    padded = jnp.pad(reference_image, 1)

    def source_terms(depth_index, gradient):
        plane = lax.dynamic_index_in_dim(mismatch, depth_index, 0, keepdims=False)
        return gradient * plane[None]

    residual = restrict_planes(padded, source_terms)
    increment = jnp.zeros_like(residual)
    direction = residual
    norm_now = jnp.sum(residual * residual)
    for iteration in range(ITERS):
        curved = apply_hessian(direction, padded)
        step_size = norm_now / jnp.sum(direction * curved)
        increment = increment + step_size * direction
        residual = residual - step_size * curved
        norm_next = jnp.sum(residual * residual)
        direction = residual + (norm_next / norm_now) * direction
        norm_now = norm_next
    return increment, mismatch
```

```python
import functools

import jax
import jax.numpy as jnp
import numpy as np
from jax import lax
from jax.experimental import pallas as pl
from jax.experimental.pallas import tpu as pltpu
from jax.sharding import PartitionSpec as P

EDGE = 16
EZ = 4
EYD = 8
SPAN = 2
ITERS = 3
NEL = 32
VOL = 4096
NZ = EZ * EDGE
NY = EYD * EDGE
LAMBDA = 0.05

PAIRS = ((0, 0), (0, 1), (0, 2), (1, 1), (1, 2), (2, 2))
HROWS = 56

F32 = jnp.float32
BF16 = jnp.bfloat16

UPPER = (np.arange(EDGE) + 0.5) / EDGE
HAT = np.stack([1.0 - UPPER, UPPER])
PRODUCTS = np.stack([HAT[0] * HAT[0], HAT[0] * HAT[1], HAT[1] * HAT[1]])


def along_y_weights(weights):
    table = np.zeros((EZ, NY, 128), np.float32)
    for group, row in enumerate(weights):
        for ez in range(EZ):
            for ey in range(EYD):
                table[ez, ey * EDGE : (ey + 1) * EDGE, group * NEL + ez * EYD + ey] = row / VOL
    return table


def moment_tables():
    across = np.zeros((HROWS, 18 * EDGE), np.float32)
    for slab in range(18):
        for wx in range(3):
            across[slab * 3 + wx, slab * EDGE : (slab + 1) * EDGE] = PRODUCTS[wx]
    return across, along_y_weights(PRODUCTS)


def load_tables():
    across = np.zeros((16, 6 * EDGE), np.float32)
    for slab in range(6):
        for bx in range(2):
            across[bx * 8 + slab, slab * EDGE : (slab + 1) * EDGE] = HAT[bx]
    single = along_y_weights(HAT)
    along = np.concatenate([single, np.roll(single, 2 * NEL, axis=2)], axis=1)
    return across, along


def exact_dot(a, b):
    return jnp.dot(a, b, precision=lax.Precision.HIGHEST, preferred_element_type=F32)


def lanes(shape):
    return lax.broadcasted_iota(jnp.int32, shape, len(shape) - 1)


def rows_of(shape):
    return lax.broadcasted_iota(jnp.int32, shape, len(shape) - 2)


def even(value):
    return lax.rem(value, 2) == 0


def ask_kernel(gx_count, route, within, xshift, ref, m0, m1, m2, m3, f0, f1, own, place, count):
    gx, gy = lax.axis_index("gx"), lax.axis_index("gy")
    for j in range(5):
        count[j] = 0
    gx_even, gy_even, half_even = even(gx), even(gy), even(gy // 2)
    row, lane = rows_of((8, 128)), lanes((8, 128))

    def visit(e, asked):
        offset = route[e] - SPAN
        moved = jnp.clip(gx + xshift[e] - 1, 0, gx_count - 1) - gx
        ahead = jnp.where(gx_even, 1, 2)
        bank = jnp.where(moved == 0, 0, jnp.where(moved == 1, ahead, 3 - ahead))
        code = bank * NEL + (e // EYD) * EYD + within[e]
        near = jnp.where((offset == 1) == gy_even, 0, 1)
        far = jnp.where((offset == 2) == half_even, 2, 3)
        j = jnp.where(offset == 0, 4, jnp.where(jnp.abs(offset) == 1, near, far))
        slot = count[j]
        count[j] = slot + 1
        place[e] = j * 8 + slot
        return jnp.where((row == j) & (lane == slot), code.astype(F32), asked)

    asked = lax.fori_loop(0, NEL, visit, jnp.zeros((8, 128), F32), unroll=True)
    own[...] = asked
    m2[...] = asked
    m3[...] = asked
    m0[8:, :] = asked
    m1[8:, :] = asked
    image = ref[...]
    first = jnp.where(gy_even, NY - 1, 0)
    wanted = jnp.where(row == 0, first, jnp.where(row == 1, NY - 1 - first, -1))
    pick = (lane == wanted).astype(F32).astype(BF16)
    columns = lax.dot_general(pick, image.reshape(NZ * EDGE, NY), (((1,), (1,)), ((), ())), preferred_element_type=F32)
    for i in range(8):
        m0[i : i + 1, :] = columns[0:1, i * 128 : (i + 1) * 128]
        m1[i : i + 1, :] = columns[1:2, i * 128 : (i + 1) * 128]
    image = image.astype(F32)
    low, high = image[:, 0, :], image[:, EDGE - 1, :]
    f0[...] = jnp.where(gx_even, high, low).astype(BF16)
    f1[...] = jnp.where(gx_even, low, high).astype(BF16)


def ask(route, within, xshift, ref):
    smem = pl.BlockSpec(memory_space=pltpu.SMEM)
    vmem = pl.BlockSpec(memory_space=pltpu.VMEM)
    return pl.pallas_call(
        functools.partial(ask_kernel, lax.axis_size("gx")),
        out_shape=(
            jax.ShapeDtypeStruct((16, 128), F32),
            jax.ShapeDtypeStruct((16, 128), F32),
            jax.ShapeDtypeStruct((8, 128), F32),
            jax.ShapeDtypeStruct((8, 128), F32),
            jax.ShapeDtypeStruct((NZ, NY), BF16),
            jax.ShapeDtypeStruct((NZ, NY), BF16),
            jax.ShapeDtypeStruct((8, 128), F32),
            jax.ShapeDtypeStruct((NEL,), jnp.int32),
        ),
        in_specs=[smem] * 3 + [vmem],
        out_specs=(vmem,) * 7 + (smem,),
        scratch_shapes=[pltpu.SMEM((8,), jnp.int32)],
        name="ask",
    )(route, within, xshift, ref)


def serve_kernel(own, d0, d1, q0, q1, q2, q3, q4, o0, o1, o2, o3, o4, banks, sems):
    copies = [pltpu.make_async_copy(src, banks.at[i], sems.at[i]) for i, src in enumerate((own, d0, d1))]
    for copy in copies:
        copy.start()
    for copy in copies:
        copy.wait()
    lane = lanes((EDGE * EDGE, NY))
    for j, (asked, out) in enumerate(((q0, o0), (q1, o1), (q2, o2), (q3, o3), (q4, o4))):
        line = 8 + j if j < 2 else j

        def visit(slot, packed, asked=asked, line=line):
            code = asked[line, slot].astype(jnp.int32)
            bank, ez, column = code // NEL, lax.rem(code, NEL) // EYD, lax.rem(code, EYD)
            slab = banks[bank, pl.ds(ez * EDGE, EDGE)].reshape(EDGE * EDGE, NY).astype(F32)
            turned = pltpu.roll(slab, lax.rem((slot - column + EYD) * EDGE, NY), 1)
            return jnp.where(lane // EDGE == slot, turned, packed)

        packed = lax.fori_loop(0, 8, visit, jnp.zeros((EDGE * EDGE, NY), F32))
        out[...] = packed.reshape(EDGE, EDGE, NY).astype(BF16)


def serve(own, d0, d1, asked):
    smem = pl.BlockSpec(memory_space=pltpu.SMEM)
    vmem = pl.BlockSpec(memory_space=pltpu.VMEM)
    anywhere = pl.BlockSpec(memory_space=pl.ANY)
    return pl.pallas_call(
        serve_kernel,
        out_shape=(jax.ShapeDtypeStruct((EDGE, EDGE, NY), BF16),) * 5,
        in_specs=[anywhere] * 3 + [smem] * 5,
        out_specs=(vmem,) * 5,
        scratch_shapes=[pltpu.VMEM((3, NZ, EDGE, NY), BF16), pltpu.SemaphoreType.DMA((3,))],
        name="serve",
    )(own, d0, d1, *asked)


def moments_kernel(gy_count, ref, a0, a1, r0, r1, frac, across, along, grad, packed, portions, side, slabs):
    gx, gy = lax.axis_index("gx"), lax.axis_index("gy")
    gx_even, gy_even = even(gx), even(gy)
    side[...] = jnp.zeros((8, NZ * EDGE), F32)
    keep0 = jnp.where(gy_even, gy < gy_count - 1, gy > 0).astype(F32)
    keep1 = jnp.where(gy_even, gy > 0, gy < gy_count - 1).astype(F32)
    for i in range(8):
        side[0:1, i * 128 : (i + 1) * 128] = r0[i : i + 1, :] * keep0
        side[1:2, i * 128 : (i + 1) * 128] = r1[i : i + 1, :] * keep1
    row, lane = rows_of((8, 128)), lanes((8, 128))
    target0 = jnp.where(gy_even, NY - 1, 0)
    spot = jnp.where(row == 0, target0, jnp.where(row == 1, NY - 1 - target0, -1))
    spread = (lane == spot).astype(F32).astype(BF16)
    rim = lax.dot_general(
        side[...].astype(BF16), spread, (((0,), (0,)), ((), ())), preferred_element_type=F32
    ).reshape(NZ, EDGE, NY)
    from0, from1 = a0[...].astype(F32), a1[...].astype(F32)
    before = jnp.where(gx_even, from1, from0)
    after = jnp.where(gx_even, from0, from1)
    total = jnp.zeros((HROWS, 128), F32)
    lane2, row2 = lanes((EDGE, NY)), rows_of((EDGE, NY))
    for ez in range(EZ):
        collected = [[jnp.zeros((EDGE, NY), F32) for _ in range(3)] for _ in PAIRS]
        for k in range(EDGE):
            z = ez * EDGE + k
            plane = ref[z].astype(F32)
            below = ref[z - 1].astype(F32) if z > 0 else jnp.zeros((EDGE, NY), F32)
            above = ref[z + 1].astype(F32) if z + 1 < NZ else jnp.zeros((EDGE, NY), F32)
            rim_z = rim[z]
            nxt = jnp.where(row2 == EDGE - 1, after[z : z + 1, :], pltpu.roll(plane, EDGE - 1, 0))
            prv = jnp.where(row2 == 0, before[z : z + 1, :], pltpu.roll(plane, 1, 0))
            right = jnp.where(lane2 == NY - 1, rim_z, pltpu.roll(plane, NY - 1, 1))
            left = jnp.where(lane2 == 0, rim_z, pltpu.roll(plane, 1, 1))
            rounded = [((above - below) * 0.5).astype(BF16), ((nxt - prv) * 0.5).astype(BF16), ((right - left) * 0.5).astype(BF16)]
            for c in range(3):
                grad[c, z] = rounded[c]
            g = [value.astype(F32) for value in rounded]
            for p, (c, d) in enumerate(PAIRS):
                product = g[c] * g[d]
                for w in range(3):
                    collected[p][w] = collected[p][w] + float(PRODUCTS[w, k]) * product
        for p in range(len(PAIRS)):
            for w in range(3):
                slabs[(p * 3 + w) * EDGE : (p * 3 + w + 1) * EDGE, :] = collected[p][w]
        total = total + exact_dot(exact_dot(across[...], slabs[...]), along[ez])
    packed[...] = pltpu.roll(total, lax.rem(gx, 4) * NEL, 1)
    element, lane_e = rows_of((EYD, 128)), lanes((EYD, 128))
    unfold = (lane_e // EDGE == element).astype(F32).astype(BF16)
    for ez in range(EZ):
        tenths = frac[ez * EYD : (ez + 1) * EYD, :].astype(F32).astype(BF16)
        wide = lax.dot_general(tenths, unfold, (((0,), (0,)), ((), ())), preferred_element_type=F32)
        portions[ez, 0:3, :] = wide * (1.0 / EDGE)


def moments(ref, faces_x, faces_y, fractions):
    across, along = moment_tables()
    vmem = pl.BlockSpec(memory_space=pltpu.VMEM)
    return pl.pallas_call(
        functools.partial(moments_kernel, lax.axis_size("gy")),
        out_shape=(
            jax.ShapeDtypeStruct((3, NZ, EDGE, NY), BF16),
            jax.ShapeDtypeStruct((HROWS, 128), F32),
            jax.ShapeDtypeStruct((EZ, 8, 128), F32),
        ),
        in_specs=[vmem] * 8,
        out_specs=(vmem,) * 3,
        scratch_shapes=[pltpu.VMEM((8, NZ * EDGE), F32), pltpu.VMEM((18 * EDGE, NY), F32)],
        name="moments",
    )(ref, *faces_x, *faces_y, fractions, jnp.asarray(across), jnp.asarray(along))


def warp_kernel(place, b0, b1, b2, b3, b4, ref, grad, portions, across, along, mismatch, packed, bricks, slabs, sems):
    gx = lax.axis_index("gx")
    copies = [pltpu.make_async_copy(src, bricks.at[i], sems.at[i]) for i, src in enumerate((b0, b1, b2, b3, b4))]
    for copy in copies:
        copy.start()
    for copy in copies:
        copy.wait()
    flat = (EDGE * EDGE, NY)
    lane = lanes(flat)
    at_x_rim = lax.rem(lax.broadcasted_iota(jnp.int32, flat, 0), EDGE) == EDGE - 1
    at_y_rim = lax.rem(lane, EDGE) == EDGE - 1
    total = jnp.zeros((8, 128), F32)
    for ez in range(EZ):

        def visit(b, fetched, ez=ez):
            code = place[ez * EYD + b]
            slab = bricks[code // 8].reshape(flat).astype(F32)
            turned = pltpu.roll(slab, lax.rem((b - lax.rem(code, 8) + EYD) * EDGE, NY), 1)
            return jnp.where(lane // EDGE == b, turned, fetched)

        blended = lax.fori_loop(0, EYD, visit, jnp.zeros(flat, F32))
        portion = portions[ez]
        ty, tx, tz = portion[2:3, :], portion[1:2, :], portion[0:1, :]
        shifted = jnp.where(at_y_rim, blended, pltpu.roll(blended, NY - 1, 1))
        blended = (1.0 - ty) * blended + ty * shifted
        shifted = jnp.where(at_x_rim, blended, pltpu.roll(blended, EDGE * EDGE - 1, 0))
        blended = (1.0 - tx) * blended + tx * shifted
        shifted = jnp.concatenate([blended[EDGE:], blended[-EDGE:]], axis=0)
        blended = (1.0 - tz) * blended + tz * shifted
        blended = blended.reshape(EDGE, EDGE, NY)
        collected = [[jnp.zeros((EDGE, NY), F32) for _ in range(2)] for _ in range(3)]
        for k in range(EDGE):
            z = ez * EDGE + k
            apart = ref[z].astype(F32) - blended[k]
            mismatch[z] = apart
            for c in range(3):
                term = grad[c, z].astype(F32) * apart
                for a in range(2):
                    collected[c][a] = collected[c][a] + float(HAT[a, k]) * term
        for c in range(3):
            for a in range(2):
                slabs[(c * 2 + a) * EDGE : (c * 2 + a + 1) * EDGE, :] = collected[c][a]
        summed = exact_dot(across[...], slabs[...])
        total = total + exact_dot(jnp.concatenate([summed[:8], summed[8:]], axis=1), along[ez])
    packed[...] = pltpu.roll(total, lax.rem(gx, 4) * NEL, 1)


def warp(place, bricks, ref, grad, portions):
    across, along = load_tables()
    smem = pl.BlockSpec(memory_space=pltpu.SMEM)
    vmem = pl.BlockSpec(memory_space=pltpu.VMEM)
    anywhere = pl.BlockSpec(memory_space=pl.ANY)
    return pl.pallas_call(
        warp_kernel,
        out_shape=(jax.ShapeDtypeStruct((NZ, EDGE, NY), F32), jax.ShapeDtypeStruct((8, 128), F32)),
        in_specs=[smem] + [anywhere] * 5 + [vmem] * 5,
        out_specs=(vmem, vmem),
        scratch_shapes=[
            pltpu.VMEM((5, EDGE, EDGE, NY), BF16),
            pltpu.VMEM((6 * EDGE, NY), F32),
            pltpu.SemaphoreType.DMA((5,)),
        ],
        name="warp",
    )(place, *bricks, ref, grad, portions, jnp.asarray(across), jnp.asarray(along))


def spread_groups(block_of, groups, gx_count, store):
    tiles = -(-gx_count // 4)
    for tile in range(tiles):
        members = range(4 * tile, min(4 * tile + 4, gx_count))
        blocks = {gx: block_of(gx) for gx in members}
        for group in range(groups):
            merged = jnp.zeros_like(blocks[members[0]])
            lane = lanes(merged.shape)
            for gx in members:
                merged = jnp.where(lane // NEL == (group + gx) % 4, blocks[gx], merged)
            store(group, tile, pltpu.roll(merged, (128 - NEL * group) % 128, 1) if group else merged)


def solve_kernel(gx_count, gy_count, hess, load, out, coef, rhs):
    gx, gy = lax.axis_index("gx"), lax.axis_index("gy")
    tiles = -(-gx_count // 4)
    width = 128 * tiles

    def unpack(row, _):
        def hess_block(column):
            return hess[jnp.bitwise_xor(row, gy) * gx_count + jnp.bitwise_xor(gx, column)]

        def store_hess(group, tile, value):
            coef[tile, pl.ds(row * 3 * HROWS + group * HROWS, HROWS), :] = value

        def load_block(column):
            return load[column * gy_count + row]

        def store_load(group, tile, value):
            rhs[tile, pl.ds(row * 32 + group * 8, 8), :] = value

        spread_groups(hess_block, 3, gx_count, store_hess)
        spread_groups(load_block, 4, gx_count, store_load)
        return 0

    lax.fori_loop(0, gy_count, unpack, 0)
    shape = (gy_count, width)
    lane, row = lanes(shape), rows_of(shape)
    in_z, in_y, in_x = lax.rem(lane, NEL) // EYD, lax.rem(lane, EYD), lane // NEL
    last_z, first_z = in_z == EZ - 1, in_z == 0
    last_x, first_x = in_x >= gx_count - 1, in_x == 0
    last_y, first_y = in_y == EYD - 1, in_y == 0
    end_y, begin_y = last_y & (row == gy_count - 1), first_y & (row == 0)

    def turn(value, by, axis):
        size = shape[axis]
        by = by % size
        return pltpu.roll(value, by, axis) if by else value

    def corners(main, top):
        found = []
        for a in range(2):
            z_part = main if a == 0 else jnp.where(last_z, top, turn(main, -EYD, 1))
            for b in range(2):
                x_part = z_part if b == 0 else jnp.where(last_x, 0.0, turn(z_part, -NEL, 1))
                for d in range(2):
                    if d == 0:
                        found.append(x_part)
                    else:
                        wrapped = turn(turn(x_part, -1, 0), EYD - 1, 1)
                        moved = jnp.where(last_y, wrapped, turn(x_part, -1, 1))
                        found.append(jnp.where(end_y, 0.0, moved))
        return found

    def settle(parts):
        z_parts = []
        for a in range(2):
            x_parts = []
            for b in range(2):
                base, extra = parts[a * 4 + b * 2], parts[a * 4 + b * 2 + 1]
                wrapped = turn(turn(extra, 1, 0), 1 - EYD, 1)
                moved = jnp.where(first_y, wrapped, turn(extra, 1, 1))
                x_parts.append(base + jnp.where(begin_y, 0.0, moved))
            z_parts.append(x_parts[0] + jnp.where(first_x, 0.0, turn(x_parts[1], NEL, 1)))
        main = z_parts[0] + jnp.where(first_z, 0.0, turn(z_parts[1], EYD, 1))
        return main, jnp.where(last_z, z_parts[1], 0.0)

    def strided(ref, start, stride):
        found = [ref[tile, pl.ds(start, gy_count, stride=stride), :] for tile in range(tiles)]
        return found[0] if tiles == 1 else jnp.concatenate(found, axis=1)

    def channel(p, wz, wx, wy):
        return strided(coef, wy * HROWS + (p * 3 + wz) * 3 + wx, 3 * HROWS)

    pair_of = {}
    for p, (c, d) in enumerate(PAIRS):
        pair_of[c, d] = pair_of[d, c] = p
    bits = [(a, b, d) for a in range(2) for b in range(2) for d in range(2)]

    def curved_by(vector):
        known = [corners(main, top) for main, top in vector]
        sums = [[None] * 8 for _ in range(3)]

        def add(c, n, term):
            sums[c][n] = term if sums[c][n] is None else sums[c][n] + term

        for p, (c, d) in enumerate(PAIRS):
            for wz in range(3):
                for wx in range(3):
                    for wy in range(3):
                        factor = channel(p, wz, wx, wy)
                        for n, low in enumerate(bits):
                            for m, high in enumerate(bits):
                                if (low[0] + high[0], low[1] + high[1], low[2] + high[2]) == (wz, wx, wy):
                                    add(c, n, factor * known[d][m])
                                    if c != d:
                                        add(d, n, factor * known[c][m])
        result = []
        for c in range(3):
            main, top = settle(sums[c])
            result.append((main + LAMBDA * vector[c][0], top + LAMBDA * vector[c][1]))
        return result

    def inner(one, two):
        summed = sum(a[0] * b[0] + a[1] * b[1] for a, b in zip(one, two))
        return jnp.sum(jnp.sum(summed, axis=1, keepdims=True), axis=0, keepdims=True)

    def combine(one, factor, two):
        return [(a[0] + factor * b[0], a[1] + factor * b[1]) for a, b in zip(one, two)]

    residual = []
    for c in range(3):
        parts = [strided(rhs, (b * 2 + d) * 8 + c * 2 + a, 32) for a, b, d in bits]
        residual.append(settle(parts))
    direction = residual
    increment = None
    norm_now = inner(residual, residual)
    for iteration in range(ITERS):
        curved = curved_by(direction)
        step = norm_now / inner(direction, curved)
        if increment is None:
            increment = [(step * a, step * b) for a, b in direction]
        else:
            increment = combine(increment, step, direction)
        if iteration + 1 < ITERS:
            residual = combine(residual, -step, curved)
            norm_next = inner(residual, residual)
            direction = combine(residual, norm_next / norm_now, direction)
            norm_now = norm_next
    mine = (row == gy) & (in_x == gx)
    for c in range(3):
        for part, levels in ((increment[c][0], range(EZ)), (increment[c][1], [EZ])):
            line = jnp.sum(jnp.where(mine, part, 0.0), axis=0, keepdims=True)
            short = line[:, 0:128]
            for tile in range(1, tiles):
                short = short + line[:, tile * 128 : (tile + 1) * 128]
            short = pltpu.roll(jnp.broadcast_to(short, (8, 128)), lax.rem(128 - lax.rem(gx, 4) * NEL, 128), 1)
            for level in levels:
                start = min(level, EZ - 1) * EYD
                out[c, level] = short[0:1, start : start + EYD]


def solve(hess, load):
    gx_count, gy_count = lax.axis_size("gx"), lax.axis_size("gy")
    tiles = -(-gx_count // 4)
    vmem = pl.BlockSpec(memory_space=pltpu.VMEM)
    return pl.pallas_call(
        functools.partial(solve_kernel, gx_count, gy_count),
        out_shape=jax.ShapeDtypeStruct((3, EZ + 1, 1, EYD), F32),
        in_specs=[vmem, vmem],
        out_specs=vmem,
        scratch_shapes=[
            pltpu.VMEM((tiles, gy_count * 3 * HROWS, 128), F32),
            pltpu.VMEM((tiles, gy_count * 32, 128), F32),
        ],
        compiler_params=pltpu.CompilerParams(vmem_limit_bytes=48 * 1024 * 1024),
        name="solve",
    )(hess, load)


def swap(array, axis, partner):
    size = lax.axis_size(axis)
    pairs = [(i, partner(i)) for i in range(size)]
    return lax.ppermute(array, axis, [(i, j) for i, j in pairs if 0 <= j < size])


def swap_x(array, kind):
    if kind == 0:
        return swap(array, "gx", lambda i: i ^ 1)
    return swap(array, "gx", lambda i: i + 1 if i % 2 else i - 1)


def swap_y(array, kind):
    size = lax.axis_size("gy")
    partner = (
        lambda i: i ^ 1,
        lambda i: (i + 1 if i % 2 else i - 1) % size,
        lambda i: i ^ 2,
        lambda i: (i + 2 if i // 2 % 2 else i - 2) % size,
    )[kind]
    return swap(array, "gy", partner)


def everyones(block):
    known = block[None]
    for axis in ("gx", "gy"):
        step = 1
        while step < lax.axis_size(axis):
            known = jnp.concatenate([known, swap(known, axis, lambda i, step=step: i ^ step)], axis=0)
            step *= 2
    return known


def body(reference_image, deformed_image, route, within, xshift, fractions):
    d0, d1 = swap_x(deformed_image, 0), swap_x(deformed_image, 1)
    m0, m1, m2, m3, f0, f1, own, place = ask(
        route.reshape(NEL), within.reshape(NEL), xshift.reshape(NEL), reference_image
    )
    a0, a1 = swap_x(f0, 0), swap_x(f1, 1)
    q = [swap_y(m, kind) for kind, m in enumerate((m0, m1, m2, m3))]
    *served, at_home = serve(deformed_image, d0, d1, (*q, own))
    bricks = [swap_y(s, kind) for kind, s in enumerate(served)] + [at_home]
    grad, packed, portions = moments(reference_image, (a0, a1), (q[0], q[1]), fractions.reshape(NEL, 3))
    hess = everyones(packed)
    mismatch, part = warp(place, bricks, reference_image, grad, portions)
    devices = lax.axis_size("gx") * lax.axis_size("gy")
    load = lax.all_to_all(jnp.broadcast_to(part[None], (devices, 8, 128)), ("gx", "gy"), 0, 0)
    return solve(hess, load), mismatch


def solution(mesh):
    placed = (
        P(None, "gx", "gy"),
        P(None, "gx", "gy"),
        P("gx", "gy", None, None),
        P("gx", "gy", None),
        P("gx", "gy", None),
        P("gx", "gy", None, None),
    )
    return jax.shard_map(
        body,
        mesh=mesh,
        in_specs=placed,
        out_specs=(P(None, None, "gx", "gy"), P(None, "gx", "gy")),
        check_vma=False,
    )
```

```python
import functools

import jax
import jax.numpy as jnp
import numpy as np
from jax import lax
from jax.experimental import pallas as pl
from jax.experimental.pallas import tpu as pltpu
from jax.sharding import PartitionSpec as P

EDGE = 16
EZ = 4
EYD = 8
SPAN = 2
ITERS = 3
NEL = 32
VOL = 4096
NZ = EZ * EDGE
NY = EYD * EDGE
LAMBDA = 0.05

PAIRS = ((0, 0), (0, 1), (0, 2), (1, 1), (1, 2), (2, 2))
HROWS = 56
LIMIT = 32 * 1024 * 1024

F32 = jnp.float32
BF16 = jnp.bfloat16

UPPER = (np.arange(EDGE) + 0.5) / EDGE
HAT = np.stack([1.0 - UPPER, UPPER])
PRODUCTS = np.stack([HAT[0] * HAT[0], HAT[0] * HAT[1], HAT[1] * HAT[1]])


def hat_product(which, position):
    upper = (position.astype(F32) + 0.5) * (1.0 / EDGE)
    lower = 1.0 - upper
    return jnp.where(which == 0, lower * lower, jnp.where(which == 1, lower * upper, upper * upper))


def hat_weight(which, position):
    upper = (position.astype(F32) + 0.5) * (1.0 / EDGE)
    return jnp.where(which == 0, 1.0 - upper, upper)


def along_y(weight, groups):
    shape = (NY, 128)
    row, lane = rows_of(shape), lanes(shape)
    inside = (row // EDGE == lax.rem(lane, NEL)) & (lane // NEL < groups)
    return jnp.where(inside, weight(lane // NEL, lax.rem(row, EDGE)) * (1.0 / VOL), 0.0)


def exact_dot(a, b):
    return jnp.dot(a, b, precision=lax.Precision.HIGHEST, preferred_element_type=F32)


def lanes(shape):
    return lax.broadcasted_iota(jnp.int32, shape, len(shape) - 1)


def rows_of(shape):
    return lax.broadcasted_iota(jnp.int32, shape, len(shape) - 2)


def even(value):
    return lax.rem(value, 2) == 0


def takes(microseconds):
    return pl.CostEstimate(flops=0, bytes_accessed=int(microseconds * 3.69e6), transcendentals=0)


def ask_kernel(gx_count, route, within, xshift, ref, deformed, m0, m1, m2, m3, thick, own, place, count):
    gx, gy = lax.axis_index("gx"), lax.axis_index("gy")
    for j in range(5):
        count[j] = 0
    gx_even, gy_even, half_even = even(gx), even(gy), even(gy // 2)
    row, lane = rows_of((8, 128)), lanes((8, 128))

    def visit(e, asked):
        offset = route[e] - SPAN
        moved = jnp.clip(gx + xshift[e] - 1, 0, gx_count - 1) - gx
        ahead = jnp.where(gx_even, 1, 2)
        bank = jnp.where(moved == 0, 0, jnp.where(moved == 1, ahead, 3 - ahead))
        code = bank * NEL + (e // EYD) * EYD + within[e]
        near = jnp.where((offset == 1) == gy_even, 0, 1)
        far = jnp.where((offset == 2) == half_even, 2, 3)
        j = jnp.where(offset == 0, 4, jnp.where(jnp.abs(offset) == 1, near, far))
        slot = count[j]
        count[j] = slot + 1
        place[e] = j * 8 + slot
        return jnp.where((row == j) & (lane == slot), code.astype(F32), asked)

    asked = lax.fori_loop(0, NEL, visit, jnp.zeros((8, 128), F32), unroll=True)
    own[...] = asked
    m2[...] = asked
    m3[...] = asked
    m0[8:, :] = asked
    m1[8:, :] = asked
    image = ref[...]
    first = jnp.where(gy_even, NY - 1, 0)
    wanted = jnp.where(row == 0, first, jnp.where(row == 1, NY - 1 - first, -1))
    pick = (lane == wanted).astype(F32).astype(BF16)
    columns = lax.dot_general(pick, image.reshape(NZ * EDGE, NY), (((1,), (1,)), ((), ())), preferred_element_type=F32)
    for i in range(8):
        m0[i : i + 1, :] = columns[0:1, i * 128 : (i + 1) * 128]
        m1[i : i + 1, :] = columns[1:2, i * 128 : (i + 1) * 128]
    thick[0:NZ] = deformed[...]
    image = image.astype(F32)
    for k, face in enumerate((image[:, 0, :], image[:, EDGE - 1, :])):
        thick[NZ + k * EZ : NZ + (k + 1) * EZ] = face.astype(BF16).reshape(EZ, EDGE, NY)


def ask(route, within, xshift, ref, deformed):
    smem = pl.BlockSpec(memory_space=pltpu.SMEM)
    vmem = pl.BlockSpec(memory_space=pltpu.VMEM)
    return pl.pallas_call(
        functools.partial(ask_kernel, lax.axis_size("gx")),
        out_shape=(
            jax.ShapeDtypeStruct((16, 128), F32),
            jax.ShapeDtypeStruct((16, 128), F32),
            jax.ShapeDtypeStruct((8, 128), F32),
            jax.ShapeDtypeStruct((8, 128), F32),
            jax.ShapeDtypeStruct((NZ + 2 * EZ, EDGE, NY), BF16),
            jax.ShapeDtypeStruct((8, 128), F32),
            jax.ShapeDtypeStruct((NEL,), jnp.int32),
        ),
        in_specs=[smem] * 3 + [vmem] * 2,
        out_specs=(vmem,) * 6 + (smem,),
        scratch_shapes=[pltpu.SMEM((8,), jnp.int32)],
        cost_estimate=takes(2.0),
        name="ask",
    )(route, within, xshift, ref, deformed)


def gather_columns(table, slabs, sources, places):
    table[...] = jnp.zeros_like(table)
    shape = (EDGE, NY)
    row, lane = rows_of(shape), lanes(shape)
    for i, (source, place) in enumerate(zip(sources, places)):
        start = pl.multiple_of(i * NY + source * EDGE, EDGE)
        table[pl.ds(start, EDGE), :] = (lane == row + place * EDGE).astype(F32).astype(BF16)
    return jnp.dot(jnp.concatenate(slabs, axis=1), table[...], preferred_element_type=F32)


def serve_kernel(lines, *refs):
    count = len(lines)
    asked, outs = refs[3 : 3 + count], refs[3 + count : 3 + 2 * count]
    banks, tables = refs[3 + 2 * count :]
    for i in range(3):
        banks[i] = refs[i][0:NZ]
    for j in range(count):
        slabs, columns = [], []
        for slot in range(8):
            code = asked[j][lines[j], slot].astype(jnp.int32)
            slab = banks[code // NEL, pl.ds(lax.rem(code, NEL) // EYD * EDGE, EDGE)]
            slabs.append(slab.reshape(EDGE * EDGE, NY))
            columns.append(lax.rem(code, EYD))
        packed = gather_columns(tables.at[j], slabs, columns, range(8))
        outs[j][...] = packed.reshape(EDGE, EDGE, NY).astype(BF16)


def serve(own, d0, d1, asked, lines):
    smem = pl.BlockSpec(memory_space=pltpu.SMEM)
    vmem = pl.BlockSpec(memory_space=pltpu.VMEM)
    count = len(lines)
    return pl.pallas_call(
        functools.partial(serve_kernel, lines),
        out_shape=(jax.ShapeDtypeStruct((EDGE, EDGE, NY), BF16),) * count,
        in_specs=[vmem] * 3 + [smem] * count,
        out_specs=(vmem,) * count,
        scratch_shapes=[
            pltpu.VMEM((3, NZ, EDGE, NY), BF16),
            pltpu.VMEM((count, 8 * NY, NY), BF16),
        ],
        compiler_params=pltpu.CompilerParams(vmem_limit_bytes=LIMIT),
        cost_estimate=takes(1.0 + 0.2 * count),
        name="serve",
    )(own, d0, d1, *asked)


def moments_kernel(gy_count, ref, a0, a1, r0, r1, frac, grad, packed, portions, side, slabs):
    gx, gy = lax.axis_index("gx"), lax.axis_index("gy")
    gx_even, gy_even = even(gx), even(gy)
    side[...] = jnp.zeros((8, NZ * EDGE), F32)
    keep0 = jnp.where(gy_even, gy < gy_count - 1, gy > 0).astype(F32)
    keep1 = jnp.where(gy_even, gy > 0, gy < gy_count - 1).astype(F32)
    for i in range(8):
        side[0:1, i * 128 : (i + 1) * 128] = r0[i : i + 1, :] * keep0
        side[1:2, i * 128 : (i + 1) * 128] = r1[i : i + 1, :] * keep1
    row, lane = rows_of((8, 128)), lanes((8, 128))
    target0 = jnp.where(gy_even, NY - 1, 0)
    spot = jnp.where(row == 0, target0, jnp.where(row == 1, NY - 1 - target0, -1))
    spread = (lane == spot).astype(F32).astype(BF16)
    rim = lax.dot_general(
        side[...].astype(BF16), spread, (((0,), (0,)), ((), ())), preferred_element_type=F32
    ).reshape(NZ, EDGE, NY)
    low0, high0, low1, high1 = (
        thick[NZ + k * EZ : NZ + (k + 1) * EZ].astype(F32).reshape(NZ, NY) for thick in (a0, a1) for k in range(2)
    )
    before = jnp.where(gx_even, high1, high0)
    after = jnp.where(gx_even, low0, low1)
    shape = (HROWS, 18 * EDGE)
    row_a, lane_a = rows_of(shape), lanes(shape)
    across = jnp.where(row_a // 3 == lane_a // EDGE, hat_product(lax.rem(row_a, 3), lax.rem(lane_a, EDGE)), 0.0)
    along = along_y(hat_product, 3)
    total = jnp.zeros((HROWS, 128), F32)
    lane2, row2 = lanes((EDGE, NY)), rows_of((EDGE, NY))
    for ez in range(EZ):
        collected = [[jnp.zeros((EDGE, NY), F32) for _ in range(3)] for _ in PAIRS]
        for k in range(EDGE):
            z = ez * EDGE + k
            plane = ref[z].astype(F32)
            below = ref[z - 1].astype(F32) if z > 0 else jnp.zeros((EDGE, NY), F32)
            above = ref[z + 1].astype(F32) if z + 1 < NZ else jnp.zeros((EDGE, NY), F32)
            rim_z = rim[z]
            nxt = jnp.where(row2 == EDGE - 1, after[z : z + 1, :], pltpu.roll(plane, EDGE - 1, 0))
            prv = jnp.where(row2 == 0, before[z : z + 1, :], pltpu.roll(plane, 1, 0))
            right = jnp.where(lane2 == NY - 1, rim_z, pltpu.roll(plane, NY - 1, 1))
            left = jnp.where(lane2 == 0, rim_z, pltpu.roll(plane, 1, 1))
            rounded = [((above - below) * 0.5).astype(BF16), ((nxt - prv) * 0.5).astype(BF16), ((right - left) * 0.5).astype(BF16)]
            for c in range(3):
                grad[c, z] = rounded[c]
            g = [value.astype(F32) for value in rounded]
            for p, (c, d) in enumerate(PAIRS):
                product = g[c] * g[d]
                for w in range(3):
                    collected[p][w] = collected[p][w] + float(PRODUCTS[w, k]) * product
        for p in range(len(PAIRS)):
            for w in range(3):
                slabs[(p * 3 + w) * EDGE : (p * 3 + w + 1) * EDGE, :] = collected[p][w]
        found = exact_dot(exact_dot(across, slabs[...]), along)
        total = total + (pltpu.roll(found, ez * EYD, 1) if ez else found)
    packed[...] = pltpu.roll(total, lax.rem(gx, 4) * NEL, 1)
    element, lane_e = rows_of((EYD, 128)), lanes((EYD, 128))
    unfold = (lane_e // EDGE == element).astype(F32).astype(BF16)
    for ez in range(EZ):
        tenths = frac[ez * EYD : (ez + 1) * EYD, :].astype(F32).astype(BF16)
        wide = lax.dot_general(tenths, unfold, (((0,), (0,)), ((), ())), preferred_element_type=F32)
        portions[ez, 0:3, :] = wide * (1.0 / EDGE)


def moments(ref, faces_x, faces_y, fractions):
    vmem = pl.BlockSpec(memory_space=pltpu.VMEM)
    return pl.pallas_call(
        functools.partial(moments_kernel, lax.axis_size("gy")),
        out_shape=(
            jax.ShapeDtypeStruct((3, NZ, EDGE, NY), BF16),
            jax.ShapeDtypeStruct((HROWS, 128), F32),
            jax.ShapeDtypeStruct((EZ, 8, 128), F32),
        ),
        in_specs=[vmem] * 6,
        out_specs=(vmem,) * 3,
        scratch_shapes=[pltpu.VMEM((8, NZ * EDGE), F32), pltpu.VMEM((18 * EDGE, NY), F32)],
        compiler_params=pltpu.CompilerParams(vmem_limit_bytes=LIMIT),
        cost_estimate=takes(2.2),
        name="moments",
    )(ref, *faces_x, *faces_y, fractions)


def warp_kernel(place, b0, b1, b2, b3, b4, ref, grad, portions, mismatch, packed, bricks, tables, slabs):
    gx = lax.axis_index("gx")
    for i, source in enumerate((b0, b1, b2, b3, b4)):
        bricks[i] = source[...]
    flat = (EDGE * EDGE, NY)
    lane = lanes(flat)
    at_x_rim = lax.rem(lax.broadcasted_iota(jnp.int32, flat, 0), EDGE) == EDGE - 1
    at_y_rim = lax.rem(lane, EDGE) == EDGE - 1
    shape = (16, 6 * EDGE)
    row_a, lane_a = rows_of(shape), lanes(shape)
    across = jnp.where(lax.rem(row_a, 8) == lane_a // EDGE, hat_weight(row_a // 8, lax.rem(lane_a, EDGE)), 0.0)
    along = along_y(hat_weight, 2)
    along = jnp.concatenate([along, pltpu.roll(along, 2 * NEL, 1)], axis=0)
    total = jnp.zeros((8, 128), F32)
    for ez in range(EZ):

        codes = [place[ez * EYD + b] for b in range(EYD)]
        found = [bricks[code // 8].reshape(flat) for code in codes]
        blended = gather_columns(tables.at[ez], found, [lax.rem(code, 8) for code in codes], range(EYD))
        portion = portions[ez]
        ty, tx, tz = portion[2:3, :], portion[1:2, :], portion[0:1, :]
        shifted = jnp.where(at_y_rim, blended, pltpu.roll(blended, NY - 1, 1))
        blended = (1.0 - ty) * blended + ty * shifted
        shifted = jnp.where(at_x_rim, blended, pltpu.roll(blended, EDGE * EDGE - 1, 0))
        blended = (1.0 - tx) * blended + tx * shifted
        shifted = jnp.concatenate([blended[EDGE:], blended[-EDGE:]], axis=0)
        blended = (1.0 - tz) * blended + tz * shifted
        blended = blended.reshape(EDGE, EDGE, NY)
        collected = [[jnp.zeros((EDGE, NY), F32) for _ in range(2)] for _ in range(3)]
        for k in range(EDGE):
            z = ez * EDGE + k
            apart = ref[z].astype(F32) - blended[k]
            mismatch[z] = apart
            for c in range(3):
                term = grad[c, z].astype(F32) * apart
                for a in range(2):
                    collected[c][a] = collected[c][a] + float(HAT[a, k]) * term
        for c in range(3):
            for a in range(2):
                slabs[(c * 2 + a) * EDGE : (c * 2 + a + 1) * EDGE, :] = collected[c][a]
        summed = exact_dot(across, slabs[...])
        found = exact_dot(jnp.concatenate([summed[:8], summed[8:]], axis=1), along)
        total = total + (pltpu.roll(found, ez * EYD, 1) if ez else found)
    packed[...] = jnp.broadcast_to(pltpu.roll(total, lax.rem(gx, 4) * NEL, 1), packed.shape)


def warp(place, bricks, ref, grad, portions):
    smem = pl.BlockSpec(memory_space=pltpu.SMEM)
    vmem = pl.BlockSpec(memory_space=pltpu.VMEM)
    devices = lax.axis_size("gx") * lax.axis_size("gy")
    return pl.pallas_call(
        warp_kernel,
        out_shape=(jax.ShapeDtypeStruct((NZ, EDGE, NY), F32), jax.ShapeDtypeStruct((devices, 8, 128), F32)),
        in_specs=[smem] + [vmem] * 8,
        out_specs=(vmem, vmem),
        scratch_shapes=[
            pltpu.VMEM((5, EDGE, EDGE, NY), BF16),
            pltpu.VMEM((EZ, EYD * NY, NY), BF16),
            pltpu.VMEM((6 * EDGE, NY), F32),
        ],
        compiler_params=pltpu.CompilerParams(vmem_limit_bytes=LIMIT),
        cost_estimate=takes(4.0),
        name="warp",
    )(place, *bricks, ref, grad, portions)


def spread_groups(block_of, groups, gx_count, store):
    tiles = -(-gx_count // 4)
    for tile in range(tiles):
        members = range(4 * tile, min(4 * tile + 4, gx_count))
        blocks = {gx: block_of(gx) for gx in members}
        for group in range(groups):
            merged = jnp.zeros_like(blocks[members[0]])
            lane = lanes(merged.shape)
            for gx in members:
                merged = jnp.where(lane // NEL == (group + gx) % 4, blocks[gx], merged)
            store(group, tile, pltpu.roll(merged, (128 - NEL * group) % 128, 1) if group else merged)


def solve_kernel(gx_count, gy_count, hess, load, out, coef, rhs):
    gx, gy = lax.axis_index("gx"), lax.axis_index("gy")
    steps = gather_steps(gx_count, gy_count)
    tiles = -(-gx_count // 4)
    width = 128 * tiles

    def unpack(row, _):
        def hess_block(column):
            return hess[block_index(steps, dict(gx=jnp.bitwise_xor(gx, column), gy=jnp.bitwise_xor(gy, row)))]

        def store_hess(group, tile, value):
            coef[tile, pl.ds(row * 3 * HROWS + group * HROWS, HROWS), :] = value

        def load_block(column):
            return load[column * gy_count + row]

        def store_load(group, tile, value):
            rhs[tile, pl.ds(row * 32 + group * 8, 8), :] = value

        spread_groups(hess_block, 3, gx_count, store_hess)
        spread_groups(load_block, 4, gx_count, store_load)
        return 0

    lax.fori_loop(0, gy_count, unpack, 0)
    shape = (gy_count, width)
    lane, row = lanes(shape), rows_of(shape)
    in_z, in_y, in_x = lax.rem(lane, NEL) // EYD, lax.rem(lane, EYD), lane // NEL
    last_z, first_z = in_z == EZ - 1, in_z == 0
    last_x, first_x = in_x >= gx_count - 1, in_x == 0
    last_y, first_y = in_y == EYD - 1, in_y == 0
    end_y, begin_y = last_y & (row == gy_count - 1), first_y & (row == 0)

    def turn(value, by, axis):
        size = shape[axis]
        by = by % size
        return pltpu.roll(value, by, axis) if by else value

    def corners(main, top):
        found = []
        for a in range(2):
            z_part = main if a == 0 else jnp.where(last_z, top, turn(main, -EYD, 1))
            for b in range(2):
                x_part = z_part if b == 0 else jnp.where(last_x, 0.0, turn(z_part, -NEL, 1))
                for d in range(2):
                    if d == 0:
                        found.append(x_part)
                    else:
                        wrapped = turn(turn(x_part, -1, 0), EYD - 1, 1)
                        moved = jnp.where(last_y, wrapped, turn(x_part, -1, 1))
                        found.append(jnp.where(end_y, 0.0, moved))
        return found

    def settle(parts):
        z_parts = []
        for a in range(2):
            x_parts = []
            for b in range(2):
                base, extra = parts[a * 4 + b * 2], parts[a * 4 + b * 2 + 1]
                wrapped = turn(turn(extra, 1, 0), 1 - EYD, 1)
                moved = jnp.where(first_y, wrapped, turn(extra, 1, 1))
                x_parts.append(base + jnp.where(begin_y, 0.0, moved))
            z_parts.append(x_parts[0] + jnp.where(first_x, 0.0, turn(x_parts[1], NEL, 1)))
        main = z_parts[0] + jnp.where(first_z, 0.0, turn(z_parts[1], EYD, 1))
        return main, jnp.where(last_z, z_parts[1], 0.0)

    def strided(ref, start, stride):
        found = [ref[tile, pl.ds(start, gy_count, stride=stride), :] for tile in range(tiles)]
        return found[0] if tiles == 1 else jnp.concatenate(found, axis=1)

    def channel(p, wz, wx, wy):
        return strided(coef, wy * HROWS + (p * 3 + wz) * 3 + wx, 3 * HROWS)

    pair_of = {}
    for p, (c, d) in enumerate(PAIRS):
        pair_of[c, d] = pair_of[d, c] = p
    bits = [(a, b, d) for a in range(2) for b in range(2) for d in range(2)]

    def curved_by(vector):
        known = [corners(main, top) for main, top in vector]
        sums = [[None] * 8 for _ in range(3)]

        def add(c, n, term):
            sums[c][n] = term if sums[c][n] is None else sums[c][n] + term

        for p, (c, d) in enumerate(PAIRS):
            for wz in range(3):
                for wx in range(3):
                    for wy in range(3):
                        factor = channel(p, wz, wx, wy)
                        for n, low in enumerate(bits):
                            for m, high in enumerate(bits):
                                if (low[0] + high[0], low[1] + high[1], low[2] + high[2]) == (wz, wx, wy):
                                    add(c, n, factor * known[d][m])
                                    if c != d:
                                        add(d, n, factor * known[c][m])
        result = []
        for c in range(3):
            main, top = settle(sums[c])
            result.append((main + LAMBDA * vector[c][0], top + LAMBDA * vector[c][1]))
        return result

    def inner(one, two):
        summed = sum(a[0] * b[0] + a[1] * b[1] for a, b in zip(one, two))
        return jnp.sum(jnp.sum(summed, axis=1, keepdims=True), axis=0, keepdims=True)

    def combine(one, factor, two):
        return [(a[0] + factor * b[0], a[1] + factor * b[1]) for a, b in zip(one, two)]

    residual = []
    for c in range(3):
        parts = [strided(rhs, (b * 2 + d) * 8 + c * 2 + a, 32) for a, b, d in bits]
        residual.append(settle(parts))
    direction = residual
    increment = None
    norm_now = inner(residual, residual)
    for iteration in range(ITERS):
        curved = curved_by(direction)
        step = norm_now / inner(direction, curved)
        if increment is None:
            increment = [(step * a, step * b) for a, b in direction]
        else:
            increment = combine(increment, step, direction)
        if iteration + 1 < ITERS:
            residual = combine(residual, -step, curved)
            norm_next = inner(residual, residual)
            direction = combine(residual, norm_next / norm_now, direction)
            norm_now = norm_next
    mine = (row == gy) & (in_x == gx)
    for c in range(3):
        for part, levels in ((increment[c][0], range(EZ)), (increment[c][1], [EZ])):
            line = jnp.sum(jnp.where(mine, part, 0.0), axis=0, keepdims=True)
            short = line[:, 0:128]
            for tile in range(1, tiles):
                short = short + line[:, tile * 128 : (tile + 1) * 128]
            short = pltpu.roll(jnp.broadcast_to(short, (8, 128)), lax.rem(128 - lax.rem(gx, 4) * NEL, 128), 1)
            for level in levels:
                start = min(level, EZ - 1) * EYD
                out[c, level] = short[0:1, start : start + EYD]


def solve(hess, load):
    gx_count, gy_count = lax.axis_size("gx"), lax.axis_size("gy")
    tiles = -(-gx_count // 4)
    vmem = pl.BlockSpec(memory_space=pltpu.VMEM)
    return pl.pallas_call(
        functools.partial(solve_kernel, gx_count, gy_count),
        out_shape=jax.ShapeDtypeStruct((3, EZ + 1, 1, EYD), F32),
        in_specs=[vmem, vmem],
        out_specs=vmem,
        scratch_shapes=[
            pltpu.VMEM((tiles, gy_count * 3 * HROWS, 128), F32),
            pltpu.VMEM((tiles, gy_count * 32, 128), F32),
        ],
        compiler_params=pltpu.CompilerParams(vmem_limit_bytes=LIMIT),
        cost_estimate=takes(3.5),
        name="solve",
    )(hess, load)


def swap(array, axis, partner):
    size = lax.axis_size(axis)
    pairs = [(i, partner(i)) for i in range(size)]
    return lax.ppermute(array, axis, [(i, j) for i, j in pairs if 0 <= j < size])


def swap_x(array, kind):
    if kind == 0:
        return swap(array, "gx", lambda i: i ^ 1)
    return swap(array, "gx", lambda i: i + 1 if i % 2 else i - 1)


def swap_y(array, kind):
    size = lax.axis_size("gy")
    partner = (
        lambda i: i ^ 1,
        lambda i: (i + 1 if i % 2 else i - 1) % size,
        lambda i: i ^ 2,
        lambda i: (i + 2 if i // 2 % 2 else i - 2) % size,
    )[kind]
    return swap(array, "gy", partner)


def gather_steps(gx_count, gy_count):
    steps = []
    for axis, size in (("gy", gy_count), ("gx", gx_count)):
        bit = size // 2
        while bit:
            steps.append((axis, bit))
            bit //= 2
    return steps


def block_index(steps, relative):
    found = 0
    for k, (axis, bit) in enumerate(steps):
        found = found + jnp.where(jnp.bitwise_and(relative[axis], bit) != 0, 1 << k, 0)
    return found


def body(reference_image, deformed_image, route, within, xshift, fractions):
    m0, m1, m2, m3, thick, own, place = ask(
        route.reshape(NEL), within.reshape(NEL), xshift.reshape(NEL), reference_image, deformed_image
    )
    q = [swap_y(m, kind) for kind, m in enumerate((m0, m1, m2, m3))]
    d0, d1 = swap_x(thick, 0), swap_x(thick, 1)
    *q, d0, d1 = lax.optimization_barrier((*q, d0, d1))
    image, _ = lax.optimization_barrier((reference_image, q))
    grad, packed, portions = moments(image, (d0, d1), (q[0], q[1]), fractions.reshape(NEL, 3))
    q[2], packed = lax.optimization_barrier((q[2], packed))
    served = serve(deformed_image, d0, d1, q, (8, 9, 2, 3))
    own, _ = lax.optimization_barrier((own, served))
    (at_home,) = serve(deformed_image, d0, d1, [own], (4,))
    known = packed[None]
    bricks = [swap_y(block, kind) for kind, block in enumerate(served)] + [at_home]
    steps = gather_steps(lax.axis_size("gx"), lax.axis_size("gy"))
    for k, (axis, bit) in enumerate(steps):
        if k == 1:
            known, _ = lax.optimization_barrier((known, at_home))
        if k == len(steps) - 3:
            bricks, known = lax.optimization_barrier((bricks, known))
            mismatch, part = warp(place, bricks, reference_image, grad, portions)
        if k == len(steps) - 2:
            known, part = lax.optimization_barrier((known, part))
            load = lax.all_to_all(part, ("gx", "gy"), 0, 0)
        pieces = 4 if k + 1 == len(steps) else 1
        size = known.shape[0] // pieces
        sent = [swap(known[i * size : (i + 1) * size], axis, lambda i, bit=bit: i ^ bit) for i in range(pieces)]
        known = jnp.concatenate([known, *sent], axis=0)
    return solve(known, load), mismatch


def solution(mesh):
    placed = (
        P(None, "gx", "gy"),
        P(None, "gx", "gy"),
        P("gx", "gy", None, None),
        P("gx", "gy", None),
        P("gx", "gy", None),
        P("gx", "gy", None, None),
    )
    return jax.shard_map(
        body,
        mesh=mesh,
        in_specs=placed,
        out_specs=(P(None, None, "gx", "gy"), P(None, "gx", "gy")),
        check_vma=False,
    )
```

```python
import functools

import jax
import jax.numpy as jnp
import numpy as np
from jax import lax
from jax.experimental import pallas as pl
from jax.experimental.pallas import tpu as pltpu
from jax.sharding import PartitionSpec as P

EDGE = 16
EZ = 4
EYD = 8
SPAN = 2
ITERS = 3
NEL = 32
VOL = 4096
NZ = EZ * EDGE
NY = EYD * EDGE
LAMBDA = 0.05

PAIRS = ((0, 0), (0, 1), (0, 2), (1, 1), (1, 2), (2, 2))
HROWS = 40
SPLIT = 24
KINDS = (3, 0, 1, 2)
LIMIT = 32 * 1024 * 1024

F32 = jnp.float32
BF16 = jnp.bfloat16

UPPER = (np.arange(EDGE) + 0.5) / EDGE
HAT = np.stack([1.0 - UPPER, UPPER])
PRODUCTS = np.stack([HAT[0] * HAT[0], HAT[0] * HAT[1], HAT[1] * HAT[1]])


def hat_product(which, position):
    upper = (position.astype(F32) + 0.5) * (1.0 / EDGE)
    lower = 1.0 - upper
    return jnp.where(which == 0, lower * lower, jnp.where(which == 1, lower * upper, upper * upper))


def hat_weight(which, position):
    upper = (position.astype(F32) + 0.5) * (1.0 / EDGE)
    return jnp.where(which == 0, 1.0 - upper, upper)


def along_y(weight, groups):
    shape = (NY, 128)
    row, lane = rows_of(shape), lanes(shape)
    group = lane // NEL
    inside = (row // EDGE == lax.rem(lane, NEL)) & (group >= groups[0]) & (group <= groups[-1])
    return jnp.where(inside, weight(group, lax.rem(row, EDGE)) * (1.0 / VOL), 0.0)


def three_parts(value):
    high = value.astype(BF16)
    rest = value - high.astype(F32)
    middle = rest.astype(BF16)
    return [high, middle, (rest - middle.astype(F32)).astype(BF16)]


def weighed(value, weights):
    high = weights.astype(BF16)
    both = jnp.concatenate([high, (weights - high.astype(F32)).astype(BF16)], axis=1)
    found = jnp.dot(
        jnp.concatenate(three_parts(value), axis=1),
        jnp.concatenate([both] * 3, axis=0),
        preferred_element_type=F32,
    )
    return found[:, :128] + found[:, 128:]


def weighed_once(value, weights):
    weights = weights.astype(BF16)
    return jnp.dot(
        jnp.concatenate(three_parts(value), axis=1),
        jnp.concatenate([weights] * 3, axis=0),
        preferred_element_type=F32,
    )


def layered(found, slab, slabs, weights):
    total = None
    for ez in range(EZ):
        start = (ez * slabs + slab) * EDGE
        part = found[start : start + EDGE] * weights
        part = part[:8] + part[8:]
        part = pltpu.roll(part, ez * EYD, 1) if ez else part
        total = part if total is None else total + part
    return jnp.sum(total, axis=0, keepdims=True)


def lanes(shape):
    return lax.broadcasted_iota(jnp.int32, shape, len(shape) - 1)


def rows_of(shape):
    return lax.broadcasted_iota(jnp.int32, shape, len(shape) - 2)


def even(value):
    return lax.rem(value, 2) == 0


def takes(microseconds):
    return pl.CostEstimate(flops=0, bytes_accessed=int(microseconds * 3.69e6), transcendentals=0)


def ask_kernel(gx_count, route, within, xshift, ref, deformed, m0, m1, m2, m3, thick, own, place, count):
    gx, gy = lax.axis_index("gx"), lax.axis_index("gy")
    for j in range(5):
        count[j] = 0
    gx_even, gy_even, half_even = even(gx), even(gy), even(gy // 2)
    row, lane = rows_of((8, 128)), lanes((8, 128))

    def visit(e, found):
        offset = route[e] - SPAN
        moved = jnp.clip(gx + xshift[e] - 1, 0, gx_count - 1) - gx
        ahead = jnp.where(gx_even, 1, 2)
        bank = jnp.where(moved == 0, 0, jnp.where(moved == 1, ahead, 3 - ahead))
        code = bank * NEL + (e // EYD) * EYD + within[e]
        near = jnp.where((offset == 1) == gy_even, 0, 1)
        far = jnp.where((offset == 2) == half_even, 2, 3)
        j = jnp.where(offset == 0, 4, jnp.where(jnp.abs(offset) == 1, near, far))
        slot = count[j]
        count[j] = slot + 1
        asked, places = found
        asked = jnp.where((row == j) & (lane == slot), code.astype(F32), asked)
        return asked, jnp.where(lane == e, j * 8 + slot, places)

    zero = jnp.zeros((8, 128), jnp.int32)
    asked, places = lax.fori_loop(0, NEL, visit, (zero.astype(F32), zero), unroll=True)
    place[...] = places
    own[...] = asked
    m2[...] = asked
    m3[...] = asked
    m0[8:, :] = asked
    m1[8:, :] = asked
    image = ref[...]
    first = jnp.where(gy_even, NY - 1, 0)
    wanted = jnp.where(row == 0, first, jnp.where(row == 1, NY - 1 - first, -1))
    pick = (lane == wanted).astype(F32).astype(BF16)
    columns = lax.dot_general(pick, image.reshape(NZ * EDGE, NY), (((1,), (1,)), ((), ())), preferred_element_type=F32)
    for i in range(8):
        m0[i : i + 1, :] = columns[0:1, i * 128 : (i + 1) * 128]
        m1[i : i + 1, :] = columns[1:2, i * 128 : (i + 1) * 128]
    thick[0:NZ] = deformed[...]
    image = image.astype(F32)
    for k, face in enumerate((image[:, 0, :], image[:, EDGE - 1, :])):
        thick[NZ + k * EZ : NZ + (k + 1) * EZ] = face.astype(BF16).reshape(EZ, EDGE, NY)


def ask(route, within, xshift, ref, deformed):
    smem = pl.BlockSpec(memory_space=pltpu.SMEM)
    vmem = pl.BlockSpec(memory_space=pltpu.VMEM)
    return pl.pallas_call(
        functools.partial(ask_kernel, lax.axis_size("gx")),
        out_shape=(
            jax.ShapeDtypeStruct((16, 128), F32),
            jax.ShapeDtypeStruct((16, 128), F32),
            jax.ShapeDtypeStruct((8, 128), F32),
            jax.ShapeDtypeStruct((8, 128), F32),
            jax.ShapeDtypeStruct((NZ + 2 * EZ, EDGE, NY), BF16),
            jax.ShapeDtypeStruct((8, 128), F32),
            jax.ShapeDtypeStruct((8, 128), jnp.int32),
        ),
        in_specs=[smem] * 3 + [vmem] * 2,
        out_specs=(vmem,) * 7,
        scratch_shapes=[pltpu.SMEM((8,), jnp.int32)],
        cost_estimate=takes(2.0),
        name="ask",
    )(route, within, xshift, ref, deformed)


def gather_columns(table, slabs, sources, places):
    table[...] = jnp.zeros_like(table)
    shape = (EDGE, NY)
    row, lane = rows_of(shape), lanes(shape)
    for i, (source, place) in enumerate(zip(sources, places)):
        start = pl.multiple_of(i * NY + source * EDGE, EDGE)
        table[pl.ds(start, EDGE), :] = (lane == row + place * EDGE).astype(F32).astype(BF16)
    return jnp.dot(jnp.concatenate(slabs, axis=1), table[...], preferred_element_type=F32)


def serve_kernel(lines, *refs):
    count = len(lines)
    asked, outs = refs[3 : 3 + count], refs[3 + count : 3 + 2 * count]
    banks, tables, last, sem = refs[3 + 2 * count :]
    copy = pltpu.make_async_copy(asked[-1], last, sem)
    copy.start()
    asked = (*asked[:-1], last)
    for i in range(3):
        banks[i] = refs[i][0:NZ]
    for j in range(count):
        slabs, columns = [], []
        if j == count - 1:
            copy.wait()
        for slot in range(8):
            code = asked[j][lines[j], slot].astype(jnp.int32)
            slab = banks[code // NEL, pl.ds(lax.rem(code, NEL) // EYD * EDGE, EDGE)]
            slabs.append(slab.reshape(EDGE * EDGE, NY))
            columns.append(lax.rem(code, EYD))
        packed = gather_columns(tables.at[j], slabs, columns, range(8))
        outs[j][...] = packed.reshape(EDGE, EDGE, NY).astype(BF16)


def serve(own, d0, d1, asked, lines):
    smem = pl.BlockSpec(memory_space=pltpu.SMEM)
    vmem = pl.BlockSpec(memory_space=pltpu.VMEM)
    count = len(lines)
    return pl.pallas_call(
        functools.partial(serve_kernel, lines),
        out_shape=(jax.ShapeDtypeStruct((EDGE, EDGE, NY), BF16),) * count,
        in_specs=[vmem] * 3 + [smem] * (count - 1) + [vmem],
        out_specs=(vmem,) * count,
        scratch_shapes=[
            pltpu.VMEM((3, NZ, EDGE, NY), BF16),
            pltpu.VMEM((count, 8 * NY, NY), BF16),
            pltpu.SMEM((8, 128), F32),
            pltpu.SemaphoreType.DMA,
        ],
        compiler_params=pltpu.CompilerParams(vmem_limit_bytes=LIMIT),
        cost_estimate=takes(1.0 + 0.2 * count),
        name="serve",
    )(own, d0, d1, *asked)


def moments_kernel(gy_count, r1, r0, a1, a0, ref, frac, grad, packed, extra, portions, side, slabs):
    gx, gy = lax.axis_index("gx"), lax.axis_index("gy")
    gx_even, gy_even = even(gx), even(gy)
    side[...] = jnp.zeros((8, NZ * EDGE), F32)
    keep0 = jnp.where(gy_even, gy < gy_count - 1, gy > 0).astype(F32)
    keep1 = jnp.where(gy_even, gy > 0, gy < gy_count - 1).astype(F32)
    for i in range(8):
        side[0:1, i * 128 : (i + 1) * 128] = r0[i : i + 1, :] * keep0
        side[1:2, i * 128 : (i + 1) * 128] = r1[i : i + 1, :] * keep1
    row, lane = rows_of((8, 128)), lanes((8, 128))
    target0 = jnp.where(gy_even, NY - 1, 0)
    spot = jnp.where(row == 0, target0, jnp.where(row == 1, NY - 1 - target0, -1))
    spread = (lane == spot).astype(F32).astype(BF16)
    rim = lax.dot_general(
        side[...].astype(BF16), spread, (((0,), (0,)), ((), ())), preferred_element_type=F32
    ).reshape(NZ, EDGE, NY)
    low0, high0, low1, high1 = (
        thick[NZ + k * EZ : NZ + (k + 1) * EZ].astype(F32).reshape(NZ, NY) for thick in (a0, a1) for k in range(2)
    )
    before = jnp.where(gx_even, high1, high0)
    after = jnp.where(gx_even, low0, low1)
    lane2, row2 = lanes((EDGE, NY)), rows_of((EDGE, NY))
    for ez in range(EZ):
        collected = [[jnp.zeros((EDGE, NY), F32) for _ in range(3)] for _ in PAIRS]
        for k in range(EDGE):
            z = ez * EDGE + k
            plane = ref[z].astype(F32)
            below = ref[z - 1].astype(F32) if z > 0 else jnp.zeros((EDGE, NY), F32)
            above = ref[z + 1].astype(F32) if z + 1 < NZ else jnp.zeros((EDGE, NY), F32)
            rim_z = rim[z]
            nxt = jnp.where(row2 == EDGE - 1, after[z : z + 1, :], pltpu.roll(plane, EDGE - 1, 0))
            prv = jnp.where(row2 == 0, before[z : z + 1, :], pltpu.roll(plane, 1, 0))
            right = jnp.where(lane2 == NY - 1, rim_z, pltpu.roll(plane, NY - 1, 1))
            left = jnp.where(lane2 == 0, rim_z, pltpu.roll(plane, 1, 1))
            rounded = [((above - below) * 0.5).astype(BF16), ((nxt - prv) * 0.5).astype(BF16), ((right - left) * 0.5).astype(BF16)]
            for c in range(3):
                grad[c, z] = rounded[c]
            g = [value.astype(F32) for value in rounded]
            for p, (c, d) in enumerate(PAIRS):
                product = g[c] * g[d]
                for w in range(3):
                    collected[p][w] = collected[p][w] + float(PRODUCTS[w, k]) * product
        for p in range(len(PAIRS)):
            for w in range(3):
                start = (ez * 18 + p * 3 + w) * EDGE
                slabs[start : start + EDGE, :] = collected[p][w]
    found = weighed(slabs[...], along_y(hat_product, (0, 1, 2)))
    across = [hat_product(w, row2) for w in range(3)]
    row8, group8 = rows_of((8, 128)), lanes((8, 128)) // NEL
    tiles = [jnp.zeros((8, 128), F32) for _ in range(HROWS // 8 + 1)]
    for slab in range(18):
        for w in range(3):
            line = layered(found, slab, 18, across[w])
            source = slab * 3 + w
            if source < HROWS:
                tiles[source // 8] = jnp.where((row8 == source % 8) & (group8 < 3), line, tiles[source // 8])
            else:
                for wy in range(3):
                    spare = wy * 14 + source - HROWS
                    turned = pltpu.roll(line, (3 - wy) * NEL, 1)
                    tiles[spare // 8] = jnp.where((row8 == spare % 8) & (group8 == 3), turned, tiles[spare // 8])
    total = jnp.concatenate(tiles, axis=0)
    total = pltpu.roll(total, lax.rem(gx, 4) * NEL, 1)
    packed[...] = total[:HROWS]
    line = pltpu.roll(total[HROWS:], NEL, 1)[0:1] + pltpu.roll(total[HROWS:], 2 * NEL, 1)[1:2]
    extra[...] = jnp.where(row == 6, line, 0.0)
    element, lane_e = rows_of((EYD, 128)), lanes((EYD, 128))
    unfold = (lane_e // EDGE == element).astype(F32).astype(BF16)
    for ez in range(EZ):
        tenths = frac[ez * EYD : (ez + 1) * EYD, :].astype(F32).astype(BF16)
        wide = lax.dot_general(tenths, unfold, (((0,), (0,)), ((), ())), preferred_element_type=F32)
        portions[ez, 0:3, :] = wide * (1.0 / EDGE)


def moments(ref, faces_x, faces_y, fractions):
    vmem = pl.BlockSpec(memory_space=pltpu.VMEM)
    return pl.pallas_call(
        functools.partial(moments_kernel, lax.axis_size("gy")),
        out_shape=(
            jax.ShapeDtypeStruct((3, NZ, EDGE, NY), BF16),
            jax.ShapeDtypeStruct((HROWS, 128), F32),
            jax.ShapeDtypeStruct((8, 128), F32),
            jax.ShapeDtypeStruct((EZ, 8, 128), F32),
        ),
        in_specs=[vmem] * 6,
        out_specs=(vmem,) * 4,
        scratch_shapes=[pltpu.VMEM((8, NZ * EDGE), F32), pltpu.VMEM((EZ * 18 * EDGE, NY), F32)],
        compiler_params=pltpu.CompilerParams(vmem_limit_bytes=LIMIT),
        cost_estimate=takes(2.2),
        name="moments",
    )(faces_y[1], faces_y[0], faces_x[1], faces_x[0], ref, fractions)


def warp_kernel(b0, b1, b2, b3, b4, place, ref, grad, portions, extra, mismatch, packed, bricks, tables, slabs, spots, sem):
    gx = lax.axis_index("gx")
    copy = pltpu.make_async_copy(place, spots, sem)
    copy.start()
    for i, source in zip((*KINDS, 4), (b0, b1, b2, b3, b4)):
        bricks[i] = source[...]
    copy.wait()
    flat = (EDGE * EDGE, NY)
    lane = lanes(flat)
    at_x_rim = lax.rem(lax.broadcasted_iota(jnp.int32, flat, 0), EDGE) == EDGE - 1
    at_y_rim = lax.rem(lane, EDGE) == EDGE - 1
    for ez in range(EZ):
        codes = [spots[0, ez * EYD + b] for b in range(EYD)]
        found = [bricks[code // 8].reshape(flat) for code in codes]
        blended = gather_columns(tables.at[ez], found, [lax.rem(code, 8) for code in codes], range(EYD))
        portion = portions[ez]
        ty, tx, tz = portion[2:3, :], portion[1:2, :], portion[0:1, :]
        shifted = jnp.where(at_y_rim, blended, pltpu.roll(blended, NY - 1, 1))
        blended = (1.0 - ty) * blended + ty * shifted
        shifted = jnp.where(at_x_rim, blended, pltpu.roll(blended, EDGE * EDGE - 1, 0))
        blended = (1.0 - tx) * blended + tx * shifted
        shifted = jnp.concatenate([blended[EDGE:], blended[-EDGE:]], axis=0)
        blended = (1.0 - tz) * blended + tz * shifted
        blended = blended.reshape(EDGE, EDGE, NY)
        collected = [[jnp.zeros((EDGE, NY), F32) for _ in range(2)] for _ in range(3)]
        for k in range(EDGE):
            z = ez * EDGE + k
            apart = ref[z].astype(F32) - blended[k]
            mismatch[z] = apart
            for c in range(3):
                term = grad[c, z].astype(F32) * apart
                for a in range(2):
                    collected[c][a] = collected[c][a] + float(HAT[a, k]) * term
        for c in range(3):
            for a in range(2):
                start = (ez * 6 + c * 2 + a) * EDGE
                slabs[start : start + EDGE, :] = collected[c][a]
    found = weighed_once(slabs[...], along_y(lambda group, at: hat_weight(lax.rem(group, 2), at), (0, 1, 2, 3)))
    across = hat_weight(lanes((EDGE, 128)) // (2 * NEL), rows_of((EDGE, 128)))
    row8 = rows_of((8, 128))
    total = jnp.zeros((8, 128), F32)
    for slab in range(6):
        total = jnp.where(row8 == slab, layered(found, slab, 6, across), total)
    packed[...] = jnp.broadcast_to(pltpu.roll(total, lax.rem(gx, 4) * NEL, 1) + extra[...], packed.shape)


def warp(place, bricks, ref, grad, portions, extra):
    vmem = pl.BlockSpec(memory_space=pltpu.VMEM)
    devices = lax.axis_size("gx") * lax.axis_size("gy")
    return pl.pallas_call(
        warp_kernel,
        out_shape=(jax.ShapeDtypeStruct((NZ, EDGE, NY), F32), jax.ShapeDtypeStruct((devices, 8, 128), F32)),
        in_specs=[vmem] * 10,
        out_specs=(vmem, vmem),
        scratch_shapes=[
            pltpu.VMEM((5, EDGE, EDGE, NY), BF16),
            pltpu.VMEM((EZ, EYD * NY, NY), BF16),
            pltpu.VMEM((EZ * 6 * EDGE, NY), F32),
            pltpu.SMEM((8, 128), jnp.int32),
            pltpu.SemaphoreType.DMA,
        ],
        compiler_params=pltpu.CompilerParams(vmem_limit_bytes=LIMIT),
        cost_estimate=takes(4.0),
        name="warp",
    )(*bricks, place, ref, grad, portions, extra)


def spread_groups(block_of, groups, gx_count, store):
    tiles = -(-gx_count // 4)
    for tile in range(tiles):
        members = range(4 * tile, min(4 * tile + 4, gx_count))
        blocks = {gx: block_of(gx) for gx in members}
        for group in range(groups):
            merged = jnp.zeros_like(blocks[members[0]])
            lane = lanes(merged.shape)
            for gx in members:
                merged = jnp.where(lane // NEL == (group + gx) % 4, blocks[gx], merged)
            store(group, tile, pltpu.roll(merged, (128 - NEL * group) % 128, 1) if group else merged)


def solve_kernel(gx_count, gy_count, first, second, load, out, coef, rhs):
    gx, gy = lax.axis_index("gx"), lax.axis_index("gy")
    orders = gather_orders(gx_count, gy_count)
    tiles = -(-gx_count // 4)
    width = 128 * tiles

    def unpack(row, _):
        def hess_block(column):
            relative = dict(gx=jnp.bitwise_xor(gx, column), gy=jnp.bitwise_xor(gy, row))
            parts = [half[block_index(order, relative)] for half, order in zip((first, second), orders)]
            return jnp.concatenate(parts, axis=0)

        def store_hess(group, tile, value):
            coef[tile, pl.ds(row * 4 * HROWS + group * HROWS, HROWS), :] = value

        def load_block(column):
            return load[column * gy_count + row]

        def store_load(group, tile, value):
            rhs[tile, pl.ds(row * 32 + group * 8, 8), :] = value

        spread_groups(hess_block, 4, gx_count, store_hess)
        spread_groups(load_block, 4, gx_count, store_load)
        return 0

    lax.fori_loop(0, gy_count, unpack, 0)
    shape = (gy_count, width)
    lane, row = lanes(shape), rows_of(shape)
    in_z, in_y, in_x = lax.rem(lane, NEL) // EYD, lax.rem(lane, EYD), lane // NEL
    last_z, first_z = in_z == EZ - 1, in_z == 0
    last_x, first_x = in_x >= gx_count - 1, in_x == 0
    last_y, first_y = in_y == EYD - 1, in_y == 0
    end_y, begin_y = last_y & (row == gy_count - 1), first_y & (row == 0)

    def turn(value, by, axis):
        size = shape[axis]
        by = by % size
        return pltpu.roll(value, by, axis) if by else value

    def corners(main, top):
        found = []
        for a in range(2):
            z_part = main if a == 0 else jnp.where(last_z, top, turn(main, -EYD, 1))
            for b in range(2):
                x_part = z_part if b == 0 else jnp.where(last_x, 0.0, turn(z_part, -NEL, 1))
                for d in range(2):
                    if d == 0:
                        found.append(x_part)
                    else:
                        wrapped = turn(turn(x_part, -1, 0), EYD - 1, 1)
                        moved = jnp.where(last_y, wrapped, turn(x_part, -1, 1))
                        found.append(jnp.where(end_y, 0.0, moved))
        return found

    def settle(parts):
        z_parts = []
        for a in range(2):
            x_parts = []
            for b in range(2):
                base, extra = parts[a * 4 + b * 2], parts[a * 4 + b * 2 + 1]
                wrapped = turn(turn(extra, 1, 0), 1 - EYD, 1)
                moved = jnp.where(first_y, wrapped, turn(extra, 1, 1))
                x_parts.append(base + jnp.where(begin_y, 0.0, moved))
            z_parts.append(x_parts[0] + jnp.where(first_x, 0.0, turn(x_parts[1], NEL, 1)))
        main = z_parts[0] + jnp.where(first_z, 0.0, turn(z_parts[1], EYD, 1))
        return main, jnp.where(last_z, z_parts[1], 0.0)

    def strided(ref, start, stride):
        found = [ref[tile, pl.ds(start, gy_count, stride=stride), :] for tile in range(tiles)]
        return found[0] if tiles == 1 else jnp.concatenate(found, axis=1)

    def channel(p, wz, wx, wy):
        source = (p * 3 + wz) * 3 + wx
        if source < HROWS:
            return strided(coef, wy * HROWS + source, 4 * HROWS)
        spare = wy * 14 + source - HROWS
        if spare < HROWS:
            return strided(coef, 3 * HROWS + spare, 4 * HROWS)
        return strided(rhs, (spare - HROWS) * 8 + 6, 32)

    pair_of = {}
    for p, (c, d) in enumerate(PAIRS):
        pair_of[c, d] = pair_of[d, c] = p
    bits = [(a, b, d) for a in range(2) for b in range(2) for d in range(2)]

    def curved_by(vector):
        known = [corners(main, top) for main, top in vector]
        sums = [[None] * 8 for _ in range(3)]

        def add(c, n, term):
            sums[c][n] = term if sums[c][n] is None else sums[c][n] + term

        for p, (c, d) in enumerate(PAIRS):
            for wz in range(3):
                for wx in range(3):
                    for wy in range(3):
                        factor = channel(p, wz, wx, wy)
                        for n, low in enumerate(bits):
                            for m, high in enumerate(bits):
                                if (low[0] + high[0], low[1] + high[1], low[2] + high[2]) == (wz, wx, wy):
                                    add(c, n, factor * known[d][m])
                                    if c != d:
                                        add(d, n, factor * known[c][m])
        result = []
        for c in range(3):
            main, top = settle(sums[c])
            result.append((main + LAMBDA * vector[c][0], top + LAMBDA * vector[c][1]))
        bent = sum(known[c][n] * sums[c][n] for c in range(3) for n in range(8))
        return result, total(bent) + LAMBDA * inner(vector, vector)

    def total(value):
        return jnp.sum(jnp.sum(value, axis=0, keepdims=True), axis=1, keepdims=True)

    def inner(one, two):
        return total(sum(a[0] * b[0] + a[1] * b[1] for a, b in zip(one, two)))

    def combine(one, factor, two):
        return [(a[0] + factor * b[0], a[1] + factor * b[1]) for a, b in zip(one, two)]

    residual = []
    for c in range(3):
        parts = [strided(rhs, (b * 2 + d) * 8 + c * 2 + a, 32) for a, b, d in bits]
        residual.append(settle(parts))
    direction = residual
    increment = None
    norm_now = inner(residual, residual)
    for iteration in range(ITERS):
        curved, bent = curved_by(direction)
        step = norm_now / bent
        if increment is None:
            increment = [(step * a, step * b) for a, b in direction]
        else:
            increment = combine(increment, step, direction)
        if iteration + 1 < ITERS:
            residual = combine(residual, -step, curved)
            norm_next = inner(residual, residual)
            direction = combine(residual, norm_next / norm_now, direction)
            norm_now = norm_next
    mine = (row == gy) & (in_x == gx)
    for c in range(3):
        for part, levels in ((increment[c][0], range(EZ)), (increment[c][1], [EZ])):
            line = jnp.sum(jnp.where(mine, part, 0.0), axis=0, keepdims=True)
            short = line[:, 0:128]
            for tile in range(1, tiles):
                short = short + line[:, tile * 128 : (tile + 1) * 128]
            short = pltpu.roll(jnp.broadcast_to(short, (8, 128)), lax.rem(128 - lax.rem(gx, 4) * NEL, 128), 1)
            for level in levels:
                start = min(level, EZ - 1) * EYD
                out[c, level] = short[0:1, start : start + EYD]


def solve(first, second, load):
    gx_count, gy_count = lax.axis_size("gx"), lax.axis_size("gy")
    tiles = -(-gx_count // 4)
    vmem = pl.BlockSpec(memory_space=pltpu.VMEM)
    return pl.pallas_call(
        functools.partial(solve_kernel, gx_count, gy_count),
        out_shape=jax.ShapeDtypeStruct((3, EZ + 1, 1, EYD), F32),
        in_specs=[vmem] * 3,
        out_specs=vmem,
        scratch_shapes=[
            pltpu.VMEM((tiles, gy_count * 4 * HROWS, 128), F32),
            pltpu.VMEM((tiles, gy_count * 32, 128), F32),
        ],
        compiler_params=pltpu.CompilerParams(vmem_limit_bytes=LIMIT),
        cost_estimate=takes(3.5),
        name="solve",
    )(first, second, load)


def swap(array, axis, partner):
    size = lax.axis_size(axis)
    pairs = [(i, partner(i)) for i in range(size)]
    return lax.ppermute(array, axis, [(i, j) for i, j in pairs if 0 <= j < size])


def swap_x(array, kind):
    if kind == 0:
        return swap(array, "gx", lambda i: i ^ 1)
    return swap(array, "gx", lambda i: i + 1 if i % 2 else i - 1)


def swap_y(array, kind):
    size = lax.axis_size("gy")
    partner = (
        lambda i: i ^ 1,
        lambda i: (i + 1 if i % 2 else i - 1) % size,
        lambda i: i ^ 2,
        lambda i: (i + 2 if i // 2 % 2 else i - 2) % size,
    )[kind]
    return swap(array, "gy", partner)


def gather_steps(gx_count, gy_count):
    far = [("gy", 1 << k) for k in range(1, gy_count.bit_length() - 1)]
    return [*far, ("gy", 1), *[("gx", 1 << k) for k in reversed(range(gx_count.bit_length() - 1))]]


def gather_orders(gx_count, gy_count):
    steps = gather_steps(gx_count, gy_count)
    return steps, [*steps[:-3], steps[-2], steps[-3], steps[-1]]


def block_index(steps, relative):
    found = 0
    for k, (axis, bit) in enumerate(steps):
        found = found + jnp.where(jnp.bitwise_and(relative[axis], bit) != 0, 1 << k, 0)
    return found


def doubled(known, step, pieces=1):
    axis, bit = step
    size = known.shape[0] // pieces
    sent = [swap(known[i * size : (i + 1) * size], axis, lambda j: j ^ bit) for i in range(pieces)]
    return jnp.concatenate([known, *sent], axis=0)


def body(reference_image, deformed_image, route, within, xshift, fractions):
    m0, m1, m2, m3, thick, own, place = ask(
        route.reshape(NEL), within.reshape(NEL), xshift.reshape(NEL), reference_image, deformed_image
    )
    asks = (m0, m1, m2, m3)
    q = {kind: swap_y(asks[kind], kind) for kind in KINDS}
    d1, d0 = swap_x(thick, 1), swap_x(thick, 0)
    grad, packed, extra, portions = moments(reference_image, (d0, d1), (q[0], q[1]), fractions.reshape(NEL, 3))
    *served, at_home = serve(deformed_image, d0, d1, [q[kind] for kind in KINDS] + [own], [8 * (k < 2) + k for k in KINDS] + [4])
    known, at_home = lax.optimization_barrier((packed[None], at_home))
    bricks = [swap_y(block, kind) for kind, block in zip(KINDS, served)] + [at_home]
    orders = gather_orders(lax.axis_size("gx"), lax.axis_size("gy"))
    steps = orders[0]
    for step in steps[:-4]:
        known = doubled(known, step)
    bricks, known = lax.optimization_barrier((bricks, known))
    mismatch, part = warp(place, bricks, reference_image, grad, portions, extra)
    known = doubled(known, steps[-4])
    known, part = lax.optimization_barrier((known, part))
    load = lax.all_to_all(part, ("gx", "gy"), 0, 0)
    halves = [known[:, :SPLIT], known[:, SPLIT:]]
    for k in (-3, -2, -1):
        halves = [doubled(half, order[k], 2 if k == -1 else 1) for half, order in zip(halves, orders)]
    return solve(*halves, load), mismatch


def solution(mesh):
    placed = (
        P(None, "gx", "gy"),
        P(None, "gx", "gy"),
        P("gx", "gy", None, None),
        P("gx", "gy", None),
        P("gx", "gy", None),
        P("gx", "gy", None, None),
    )
    return jax.shard_map(
        body,
        mesh=mesh,
        in_specs=placed,
        out_specs=(P(None, None, "gx", "gy"), P(None, "gx", "gy")),
        check_vma=False,
    )
```

```python
import functools

import jax
import jax.numpy as jnp
import numpy as np
from jax import lax
from jax.experimental import pallas as pl
from jax.experimental.pallas import tpu as pltpu
from jax.sharding import PartitionSpec as P

EDGE = 16
EZ = 4
EYD = 8
SPAN = 2
ITERS = 3
NEL = 32
VOL = 4096
NZ = EZ * EDGE
NY = EYD * EDGE
LAMBDA = 0.05

PAIRS = ((0, 0), (0, 1), (0, 2), (1, 1), (1, 2), (2, 2))
HROWS = 40
KINDS = (3, 0, 1, 2)
LIMIT = 32 * 1024 * 1024

F32 = jnp.float32
BF16 = jnp.bfloat16

UPPER = (np.arange(EDGE) + 0.5) / EDGE
HAT = np.stack([1.0 - UPPER, UPPER])
PRODUCTS = np.stack([HAT[0] * HAT[0], HAT[0] * HAT[1], HAT[1] * HAT[1]])


def hat_product(which, position):
    upper = (position.astype(F32) + 0.5) * (1.0 / EDGE)
    lower = 1.0 - upper
    return jnp.where(which == 0, lower * lower, jnp.where(which == 1, lower * upper, upper * upper))


def hat_weight(which, position):
    upper = (position.astype(F32) + 0.5) * (1.0 / EDGE)
    return jnp.where(which == 0, 1.0 - upper, upper)


def along_y(weight, groups):
    shape = (NY, 128)
    row, lane = rows_of(shape), lanes(shape)
    group = lane // NEL
    inside = (row // EDGE == lax.rem(lane, NEL)) & (group >= groups[0]) & (group <= groups[-1])
    return jnp.where(inside, weight(group, lax.rem(row, EDGE)) * (1.0 / VOL), 0.0)


def three_parts(value):
    high = value.astype(BF16)
    rest = value - high.astype(F32)
    middle = rest.astype(BF16)
    return [high, middle, (rest - middle.astype(F32)).astype(BF16)]


def weighed(value, weights):
    high = weights.astype(BF16)
    both = jnp.concatenate([high, (weights - high.astype(F32)).astype(BF16)], axis=1)
    found = jnp.dot(
        jnp.concatenate(three_parts(value), axis=1),
        jnp.concatenate([both] * 3, axis=0),
        preferred_element_type=F32,
    )
    return found[:, :128] + found[:, 128:]


def weighed_once(value, weights):
    weights = weights.astype(BF16)
    return jnp.dot(
        jnp.concatenate(three_parts(value), axis=1),
        jnp.concatenate([weights] * 3, axis=0),
        preferred_element_type=F32,
    )


def layered(found, slab, slabs, weights):
    total = None
    for ez in range(EZ):
        start = (ez * slabs + slab) * EDGE
        part = found[start : start + EDGE] * weights
        part = part[:8] + part[8:]
        part = pltpu.roll(part, ez * EYD, 1) if ez else part
        total = part if total is None else total + part
    return jnp.sum(total, axis=0, keepdims=True)


def lanes(shape):
    return lax.broadcasted_iota(jnp.int32, shape, len(shape) - 1)


def rows_of(shape):
    return lax.broadcasted_iota(jnp.int32, shape, len(shape) - 2)


def even(value):
    return lax.rem(value, 2) == 0


def takes(microseconds):
    return pl.CostEstimate(flops=0, bytes_accessed=int(microseconds * 3.69e6), transcendentals=0)


def ask_kernel(gx_count, route, within, xshift, ref, deformed, m0, m1, m2, m3, thick, own, place, count):
    gx, gy = lax.axis_index("gx"), lax.axis_index("gy")
    for j in range(5):
        count[j] = 0
    gx_even, gy_even, half_even = even(gx), even(gy), even(gy // 2)
    row, lane = rows_of((8, 128)), lanes((8, 128))

    def visit(e, found):
        offset = route[e] - SPAN
        moved = jnp.clip(gx + xshift[e] - 1, 0, gx_count - 1) - gx
        ahead = jnp.where(gx_even, 1, 2)
        bank = jnp.where(moved == 0, 0, jnp.where(moved == 1, ahead, 3 - ahead))
        code = bank * NEL + (e // EYD) * EYD + within[e]
        near = jnp.where((offset == 1) == gy_even, 0, 1)
        far = jnp.where((offset == 2) == half_even, 2, 3)
        j = jnp.where(offset == 0, 4, jnp.where(jnp.abs(offset) == 1, near, far))
        slot = count[j]
        count[j] = slot + 1
        asked, places = found
        asked = jnp.where((row == j) & (lane == slot), code.astype(F32), asked)
        return asked, jnp.where(lane == e, j * 8 + slot, places)

    zero = jnp.zeros((8, 128), jnp.int32)
    asked, places = lax.fori_loop(0, NEL, visit, (zero.astype(F32), zero), unroll=True)
    place[...] = places
    own[...] = asked
    m2[...] = asked
    m3[...] = asked
    m0[8:, :] = asked
    m1[8:, :] = asked
    image = ref[...]
    first = jnp.where(gy_even, NY - 1, 0)
    wanted = jnp.where(row == 0, first, jnp.where(row == 1, NY - 1 - first, -1))
    pick = (lane == wanted).astype(F32).astype(BF16)
    columns = lax.dot_general(pick, image.reshape(NZ * EDGE, NY), (((1,), (1,)), ((), ())), preferred_element_type=F32)
    for i in range(8):
        m0[i : i + 1, :] = columns[0:1, i * 128 : (i + 1) * 128]
        m1[i : i + 1, :] = columns[1:2, i * 128 : (i + 1) * 128]
    thick[0:NZ] = deformed[...]
    image = image.astype(F32)
    for k, face in enumerate((image[:, 0, :], image[:, EDGE - 1, :])):
        thick[NZ + k * EZ : NZ + (k + 1) * EZ] = face.astype(BF16).reshape(EZ, EDGE, NY)


def ask(route, within, xshift, ref, deformed):
    smem = pl.BlockSpec(memory_space=pltpu.SMEM)
    vmem = pl.BlockSpec(memory_space=pltpu.VMEM)
    return pl.pallas_call(
        functools.partial(ask_kernel, lax.axis_size("gx")),
        out_shape=(
            jax.ShapeDtypeStruct((16, 128), F32),
            jax.ShapeDtypeStruct((16, 128), F32),
            jax.ShapeDtypeStruct((8, 128), F32),
            jax.ShapeDtypeStruct((8, 128), F32),
            jax.ShapeDtypeStruct((NZ + 2 * EZ, EDGE, NY), BF16),
            jax.ShapeDtypeStruct((8, 128), F32),
            jax.ShapeDtypeStruct((8, 128), jnp.int32),
        ),
        in_specs=[smem] * 3 + [vmem] * 2,
        out_specs=(vmem,) * 7,
        scratch_shapes=[pltpu.SMEM((8,), jnp.int32)],
        cost_estimate=takes(2.0),
        name="ask",
    )(route, within, xshift, ref, deformed)


def gather_columns(table, slabs, sources, places):
    table[...] = jnp.zeros_like(table)
    shape = (EDGE, NY)
    row, lane = rows_of(shape), lanes(shape)
    for i, (source, place) in enumerate(zip(sources, places)):
        start = pl.multiple_of(i * NY + source * EDGE, EDGE)
        table[pl.ds(start, EDGE), :] = (lane == row + place * EDGE).astype(F32).astype(BF16)
    return jnp.dot(jnp.concatenate(slabs, axis=1), table[...], preferred_element_type=F32)


def serve_kernel(lines, *refs):
    count = len(lines)
    asked, outs = refs[3 : 3 + count], refs[3 + count : 3 + 2 * count]
    banks, tables, last, sem = refs[3 + 2 * count :]
    copy = pltpu.make_async_copy(asked[-1], last, sem)
    copy.start()
    asked = (*asked[:-1], last)
    for i in range(3):
        banks[i] = refs[i][0:NZ]
    for j in range(count):
        slabs, columns = [], []
        if j == count - 1:
            copy.wait()
        for slot in range(8):
            code = asked[j][lines[j], slot].astype(jnp.int32)
            slab = banks[code // NEL, pl.ds(lax.rem(code, NEL) // EYD * EDGE, EDGE)]
            slabs.append(slab.reshape(EDGE * EDGE, NY))
            columns.append(lax.rem(code, EYD))
        packed = gather_columns(tables.at[j], slabs, columns, range(8))
        outs[j][...] = packed.reshape(EDGE, EDGE, NY).astype(BF16)


def serve(own, d0, d1, asked, lines):
    smem = pl.BlockSpec(memory_space=pltpu.SMEM)
    vmem = pl.BlockSpec(memory_space=pltpu.VMEM)
    count = len(lines)
    return pl.pallas_call(
        functools.partial(serve_kernel, lines),
        out_shape=(jax.ShapeDtypeStruct((EDGE, EDGE, NY), BF16),) * count,
        in_specs=[vmem] * 3 + [smem] * (count - 1) + [vmem],
        out_specs=(vmem,) * count,
        scratch_shapes=[
            pltpu.VMEM((3, NZ, EDGE, NY), BF16),
            pltpu.VMEM((count, 8 * NY, NY), BF16),
            pltpu.SMEM((8, 128), F32),
            pltpu.SemaphoreType.DMA,
        ],
        compiler_params=pltpu.CompilerParams(vmem_limit_bytes=LIMIT),
        cost_estimate=takes(1.0 + 0.2 * count),
        name="serve",
    )(own, d0, d1, *asked)


def moments_kernel(gy_count, r0, r1, a1, a0, ref, frac, grad, packed, extra, portions, side, slabs):
    gx, gy = lax.axis_index("gx"), lax.axis_index("gy")
    gx_even, gy_even = even(gx), even(gy)
    side[...] = jnp.zeros((8, NZ * EDGE), F32)
    keep0 = jnp.where(gy_even, gy < gy_count - 1, gy > 0).astype(F32)
    keep1 = jnp.where(gy_even, gy > 0, gy < gy_count - 1).astype(F32)
    for i in range(8):
        side[0:1, i * 128 : (i + 1) * 128] = r0[i : i + 1, :] * keep0
        side[1:2, i * 128 : (i + 1) * 128] = r1[i : i + 1, :] * keep1
    row, lane = rows_of((8, 128)), lanes((8, 128))
    target0 = jnp.where(gy_even, NY - 1, 0)
    spot = jnp.where(row == 0, target0, jnp.where(row == 1, NY - 1 - target0, -1))
    spread = (lane == spot).astype(F32).astype(BF16)
    rim = lax.dot_general(
        side[...].astype(BF16), spread, (((0,), (0,)), ((), ())), preferred_element_type=F32
    ).reshape(NZ, EDGE, NY)
    low0, high0, low1, high1 = (
        thick[NZ + k * EZ : NZ + (k + 1) * EZ].astype(F32).reshape(NZ, NY) for thick in (a0, a1) for k in range(2)
    )
    before = jnp.where(gx_even, high1, high0)
    after = jnp.where(gx_even, low0, low1)
    lane2, row2 = lanes((EDGE, NY)), rows_of((EDGE, NY))
    for ez in range(EZ):
        collected = [[jnp.zeros((EDGE, NY), F32) for _ in range(3)] for _ in PAIRS]
        for k in range(EDGE):
            z = ez * EDGE + k
            plane = ref[z].astype(F32)
            below = ref[z - 1].astype(F32) if z > 0 else jnp.zeros((EDGE, NY), F32)
            above = ref[z + 1].astype(F32) if z + 1 < NZ else jnp.zeros((EDGE, NY), F32)
            rim_z = rim[z]
            nxt = jnp.where(row2 == EDGE - 1, after[z : z + 1, :], pltpu.roll(plane, EDGE - 1, 0))
            prv = jnp.where(row2 == 0, before[z : z + 1, :], pltpu.roll(plane, 1, 0))
            right = jnp.where(lane2 == NY - 1, rim_z, pltpu.roll(plane, NY - 1, 1))
            left = jnp.where(lane2 == 0, rim_z, pltpu.roll(plane, 1, 1))
            rounded = [((above - below) * 0.5).astype(BF16), ((nxt - prv) * 0.5).astype(BF16), ((right - left) * 0.5).astype(BF16)]
            for c in range(3):
                grad[c, z] = rounded[c]
            g = [value.astype(F32) for value in rounded]
            for p, (c, d) in enumerate(PAIRS):
                product = g[c] * g[d]
                for w in range(3):
                    collected[p][w] = collected[p][w] + float(PRODUCTS[w, k]) * product
        for p in range(len(PAIRS)):
            for w in range(3):
                start = (ez * 18 + p * 3 + w) * EDGE
                slabs[start : start + EDGE, :] = collected[p][w]
    found = weighed(slabs[...], along_y(hat_product, (0, 1, 2)))
    across = [hat_product(w, row2) for w in range(3)]
    row8, group8 = rows_of((8, 128)), lanes((8, 128)) // NEL
    tiles = [jnp.zeros((8, 128), F32) for _ in range(HROWS // 8 + 1)]
    for slab in range(18):
        for w in range(3):
            line = layered(found, slab, 18, across[w])
            source = slab * 3 + w
            if source < HROWS:
                tiles[source // 8] = jnp.where((row8 == source % 8) & (group8 < 3), line, tiles[source // 8])
            else:
                for wy in range(3):
                    spare = wy * 14 + source - HROWS
                    turned = pltpu.roll(line, (3 - wy) * NEL, 1)
                    tiles[spare // 8] = jnp.where((row8 == spare % 8) & (group8 == 3), turned, tiles[spare // 8])
    total = jnp.concatenate(tiles, axis=0)
    total = pltpu.roll(total, lax.rem(gx, 4) * NEL, 1)
    packed[...] = total[:HROWS]
    line = pltpu.roll(total[HROWS:], NEL, 1)[0:1] + pltpu.roll(total[HROWS:], 2 * NEL, 1)[1:2]
    extra[...] = jnp.where(row == 3, line, 0.0)
    element, lane_e = rows_of((EYD, 128)), lanes((EYD, 128))
    unfold = (lane_e // EDGE == element).astype(F32).astype(BF16)
    for ez in range(EZ):
        tenths = frac[ez * EYD : (ez + 1) * EYD, :].astype(F32).astype(BF16)
        wide = lax.dot_general(tenths, unfold, (((0,), (0,)), ((), ())), preferred_element_type=F32)
        portions[ez, 0:3, :] = wide * (1.0 / EDGE)


def moments(ref, faces_x, faces_y, fractions):
    vmem = pl.BlockSpec(memory_space=pltpu.VMEM)
    return pl.pallas_call(
        functools.partial(moments_kernel, lax.axis_size("gy")),
        out_shape=(
            jax.ShapeDtypeStruct((3, NZ, EDGE, NY), BF16),
            jax.ShapeDtypeStruct((HROWS, 128), F32),
            jax.ShapeDtypeStruct((8, 128), F32),
            jax.ShapeDtypeStruct((EZ, 8, 128), F32),
        ),
        in_specs=[vmem] * 6,
        out_specs=(vmem,) * 4,
        scratch_shapes=[pltpu.VMEM((8, NZ * EDGE), F32), pltpu.VMEM((EZ * 18 * EDGE, NY), F32)],
        compiler_params=pltpu.CompilerParams(vmem_limit_bytes=LIMIT),
        cost_estimate=takes(2.2),
        name="moments",
    )(faces_y[0], faces_y[1], faces_x[1], faces_x[0], ref, fractions)


def warp_kernel(b0, b1, b2, b3, b4, place, ref, grad, portions, extra, mismatch, packed, bricks, tables, slabs, spots, sem):
    gx = lax.axis_index("gx")
    copy = pltpu.make_async_copy(place, spots, sem)
    copy.start()
    for i, source in zip((*KINDS, 4), (b0, b1, b2, b3, b4)):
        bricks[i] = source[...]
    copy.wait()
    flat = (EDGE * EDGE, NY)
    lane = lanes(flat)
    at_x_rim = lax.rem(lax.broadcasted_iota(jnp.int32, flat, 0), EDGE) == EDGE - 1
    at_y_rim = lax.rem(lane, EDGE) == EDGE - 1
    for ez in range(EZ):
        codes = [spots[0, ez * EYD + b] for b in range(EYD)]
        found = [bricks[code // 8].reshape(flat) for code in codes]
        blended = gather_columns(tables.at[ez], found, [lax.rem(code, 8) for code in codes], range(EYD))
        portion = portions[ez]
        ty, tx, tz = portion[2:3, :], portion[1:2, :], portion[0:1, :]
        shifted = jnp.where(at_y_rim, blended, pltpu.roll(blended, NY - 1, 1))
        blended = (1.0 - ty) * blended + ty * shifted
        shifted = jnp.where(at_x_rim, blended, pltpu.roll(blended, EDGE * EDGE - 1, 0))
        blended = (1.0 - tx) * blended + tx * shifted
        shifted = jnp.concatenate([blended[EDGE:], blended[-EDGE:]], axis=0)
        blended = (1.0 - tz) * blended + tz * shifted
        blended = blended.reshape(EDGE, EDGE, NY)
        collected = [[jnp.zeros((EDGE, NY), F32) for _ in range(2)] for _ in range(3)]
        for k in range(EDGE):
            z = ez * EDGE + k
            apart = ref[z].astype(F32) - blended[k]
            mismatch[z] = apart
            for c in range(3):
                term = grad[c, z].astype(F32) * apart
                for a in range(2):
                    collected[c][a] = collected[c][a] + float(HAT[a, k]) * term
        for c in range(3):
            for a in range(2):
                start = (ez * 6 + c * 2 + a) * EDGE
                slabs[start : start + EDGE, :] = collected[c][a]
    found = weighed_once(slabs[...], along_y(lambda group, at: hat_weight(lax.rem(group, 2), at), (0, 1, 2, 3)))
    across = hat_weight(lanes((EDGE, 128)) // (2 * NEL), rows_of((EDGE, 128)))
    row, lane = rows_of((8, 128)), lanes((8, 128))
    group, in_z, in_y = lane // NEL, lax.rem(lane, NEL) // EYD, lax.rem(lane, EYD)
    total = jnp.zeros((8, 128), F32)
    for c in range(3):
        lower, upper = (layered(found, c * 2 + a, 6, across) for a in range(2))
        lower, upper = (jnp.broadcast_to(line, (8, 128)) for line in (lower, upper))
        level = lower + jnp.where(in_z > 0, pltpu.roll(upper, EYD, 1), 0.0)
        top = jnp.where(in_z == EZ - 1, upper, 0.0)

        def joined(line):
            return line + jnp.where(in_y > 0, pltpu.roll(line, 128 - NEL + 1, 1), 0.0)

        rim = jnp.where(in_y == EYD - 1, level, 0.0) + jnp.where(in_y == EYD - 2, pltpu.roll(top, 127, 1), 0.0)
        main = jnp.where(lax.rem(group, 2) == 0, joined(level), rim)
        total = jnp.where(row == c, main, total)
        top = joined(top)
        for bx in range(2):
            start = 2 * NEL + (c * 2 + bx) * EYD
            moved = pltpu.roll(top, (start - (bx * 2 * NEL + (EZ - 1) * EYD)) % 128, 1)
            total = jnp.where((row == 3) & (lane // EYD == start // EYD), moved, total)
    total = pltpu.roll(total, lax.rem(gx, 4) * NEL, 1) + extra[...]
    packed[...] = jnp.broadcast_to(total[0:4], packed.shape)


def warp(place, bricks, ref, grad, portions, extra):
    vmem = pl.BlockSpec(memory_space=pltpu.VMEM)
    devices = lax.axis_size("gx") * lax.axis_size("gy")
    return pl.pallas_call(
        warp_kernel,
        out_shape=(jax.ShapeDtypeStruct((NZ, EDGE, NY), F32), jax.ShapeDtypeStruct((devices, 4, 128), F32)),
        in_specs=[vmem] * 10,
        out_specs=(vmem, vmem),
        scratch_shapes=[
            pltpu.VMEM((5, EDGE, EDGE, NY), BF16),
            pltpu.VMEM((EZ, EYD * NY, NY), BF16),
            pltpu.VMEM((EZ * 6 * EDGE, NY), F32),
            pltpu.SMEM((8, 128), jnp.int32),
            pltpu.SemaphoreType.DMA,
        ],
        compiler_params=pltpu.CompilerParams(vmem_limit_bytes=LIMIT),
        cost_estimate=takes(4.0),
        name="warp",
    )(*bricks, place, ref, grad, portions, extra)


def spread_groups(block_of, groups, gx_count, store):
    tiles = -(-gx_count // 4)
    for tile in range(tiles):
        members = range(4 * tile, min(4 * tile + 4, gx_count))
        blocks = {gx: block_of(gx) for gx in members}
        for group in range(groups):
            merged = jnp.zeros_like(blocks[members[0]])
            lane = lanes(merged.shape)
            for gx in members:
                merged = jnp.where(lane // NEL == (group + gx) % 4, blocks[gx], merged)
            store(group, tile, pltpu.roll(merged, (128 - NEL * group) % 128, 1) if group else merged)


def solve_kernel(gx_count, gy_count, hess, load, out, coef, rhs):
    gx, gy = lax.axis_index("gx"), lax.axis_index("gy")
    steps = gather_steps(gx_count, gy_count)
    tiles = -(-gx_count // 4)
    width = 128 * tiles

    def unpack(row, _):
        def hess_block(column):
            relative = dict(gx=jnp.bitwise_xor(gx, column), gy=jnp.bitwise_xor(gy, row))
            return hess[block_index(steps, relative)]

        def store_hess(group, tile, value):
            coef[tile, pl.ds(row * 4 * HROWS + group * HROWS, HROWS), :] = value

        def load_block(column):
            return load[column * gy_count + row]

        def store_load(group, tile, value):
            rhs[tile, pl.ds(row * 16 + group * 4, 4), :] = value

        spread_groups(hess_block, 4, gx_count, store_hess)
        spread_groups(load_block, 4, gx_count, store_load)
        return 0

    lax.fori_loop(0, gy_count, unpack, 0)
    shape = (gy_count, width)
    lane, row = lanes(shape), rows_of(shape)
    in_z, in_y, in_x = lax.rem(lane, NEL) // EYD, lax.rem(lane, EYD), lane // NEL
    last_z, first_z = in_z == EZ - 1, in_z == 0
    last_x, first_x = in_x >= gx_count - 1, in_x == 0
    last_y, first_y = in_y == EYD - 1, in_y == 0
    end_y, begin_y = last_y & (row == gy_count - 1), first_y & (row == 0)

    def turn(value, by, axis):
        size = shape[axis]
        by = by % size
        return pltpu.roll(value, by, axis) if by else value

    def corners(main, top):
        found = []
        for a in range(2):
            z_part = main if a == 0 else jnp.where(last_z, top, turn(main, -EYD, 1))
            for b in range(2):
                x_part = z_part if b == 0 else jnp.where(last_x, 0.0, turn(z_part, -NEL, 1))
                for d in range(2):
                    if d == 0:
                        found.append(x_part)
                    else:
                        wrapped = turn(turn(x_part, -1, 0), EYD - 1, 1)
                        moved = jnp.where(last_y, wrapped, turn(x_part, -1, 1))
                        found.append(jnp.where(end_y, 0.0, moved))
        return found

    def settle(parts):
        z_parts = []
        for a in range(2):
            x_parts = []
            for b in range(2):
                base, extra = parts[a * 4 + b * 2], parts[a * 4 + b * 2 + 1]
                wrapped = turn(turn(extra, 1, 0), 1 - EYD, 1)
                moved = jnp.where(first_y, wrapped, turn(extra, 1, 1))
                x_parts.append(base + jnp.where(begin_y, 0.0, moved))
            z_parts.append(x_parts[0] + jnp.where(first_x, 0.0, turn(x_parts[1], NEL, 1)))
        main = z_parts[0] + jnp.where(first_z, 0.0, turn(z_parts[1], EYD, 1))
        return main, jnp.where(last_z, z_parts[1], 0.0)

    def strided(ref, start, stride):
        found = [ref[tile, pl.ds(start, gy_count, stride=stride), :] for tile in range(tiles)]
        return found[0] if tiles == 1 else jnp.concatenate(found, axis=1)

    def channel(p, wz, wx, wy):
        source = (p * 3 + wz) * 3 + wx
        if source < HROWS:
            return strided(coef, wy * HROWS + source, 4 * HROWS)
        spare = wy * 14 + source - HROWS
        if spare < HROWS:
            return strided(coef, 3 * HROWS + spare, 4 * HROWS)
        return strided(rhs, (spare - HROWS) * 4 + 3, 16)

    pair_of = {}
    for p, (c, d) in enumerate(PAIRS):
        pair_of[c, d] = pair_of[d, c] = p
    bits = [(a, b, d) for a in range(2) for b in range(2) for d in range(2)]

    def curved_by(vector):
        known = [corners(main, top) for main, top in vector]
        sums = [[None] * 8 for _ in range(3)]

        def add(c, n, term):
            sums[c][n] = term if sums[c][n] is None else sums[c][n] + term

        for p, (c, d) in enumerate(PAIRS):
            for wz in range(3):
                for wx in range(3):
                    for wy in range(3):
                        factor = channel(p, wz, wx, wy)
                        for n, low in enumerate(bits):
                            for m, high in enumerate(bits):
                                if (low[0] + high[0], low[1] + high[1], low[2] + high[2]) == (wz, wx, wy):
                                    add(c, n, factor * known[d][m])
                                    if c != d:
                                        add(d, n, factor * known[c][m])
        result = []
        for c in range(3):
            main, top = settle(sums[c])
            result.append((main + LAMBDA * vector[c][0], top + LAMBDA * vector[c][1]))
        bent = sum(known[c][n] * sums[c][n] for c in range(3) for n in range(8))
        return result, total(bent) + LAMBDA * inner(vector, vector)

    def total(value):
        return jnp.sum(jnp.sum(value, axis=0, keepdims=True), axis=1, keepdims=True)

    def inner(one, two):
        return total(sum(a[0] * b[0] + a[1] * b[1] for a, b in zip(one, two)))

    def combine(one, factor, two):
        return [(a[0] + factor * b[0], a[1] + factor * b[1]) for a, b in zip(one, two)]

    residual = []
    for c in range(3):
        main, top = None, None
        for bx in range(2):
            inside = strided(rhs, 2 * bx * 4 + c, 16)
            rim = turn(strided(rhs, (2 * bx + 1) * 4 + c, 16), 1, 0)
            spot = c * 2 + bx
            upper = strided(rhs, (2 + spot // 4) * 4 + 3, 16)
            upper = jnp.where(last_z, turn(upper, (EZ - 1 - spot % 4) * EYD, 1), 0.0)
            reached = first_y & (row > 0)
            inside = inside + jnp.where(reached, turn(rim, 1 - EYD, 1), 0.0)
            upper = upper + jnp.where(reached & last_z, turn(rim, 2 - EYD, 1), 0.0)
            if bx:
                main = main + jnp.where(first_x, 0.0, turn(inside, NEL, 1))
                top = top + jnp.where(first_x, 0.0, turn(upper, NEL, 1))
            else:
                main, top = inside, upper
        residual.append((main, top))
    direction = residual
    increment = None
    norm_now = inner(residual, residual)
    for iteration in range(ITERS):
        curved, bent = curved_by(direction)
        step = norm_now / bent
        if increment is None:
            increment = [(step * a, step * b) for a, b in direction]
        else:
            increment = combine(increment, step, direction)
        if iteration + 1 < ITERS:
            residual = combine(residual, -step, curved)
            norm_next = inner(residual, residual)
            direction = combine(residual, norm_next / norm_now, direction)
            norm_now = norm_next
    mine = (row == gy) & (in_x == gx)
    for c in range(3):
        for part, levels in ((increment[c][0], range(EZ)), (increment[c][1], [EZ])):
            line = jnp.sum(jnp.where(mine, part, 0.0), axis=0, keepdims=True)
            short = line[:, 0:128]
            for tile in range(1, tiles):
                short = short + line[:, tile * 128 : (tile + 1) * 128]
            short = pltpu.roll(jnp.broadcast_to(short, (8, 128)), lax.rem(128 - lax.rem(gx, 4) * NEL, 128), 1)
            for level in levels:
                start = min(level, EZ - 1) * EYD
                out[c, level] = short[0:1, start : start + EYD]


def solve(hess, load):
    gx_count, gy_count = lax.axis_size("gx"), lax.axis_size("gy")
    tiles = -(-gx_count // 4)
    vmem = pl.BlockSpec(memory_space=pltpu.VMEM)
    return pl.pallas_call(
        functools.partial(solve_kernel, gx_count, gy_count),
        out_shape=jax.ShapeDtypeStruct((3, EZ + 1, 1, EYD), F32),
        in_specs=[vmem] * 2,
        out_specs=vmem,
        scratch_shapes=[
            pltpu.VMEM((tiles, gy_count * 4 * HROWS, 128), F32),
            pltpu.VMEM((tiles, gy_count * 16, 128), F32),
        ],
        compiler_params=pltpu.CompilerParams(vmem_limit_bytes=LIMIT),
        cost_estimate=takes(3.5),
        name="solve",
    )(hess, load)


def swap(array, axis, partner):
    size = lax.axis_size(axis)
    pairs = [(i, partner(i)) for i in range(size)]
    return lax.ppermute(array, axis, [(i, j) for i, j in pairs if 0 <= j < size])


def swap_x(array, kind):
    if kind == 0:
        return swap(array, "gx", lambda i: i ^ 1)
    return swap(array, "gx", lambda i: i + 1 if i % 2 else i - 1)


def swap_y(array, kind):
    size = lax.axis_size("gy")
    partner = (
        lambda i: i ^ 1,
        lambda i: (i + 1 if i % 2 else i - 1) % size,
        lambda i: i ^ 2,
        lambda i: (i + 2 if i // 2 % 2 else i - 2) % size,
    )[kind]
    return swap(array, "gy", partner)


def gather_steps(gx_count, gy_count):
    far = [("gy", 1 << k) for k in range(1, gy_count.bit_length() - 1)]
    return [*far, ("gy", 1), *[("gx", 1 << k) for k in reversed(range(gx_count.bit_length() - 1))]]


def block_index(steps, relative):
    found = 0
    for k, (axis, bit) in enumerate(steps):
        found = found + jnp.where(jnp.bitwise_and(relative[axis], bit) != 0, 1 << k, 0)
    return found


def swapped(known, step):
    axis, bit = step
    return swap(known, axis, lambda j: j ^ bit)


def doubled(known, step):
    return jnp.concatenate([known, swapped(known, step)], axis=0)


def body(reference_image, deformed_image, route, within, xshift, fractions):
    m0, m1, m2, m3, thick, own, place = ask(
        route.reshape(NEL), within.reshape(NEL), xshift.reshape(NEL), reference_image, deformed_image
    )
    asks = (m0, m1, m2, m3)
    q = {kind: swap_y(asks[kind], kind) for kind in KINDS}
    d1, d0 = swap_x(thick, 1), swap_x(thick, 0)
    grad, packed, extra, portions = moments(reference_image, (d0, d1), (q[0], q[1]), fractions.reshape(NEL, 3))
    q[3], q[0], q[1], q[2], packed = lax.optimization_barrier((q[3], q[0], q[1], q[2], packed))
    *served, at_home = serve(deformed_image, d0, d1, [q[kind] for kind in KINDS] + [own], [8 * (k < 2) + k for k in KINDS] + [4])
    known = packed[None]
    bricks = [swap_y(block, kind) for kind, block in zip(KINDS, served)] + [at_home]
    steps = gather_steps(lax.axis_size("gx"), lax.axis_size("gy"))
    for k, step in enumerate(steps[:-3]):
        if k == 1:
            known, at_home = lax.optimization_barrier((known, at_home))
        known = doubled(known, step)
    bricks[-1] = at_home
    bricks, known = lax.optimization_barrier((bricks, known))
    mismatch, part = warp(place, bricks, reference_image, grad, portions, extra)
    beside, across = swapped(known, steps[-3]), swapped(known, steps[-2])
    beside, across, _ = lax.optimization_barrier((beside, across, part))
    load = lax.all_to_all(part, ("gx", "gy"), 0, 0)
    blocks = [known, beside, across, swapped(beside, steps[-2])]
    blocks = blocks + [swapped(block, steps[-1]) for block in blocks]
    return solve(jnp.concatenate(blocks, axis=0), load), mismatch


def solution(mesh):
    placed = (
        P(None, "gx", "gy"),
        P(None, "gx", "gy"),
        P("gx", "gy", None, None),
        P("gx", "gy", None),
        P("gx", "gy", None),
        P("gx", "gy", None, None),
    )
    return jax.shard_map(
        body,
        mesh=mesh,
        in_specs=placed,
        out_specs=(P(None, None, "gx", "gy"), P(None, "gx", "gy")),
        check_vma=False,
    )
```

```python
import functools

import jax
import jax.numpy as jnp
import numpy as np
from jax import lax
from jax.experimental import pallas as pl
from jax.experimental.pallas import tpu as pltpu
from jax.sharding import PartitionSpec as P

EDGE = 16
EZ = 4
EYD = 8
SPAN = 2
ITERS = 3
NEL = 32
VOL = 4096
NZ = EZ * EDGE
NY = EYD * EDGE
LAMBDA = 0.05

PAIRS = ((0, 0), (0, 1), (0, 2), (1, 1), (1, 2), (2, 2))
HROWS = 40
KINDS = (3, 0, 1, 2)
LIMIT = 32 * 1024 * 1024

F32 = jnp.float32
BF16 = jnp.bfloat16

UPPER = (np.arange(EDGE) + 0.5) / EDGE
HAT = np.stack([1.0 - UPPER, UPPER])
PRODUCTS = np.stack([HAT[0] * HAT[0], HAT[0] * HAT[1], HAT[1] * HAT[1]])


def hat_product(which, position):
    upper = (position.astype(F32) + 0.5) * (1.0 / EDGE)
    lower = 1.0 - upper
    return jnp.where(which == 0, lower * lower, jnp.where(which == 1, lower * upper, upper * upper))


def hat_weight(which, position):
    upper = (position.astype(F32) + 0.5) * (1.0 / EDGE)
    return jnp.where(which == 0, 1.0 - upper, upper)


def along_y(weight, groups):
    shape = (NY, 128)
    row, lane = rows_of(shape), lanes(shape)
    group = lane // NEL
    inside = (row // EDGE == lax.rem(lane, NEL)) & (group >= groups[0]) & (group <= groups[-1])
    return jnp.where(inside, weight(group, lax.rem(row, EDGE)) * (1.0 / VOL), 0.0)


def three_parts(value):
    high = value.astype(BF16)
    rest = value - high.astype(F32)
    middle = rest.astype(BF16)
    return [high, middle, (rest - middle.astype(F32)).astype(BF16)]


def weighed(value, weights):
    high = weights.astype(BF16)
    both = jnp.concatenate([high, (weights - high.astype(F32)).astype(BF16)], axis=1)
    found = jnp.dot(
        jnp.concatenate(three_parts(value), axis=1),
        jnp.concatenate([both] * 3, axis=0),
        preferred_element_type=F32,
    )
    return found[:, :128] + found[:, 128:]


def weighed_once(value, weights):
    weights = weights.astype(BF16)
    return jnp.dot(
        jnp.concatenate(three_parts(value), axis=1),
        jnp.concatenate([weights] * 3, axis=0),
        preferred_element_type=F32,
    )


def layered(found, slab, slabs, weights):
    total = None
    for ez in range(EZ):
        start = (ez * slabs + slab) * EDGE
        part = found[start : start + EDGE] * weights
        part = part[:8] + part[8:]
        part = pltpu.roll(part, ez * EYD, 1) if ez else part
        total = part if total is None else total + part
    return jnp.sum(total, axis=0, keepdims=True)


def lanes(shape):
    return lax.broadcasted_iota(jnp.int32, shape, len(shape) - 1)


def rows_of(shape):
    return lax.broadcasted_iota(jnp.int32, shape, len(shape) - 2)


def even(value):
    return lax.rem(value, 2) == 0


def takes(microseconds):
    return pl.CostEstimate(flops=0, bytes_accessed=int(microseconds * 3.69e6), transcendentals=0)


def ask_kernel(gx_count, route, within, xshift, ref, deformed, m0, m1, m2, m3, thick, own, place):
    gx, gy = lax.axis_index("gx"), lax.axis_index("gy")
    gx_even, gy_even, half_even = even(gx), even(gy), even(gy // 2)
    row, lane = rows_of((8, 128)), lanes((8, 128))
    wide = (8, NEL)
    offset = jnp.broadcast_to(route[...], wide) - SPAN
    moved = jnp.clip(gx + jnp.broadcast_to(xshift[...], wide) - 1, 0, gx_count - 1) - gx
    ahead = jnp.where(gx_even, 1, 2)
    bank = jnp.where(moved == 0, 0, jnp.where(moved == 1, ahead, 3 - ahead))
    code = bank * NEL + lanes(wide) // EYD * EYD + jnp.broadcast_to(within[...], wide)
    plus = jnp.where(gy_even, 0, 1)
    twice = jnp.where(half_even, 2, 3)
    j = jnp.where(offset == 1, plus, jnp.where(offset == -1, 1 - plus, jnp.where(offset == 2, twice, 5 - twice)))
    j = jnp.where(offset == 0, 4, j)
    mine = (rows_of(wide) == j).astype(F32)
    square = (NEL, NEL)
    earlier = (rows_of(square) < lanes(square)).astype(F32).astype(BF16)
    ahead_of = jnp.dot(mine.astype(BF16), earlier, preferred_element_type=F32)
    slot = jnp.sum(mine * ahead_of, axis=0, keepdims=True)
    place[...] = jnp.zeros((8, 128), jnp.int32)
    place[0:1, 0:NEL] = j[0:1] * 8 + slot.astype(jnp.int32)
    tall = (128, NEL)
    taken = (rows_of(tall) == jnp.broadcast_to(slot, tall).astype(jnp.int32)).astype(F32).astype(BF16)
    asked = lax.dot_general(
        (mine * code.astype(F32)).astype(BF16), taken, (((1,), (1,)), ((), ())), preferred_element_type=F32
    )
    own[...] = asked
    m2[...] = asked
    m3[...] = asked
    m0[8:, :] = asked
    m1[8:, :] = asked
    image = ref[...]
    first = jnp.where(gy_even, NY - 1, 0)
    wanted = jnp.where(row == 0, first, jnp.where(row == 1, NY - 1 - first, -1))
    pick = (lane == wanted).astype(F32).astype(BF16)
    columns = lax.dot_general(pick, image.reshape(NZ * EDGE, NY), (((1,), (1,)), ((), ())), preferred_element_type=F32)
    for i in range(8):
        m0[i : i + 1, :] = columns[0:1, i * 128 : (i + 1) * 128]
        m1[i : i + 1, :] = columns[1:2, i * 128 : (i + 1) * 128]
    thick[0:NZ] = deformed[...]
    image = image.astype(F32)
    for k, face in enumerate((image[:, 0, :], image[:, EDGE - 1, :])):
        thick[NZ + k * EZ : NZ + (k + 1) * EZ] = face.astype(BF16).reshape(EZ, EDGE, NY)


def ask(route, within, xshift, ref, deformed):
    smem = pl.BlockSpec(memory_space=pltpu.SMEM)
    vmem = pl.BlockSpec(memory_space=pltpu.VMEM)
    return pl.pallas_call(
        functools.partial(ask_kernel, lax.axis_size("gx")),
        out_shape=(
            jax.ShapeDtypeStruct((16, 128), F32),
            jax.ShapeDtypeStruct((16, 128), F32),
            jax.ShapeDtypeStruct((8, 128), F32),
            jax.ShapeDtypeStruct((8, 128), F32),
            jax.ShapeDtypeStruct((NZ + 2 * EZ, EDGE, NY), BF16),
            jax.ShapeDtypeStruct((8, 128), F32),
            jax.ShapeDtypeStruct((8, 128), jnp.int32),
        ),
        in_specs=[vmem] * 5,
        out_specs=(vmem,) * 7,
        cost_estimate=takes(2.0),
        name="ask",
    )(route, within, xshift, ref, deformed)


def gather_columns(table, slabs, sources, places):
    table[...] = jnp.zeros_like(table)
    shape = (EDGE, NY)
    row, lane = rows_of(shape), lanes(shape)
    for i, (source, place) in enumerate(zip(sources, places)):
        start = pl.multiple_of(i * NY + source * EDGE, EDGE)
        table[pl.ds(start, EDGE), :] = (lane == row + place * EDGE).astype(F32).astype(BF16)
    return jnp.dot(jnp.concatenate(slabs, axis=1), table[...], preferred_element_type=F32)


def serve_kernel(lines, *refs):
    count = len(lines)
    asked, outs = refs[3 : 3 + count], refs[3 + count : 3 + 2 * count]
    banks, tables, codes, scalars, sem = refs[3 + 2 * count :]
    for j in range(count):
        codes[j] = asked[j][lines[j] // 8 * 8 : lines[j] // 8 * 8 + 8].astype(jnp.int32)
    copy = pltpu.make_async_copy(codes, scalars, sem)
    copy.start()
    for i in range(3):
        banks[i] = refs[i][0:NZ]
    copy.wait()
    for j in range(count):
        slabs, columns = [], []
        for slot in range(8):
            code = scalars[j, lines[j] % 8, slot]
            start = jnp.bitwise_and(code, NEL - EYD) * (EDGE // EYD)
            slab = banks[lax.shift_right_logical(code, 5), pl.ds(start, EDGE)]
            slabs.append(slab.reshape(EDGE * EDGE, NY))
            columns.append(jnp.bitwise_and(code, EYD - 1))
        packed = gather_columns(tables.at[j], slabs, columns, range(8))
        outs[j][...] = packed.reshape(EDGE, EDGE, NY).astype(BF16)


def serve(own, d0, d1, asked, lines):
    vmem = pl.BlockSpec(memory_space=pltpu.VMEM)
    count = len(lines)
    return pl.pallas_call(
        functools.partial(serve_kernel, lines),
        out_shape=(jax.ShapeDtypeStruct((EDGE, EDGE, NY), BF16),) * count,
        in_specs=[vmem] * 3 + [vmem] * count,
        out_specs=(vmem,) * count,
        scratch_shapes=[
            pltpu.VMEM((3, NZ, EDGE, NY), BF16),
            pltpu.VMEM((count, 8 * NY, NY), BF16),
            pltpu.VMEM((count, 8, 128), jnp.int32),
            pltpu.SMEM((count, 8, 128), jnp.int32),
            pltpu.SemaphoreType.DMA,
        ],
        compiler_params=pltpu.CompilerParams(vmem_limit_bytes=LIMIT),
        cost_estimate=takes(1.0 + 0.2 * count),
        name="serve",
    )(own, d0, d1, *asked)


def moments_kernel(gy_count, r0, r1, a1, a0, ref, frac, grad, packed, extra, portions, side, slabs):
    gx, gy = lax.axis_index("gx"), lax.axis_index("gy")
    gx_even, gy_even = even(gx), even(gy)
    side[...] = jnp.zeros((8, NZ * EDGE), F32)
    keep0 = jnp.where(gy_even, gy < gy_count - 1, gy > 0).astype(F32)
    keep1 = jnp.where(gy_even, gy > 0, gy < gy_count - 1).astype(F32)
    for i in range(8):
        side[0:1, i * 128 : (i + 1) * 128] = r0[i : i + 1, :] * keep0
        side[1:2, i * 128 : (i + 1) * 128] = r1[i : i + 1, :] * keep1
    row, lane = rows_of((8, 128)), lanes((8, 128))
    target0 = jnp.where(gy_even, NY - 1, 0)
    spot = jnp.where(row == 0, target0, jnp.where(row == 1, NY - 1 - target0, -1))
    spread = (lane == spot).astype(F32).astype(BF16)
    rim = lax.dot_general(
        side[...].astype(BF16), spread, (((0,), (0,)), ((), ())), preferred_element_type=F32
    ).reshape(NZ, EDGE, NY)
    low0, high0, low1, high1 = (
        thick[NZ + k * EZ : NZ + (k + 1) * EZ].astype(F32).reshape(NZ, NY) for thick in (a0, a1) for k in range(2)
    )
    before = jnp.where(gx_even, high1, high0)
    after = jnp.where(gx_even, low0, low1)
    lane2, row2 = lanes((EDGE, NY)), rows_of((EDGE, NY))
    for ez in range(EZ):
        collected = [[jnp.zeros((EDGE, NY), F32) for _ in range(3)] for _ in PAIRS]
        for k in range(EDGE):
            z = ez * EDGE + k
            plane = ref[z].astype(F32)
            below = ref[z - 1].astype(F32) if z > 0 else jnp.zeros((EDGE, NY), F32)
            above = ref[z + 1].astype(F32) if z + 1 < NZ else jnp.zeros((EDGE, NY), F32)
            rim_z = rim[z]
            nxt = jnp.where(row2 == EDGE - 1, after[z : z + 1, :], pltpu.roll(plane, EDGE - 1, 0))
            prv = jnp.where(row2 == 0, before[z : z + 1, :], pltpu.roll(plane, 1, 0))
            right = jnp.where(lane2 == NY - 1, rim_z, pltpu.roll(plane, NY - 1, 1))
            left = jnp.where(lane2 == 0, rim_z, pltpu.roll(plane, 1, 1))
            rounded = [((above - below) * 0.5).astype(BF16), ((nxt - prv) * 0.5).astype(BF16), ((right - left) * 0.5).astype(BF16)]
            for c in range(3):
                grad[c, z] = rounded[c]
            g = [value.astype(F32) for value in rounded]
            for p, (c, d) in enumerate(PAIRS):
                product = g[c] * g[d]
                for w in range(3):
                    collected[p][w] = collected[p][w] + float(PRODUCTS[w, k]) * product
        for p in range(len(PAIRS)):
            for w in range(3):
                start = (ez * 18 + p * 3 + w) * EDGE
                slabs[start : start + EDGE, :] = collected[p][w]
    found = weighed(slabs[...], along_y(hat_product, (0, 1, 2)))
    across = [hat_product(w, row2) for w in range(3)]
    row8, group8 = rows_of((8, 128)), lanes((8, 128)) // NEL
    tiles = [jnp.zeros((8, 128), F32) for _ in range(HROWS // 8 + 1)]
    for slab in range(18):
        for w in range(3):
            line = layered(found, slab, 18, across[w])
            source = slab * 3 + w
            if source < HROWS:
                tiles[source // 8] = jnp.where((row8 == source % 8) & (group8 < 3), line, tiles[source // 8])
            else:
                for wy in range(3):
                    spare = wy * 14 + source - HROWS
                    turned = pltpu.roll(line, (3 - wy) * NEL, 1)
                    tiles[spare // 8] = jnp.where((row8 == spare % 8) & (group8 == 3), turned, tiles[spare // 8])
    total = jnp.concatenate(tiles, axis=0)
    total = pltpu.roll(total, lax.rem(gx, 4) * NEL, 1)
    packed[...] = total[:HROWS]
    line = pltpu.roll(total[HROWS:], NEL, 1)[0:1] + pltpu.roll(total[HROWS:], 2 * NEL, 1)[1:2]
    extra[...] = jnp.where(row == 3, line, 0.0)
    element, lane_e = rows_of((EYD, 128)), lanes((EYD, 128))
    unfold = (lane_e // EDGE == element).astype(F32).astype(BF16)
    for ez in range(EZ):
        tenths = frac[ez * EYD : (ez + 1) * EYD, :].astype(F32).astype(BF16)
        wide = lax.dot_general(tenths, unfold, (((0,), (0,)), ((), ())), preferred_element_type=F32)
        portions[ez, 0:3, :] = wide * (1.0 / EDGE)


def moments(ref, faces_x, faces_y, fractions):
    vmem = pl.BlockSpec(memory_space=pltpu.VMEM)
    return pl.pallas_call(
        functools.partial(moments_kernel, lax.axis_size("gy")),
        out_shape=(
            jax.ShapeDtypeStruct((3, NZ, EDGE, NY), BF16),
            jax.ShapeDtypeStruct((HROWS, 128), F32),
            jax.ShapeDtypeStruct((8, 128), F32),
            jax.ShapeDtypeStruct((EZ, 8, 128), F32),
        ),
        in_specs=[vmem] * 6,
        out_specs=(vmem,) * 4,
        scratch_shapes=[pltpu.VMEM((8, NZ * EDGE), F32), pltpu.VMEM((EZ * 18 * EDGE, NY), F32)],
        compiler_params=pltpu.CompilerParams(vmem_limit_bytes=LIMIT),
        cost_estimate=takes(2.2),
        name="moments",
    )(faces_y[0], faces_y[1], faces_x[1], faces_x[0], ref, fractions)


def warp_kernel(b0, b1, b2, b3, b4, place, ref, grad, portions, extra, mismatch, packed, bricks, tables, slabs, spots, sem):
    gx = lax.axis_index("gx")
    copy = pltpu.make_async_copy(place, spots, sem)
    copy.start()
    for i, source in zip((*KINDS, 4), (b0, b1, b2, b3, b4)):
        bricks[i] = source[...]
    copy.wait()
    flat = (EDGE * EDGE, NY)
    lane = lanes(flat)
    at_x_rim = lax.rem(lax.broadcasted_iota(jnp.int32, flat, 0), EDGE) == EDGE - 1
    at_y_rim = lax.rem(lane, EDGE) == EDGE - 1
    for ez in range(EZ):
        codes = [spots[0, ez * EYD + b] for b in range(EYD)]
        found = [bricks[lax.shift_right_logical(code, 3)].reshape(flat) for code in codes]
        blended = gather_columns(tables.at[ez], found, [jnp.bitwise_and(code, 7) for code in codes], range(EYD))
        portion = portions[ez]
        ty, tx, tz = portion[2:3, :], portion[1:2, :], portion[0:1, :]
        shifted = jnp.where(at_y_rim, blended, pltpu.roll(blended, NY - 1, 1))
        blended = (1.0 - ty) * blended + ty * shifted
        shifted = jnp.where(at_x_rim, blended, pltpu.roll(blended, EDGE * EDGE - 1, 0))
        blended = (1.0 - tx) * blended + tx * shifted
        shifted = jnp.concatenate([blended[EDGE:], blended[-EDGE:]], axis=0)
        blended = (1.0 - tz) * blended + tz * shifted
        blended = blended.reshape(EDGE, EDGE, NY)
        collected = [[jnp.zeros((EDGE, NY), F32) for _ in range(2)] for _ in range(3)]
        for k in range(EDGE):
            z = ez * EDGE + k
            apart = ref[z].astype(F32) - blended[k]
            mismatch[z] = apart
            for c in range(3):
                term = grad[c, z].astype(F32) * apart
                for a in range(2):
                    collected[c][a] = collected[c][a] + float(HAT[a, k]) * term
        for c in range(3):
            for a in range(2):
                start = (ez * 6 + c * 2 + a) * EDGE
                slabs[start : start + EDGE, :] = collected[c][a]
    found = weighed_once(slabs[...], along_y(lambda group, at: hat_weight(lax.rem(group, 2), at), (0, 1, 2, 3)))
    across = hat_weight(lanes((EDGE, 128)) // (2 * NEL), rows_of((EDGE, 128)))
    row, lane = rows_of((8, 128)), lanes((8, 128))
    group, in_z, in_y = lane // NEL, lax.rem(lane, NEL) // EYD, lax.rem(lane, EYD)
    total = jnp.zeros((8, 128), F32)
    for c in range(3):
        lower, upper = (layered(found, c * 2 + a, 6, across) for a in range(2))
        lower, upper = (jnp.broadcast_to(line, (8, 128)) for line in (lower, upper))
        level = lower + jnp.where(in_z > 0, pltpu.roll(upper, EYD, 1), 0.0)
        top = jnp.where(in_z == EZ - 1, upper, 0.0)

        def joined(line):
            return line + jnp.where(in_y > 0, pltpu.roll(line, 128 - NEL + 1, 1), 0.0)

        rim = jnp.where(in_y == EYD - 1, level, 0.0) + jnp.where(in_y == EYD - 2, pltpu.roll(top, 127, 1), 0.0)
        main = jnp.where(lax.rem(group, 2) == 0, joined(level), rim)
        total = jnp.where(row == c, main, total)
        top = joined(top)
        for bx in range(2):
            start = 2 * NEL + (c * 2 + bx) * EYD
            moved = pltpu.roll(top, (start - (bx * 2 * NEL + (EZ - 1) * EYD)) % 128, 1)
            total = jnp.where((row == 3) & (lane // EYD == start // EYD), moved, total)
    total = pltpu.roll(total, lax.rem(gx, 4) * NEL, 1) + extra[...]
    packed[...] = jnp.broadcast_to(total[0:4], packed.shape)


def warp(place, bricks, ref, grad, portions, extra):
    vmem = pl.BlockSpec(memory_space=pltpu.VMEM)
    devices = lax.axis_size("gx") * lax.axis_size("gy")
    return pl.pallas_call(
        warp_kernel,
        out_shape=(jax.ShapeDtypeStruct((NZ, EDGE, NY), F32), jax.ShapeDtypeStruct((devices, 4, 128), F32)),
        in_specs=[vmem] * 10,
        out_specs=(vmem, vmem),
        scratch_shapes=[
            pltpu.VMEM((5, EDGE, EDGE, NY), BF16),
            pltpu.VMEM((EZ, EYD * NY, NY), BF16),
            pltpu.VMEM((EZ * 6 * EDGE, NY), F32),
            pltpu.SMEM((8, 128), jnp.int32),
            pltpu.SemaphoreType.DMA,
        ],
        compiler_params=pltpu.CompilerParams(vmem_limit_bytes=LIMIT),
        cost_estimate=takes(4.0),
        name="warp",
    )(*bricks, place, ref, grad, portions, extra)


def spread_groups(block_of, groups, gx_count, store):
    tiles = -(-gx_count // 4)
    for tile in range(tiles):
        members = range(4 * tile, min(4 * tile + 4, gx_count))
        blocks = {gx: block_of(gx) for gx in members}
        for group in range(groups):
            merged = jnp.zeros_like(blocks[members[0]])
            lane = lanes(merged.shape)
            for gx in members:
                merged = jnp.where(lane // NEL == (group + gx) % 4, blocks[gx], merged)
            store(group, tile, pltpu.roll(merged, (128 - NEL * group) % 128, 1) if group else merged)


def solve_kernel(gx_count, gy_count, hess, load, out, coef, rhs):
    gx, gy = lax.axis_index("gx"), lax.axis_index("gy")
    steps = gather_steps(gx_count, gy_count)
    tiles = -(-gx_count // 4)
    width = 128 * tiles

    def unpack(row, _):
        def hess_block(column):
            relative = dict(gx=jnp.bitwise_xor(gx, column), gy=jnp.bitwise_xor(gy, row))
            return hess[block_index(steps, relative)]

        def store_hess(group, tile, value):
            coef[tile, pl.ds(group * HROWS * gy_count + row, HROWS, stride=gy_count), :] = value

        def load_block(column):
            return load[column * gy_count + row]

        def store_load(group, tile, value):
            rhs[tile, pl.ds(row * 16 + group * 4, 4), :] = value

        spread_groups(hess_block, 4, gx_count, store_hess)
        spread_groups(load_block, 4, gx_count, store_load)
        return 0

    lax.fori_loop(0, gy_count, unpack, 0, unroll=8)
    shape = (gy_count, width)
    lane, row = lanes(shape), rows_of(shape)
    in_z, in_y, in_x = lax.rem(lane, NEL) // EYD, lax.rem(lane, EYD), lane // NEL
    last_z, first_z = in_z == EZ - 1, in_z == 0
    last_x, first_x = in_x >= gx_count - 1, in_x == 0
    last_y, first_y = in_y == EYD - 1, in_y == 0
    end_y, begin_y = last_y & (row == gy_count - 1), first_y & (row == 0)

    def turn(value, by, axis):
        size = shape[axis]
        by = by % size
        return pltpu.roll(value, by, axis) if by else value

    def corners(main, top):
        found = []
        for a in range(2):
            z_part = main if a == 0 else jnp.where(last_z, top, turn(main, -EYD, 1))
            for b in range(2):
                x_part = z_part if b == 0 else jnp.where(last_x, 0.0, turn(z_part, -NEL, 1))
                for d in range(2):
                    if d == 0:
                        found.append(x_part)
                    else:
                        wrapped = turn(turn(x_part, -1, 0), EYD - 1, 1)
                        moved = jnp.where(last_y, wrapped, turn(x_part, -1, 1))
                        found.append(jnp.where(end_y, 0.0, moved))
        return found

    def settle(parts):
        z_parts = []
        for a in range(2):
            x_parts = []
            for b in range(2):
                base, extra = parts[a * 4 + b * 2], parts[a * 4 + b * 2 + 1]
                wrapped = turn(turn(extra, 1, 0), 1 - EYD, 1)
                moved = jnp.where(first_y, wrapped, turn(extra, 1, 1))
                x_parts.append(base + jnp.where(begin_y, 0.0, moved))
            z_parts.append(x_parts[0] + jnp.where(first_x, 0.0, turn(x_parts[1], NEL, 1)))
        main = z_parts[0] + jnp.where(first_z, 0.0, turn(z_parts[1], EYD, 1))
        return main, jnp.where(last_z, z_parts[1], 0.0)

    def strided(ref, start, stride):
        found = [ref[tile, pl.ds(start, gy_count, stride=stride), :] for tile in range(tiles)]
        return found[0] if tiles == 1 else jnp.concatenate(found, axis=1)

    def held(ref, index):
        found = [ref[tile, index * gy_count : (index + 1) * gy_count, :] for tile in range(tiles)]
        return found[0] if tiles == 1 else jnp.concatenate(found, axis=1)

    def channel(p, wz, wx, wy):
        source = (p * 3 + wz) * 3 + wx
        if source < HROWS:
            return held(coef, wy * HROWS + source)
        spare = wy * 14 + source - HROWS
        if spare < HROWS:
            return held(coef, 3 * HROWS + spare)
        return strided(rhs, (spare - HROWS) * 4 + 3, 16)

    pair_of = {}
    for p, (c, d) in enumerate(PAIRS):
        pair_of[c, d] = pair_of[d, c] = p
    bits = [(a, b, d) for a in range(2) for b in range(2) for d in range(2)]

    def curved_by(vector):
        known = [corners(main, top) for main, top in vector]
        sums = [[None] * 8 for _ in range(3)]

        def add(c, n, term):
            sums[c][n] = term if sums[c][n] is None else sums[c][n] + term

        for p, (c, d) in enumerate(PAIRS):
            for wz in range(3):
                for wx in range(3):
                    for wy in range(3):
                        factor = channel(p, wz, wx, wy)
                        for n, low in enumerate(bits):
                            for m, high in enumerate(bits):
                                if (low[0] + high[0], low[1] + high[1], low[2] + high[2]) == (wz, wx, wy):
                                    add(c, n, factor * known[d][m])
                                    if c != d:
                                        add(d, n, factor * known[c][m])
        result = []
        for c in range(3):
            main, top = settle(sums[c])
            result.append((main + LAMBDA * vector[c][0], top + LAMBDA * vector[c][1]))
        bent = sum(known[c][n] * sums[c][n] for c in range(3) for n in range(8))
        return result, total(bent) + LAMBDA * inner(vector, vector)

    def total(value):
        return jnp.sum(jnp.sum(value, axis=0, keepdims=True), axis=1, keepdims=True)

    def inner(one, two):
        return total(sum(a[0] * b[0] + a[1] * b[1] for a, b in zip(one, two)))

    def combine(one, factor, two):
        return [(a[0] + factor * b[0], a[1] + factor * b[1]) for a, b in zip(one, two)]

    residual = []
    for c in range(3):
        main, top = None, None
        for bx in range(2):
            inside = strided(rhs, 2 * bx * 4 + c, 16)
            rim = turn(strided(rhs, (2 * bx + 1) * 4 + c, 16), 1, 0)
            spot = c * 2 + bx
            upper = strided(rhs, (2 + spot // 4) * 4 + 3, 16)
            upper = jnp.where(last_z, turn(upper, (EZ - 1 - spot % 4) * EYD, 1), 0.0)
            reached = first_y & (row > 0)
            inside = inside + jnp.where(reached, turn(rim, 1 - EYD, 1), 0.0)
            upper = upper + jnp.where(reached & last_z, turn(rim, 2 - EYD, 1), 0.0)
            if bx:
                main = main + jnp.where(first_x, 0.0, turn(inside, NEL, 1))
                top = top + jnp.where(first_x, 0.0, turn(upper, NEL, 1))
            else:
                main, top = inside, upper
        residual.append((main, top))
    direction = residual
    increment = None
    norm_now = inner(residual, residual)
    for iteration in range(ITERS):
        curved, bent = curved_by(direction)
        step = norm_now / bent
        if increment is None:
            increment = [(step * a, step * b) for a, b in direction]
        else:
            increment = combine(increment, step, direction)
        if iteration + 1 < ITERS:
            residual = combine(residual, -step, curved)
            norm_next = inner(residual, residual)
            direction = combine(residual, norm_next / norm_now, direction)
            norm_now = norm_next
    mine = (row == gy) & (in_x == gx)
    for c in range(3):
        for part, levels in ((increment[c][0], range(EZ)), (increment[c][1], [EZ])):
            line = jnp.sum(jnp.where(mine, part, 0.0), axis=0, keepdims=True)
            short = line[:, 0:128]
            for tile in range(1, tiles):
                short = short + line[:, tile * 128 : (tile + 1) * 128]
            short = pltpu.roll(jnp.broadcast_to(short, (8, 128)), lax.rem(128 - lax.rem(gx, 4) * NEL, 128), 1)
            for level in levels:
                start = min(level, EZ - 1) * EYD
                out[c, level] = short[0:1, start : start + EYD]


def solve(hess, load):
    gx_count, gy_count = lax.axis_size("gx"), lax.axis_size("gy")
    tiles = -(-gx_count // 4)
    vmem = pl.BlockSpec(memory_space=pltpu.VMEM)
    return pl.pallas_call(
        functools.partial(solve_kernel, gx_count, gy_count),
        out_shape=jax.ShapeDtypeStruct((3, EZ + 1, 1, EYD), F32),
        in_specs=[vmem] * 2,
        out_specs=vmem,
        scratch_shapes=[
            pltpu.VMEM((tiles, gy_count * 4 * HROWS, 128), F32),
            pltpu.VMEM((tiles, gy_count * 16, 128), F32),
        ],
        compiler_params=pltpu.CompilerParams(vmem_limit_bytes=LIMIT),
        cost_estimate=takes(3.5),
        name="solve",
    )(hess, load)


def swap(array, axis, partner):
    size = lax.axis_size(axis)
    pairs = [(i, partner(i)) for i in range(size)]
    return lax.ppermute(array, axis, [(i, j) for i, j in pairs if 0 <= j < size])


def swap_x(array, kind):
    if kind == 0:
        return swap(array, "gx", lambda i: i ^ 1)
    return swap(array, "gx", lambda i: i + 1 if i % 2 else i - 1)


def swap_y(array, kind):
    size = lax.axis_size("gy")
    partner = (
        lambda i: i ^ 1,
        lambda i: (i + 1 if i % 2 else i - 1) % size,
        lambda i: i ^ 2,
        lambda i: (i + 2 if i // 2 % 2 else i - 2) % size,
    )[kind]
    return swap(array, "gy", partner)


def gather_steps(gx_count, gy_count):
    far = [("gy", 1 << k) for k in range(1, gy_count.bit_length() - 1)]
    return [*far, ("gy", 1), *[("gx", 1 << k) for k in reversed(range(gx_count.bit_length() - 1))]]


def block_index(steps, relative):
    found = 0
    for k, (axis, bit) in enumerate(steps):
        found = found + jnp.where(jnp.bitwise_and(relative[axis], bit) != 0, 1 << k, 0)
    return found


def swapped(known, step):
    axis, bit = step
    return swap(known, axis, lambda j: j ^ bit)


def doubled(known, step):
    return jnp.concatenate([known, swapped(known, step)], axis=0)


def body(reference_image, deformed_image, route, within, xshift, fractions):
    m0, m1, m2, m3, thick, own, place = ask(
        route.reshape(1, NEL), within.reshape(1, NEL), xshift.reshape(1, NEL), reference_image, deformed_image
    )
    asks = (m0, m1, m2, m3)
    q = {kind: swap_y(asks[kind], kind) for kind in KINDS}
    d1, d0 = swap_x(thick, 1), swap_x(thick, 0)
    grad, packed, extra, portions = moments(reference_image, (d0, d1), (q[0], q[1]), fractions.reshape(NEL, 3))
    q[3], q[0], q[1], q[2], packed = lax.optimization_barrier((q[3], q[0], q[1], q[2], packed))
    *served, at_home = serve(deformed_image, d0, d1, [q[kind] for kind in KINDS] + [own], [8 * (k < 2) + k for k in KINDS] + [4])
    known = packed[None]
    bricks = [swap_y(block, kind) for kind, block in zip(KINDS, served)] + [at_home]
    steps = gather_steps(lax.axis_size("gx"), lax.axis_size("gy"))
    for k, step in enumerate(steps[:-3]):
        if k == 1:
            known, at_home = lax.optimization_barrier((known, at_home))
        known = doubled(known, step)
    bricks[-1] = at_home
    bricks, known = lax.optimization_barrier((bricks, known))
    mismatch, part = warp(place, bricks, reference_image, grad, portions, extra)
    beside, across = swapped(known, steps[-3]), swapped(known, steps[-2])
    known, beside, across, _ = lax.optimization_barrier((known, beside, across, part))
    load = lax.all_to_all(part, ("gx", "gy"), 0, 0)
    blocks = [known, beside, across, swapped(beside, steps[-2])]
    blocks = blocks + [swapped(block, steps[-1]) for block in blocks]
    return solve(jnp.concatenate(blocks, axis=0), load), mismatch


def solution(mesh):
    placed = (
        P(None, "gx", "gy"),
        P(None, "gx", "gy"),
        P("gx", "gy", None, None),
        P("gx", "gy", None),
        P("gx", "gy", None),
        P("gx", "gy", None, None),
    )
    return jax.shard_map(
        body,
        mesh=mesh,
        in_specs=placed,
        out_specs=(P(None, None, "gx", "gy"), P(None, "gx", "gy")),
        check_vma=False,
    )
```

```python
import functools

import jax
import jax.numpy as jnp
import numpy as np
from jax import lax
from jax.experimental import pallas as pl
from jax.experimental.pallas import tpu as pltpu
from jax.sharding import PartitionSpec as P

EDGE = 16
EZ = 4
EYD = 8
SPAN = 2
ITERS = 3
NEL = 32
VOL = 4096
NZ = EZ * EDGE
NY = EYD * EDGE
LAMBDA = 0.05

PAIRS = ((0, 0), (0, 1), (0, 2), (1, 1), (1, 2), (2, 2))
HROWS = 40
KINDS = (3, 0, 1, 2)
LIMIT = 32 * 1024 * 1024

F32 = jnp.float32
BF16 = jnp.bfloat16

UPPER = (np.arange(EDGE) + 0.5) / EDGE
HAT = np.stack([1.0 - UPPER, UPPER])
PRODUCTS = np.stack([HAT[0] * HAT[0], HAT[0] * HAT[1], HAT[1] * HAT[1]])


def hat_product(which, position):
    upper = (position.astype(F32) + 0.5) * (1.0 / EDGE)
    lower = 1.0 - upper
    return jnp.where(which == 0, lower * lower, jnp.where(which == 1, lower * upper, upper * upper))


def hat_weight(which, position):
    upper = (position.astype(F32) + 0.5) * (1.0 / EDGE)
    return jnp.where(which == 0, 1.0 - upper, upper)


def along_y(weight, groups):
    shape = (NY, 128)
    row, lane = rows_of(shape), lanes(shape)
    group = lane // NEL
    inside = (row // EDGE == lax.rem(lane, NEL)) & (group >= groups[0]) & (group <= groups[-1])
    return jnp.where(inside, weight(group, lax.rem(row, EDGE)) * (1.0 / VOL), 0.0)


def three_parts(value):
    high = value.astype(BF16)
    rest = value - high.astype(F32)
    middle = rest.astype(BF16)
    return [high, middle, (rest - middle.astype(F32)).astype(BF16)]


def weighed(value, weights):
    high = weights.astype(BF16)
    both = jnp.concatenate([high, (weights - high.astype(F32)).astype(BF16)], axis=1)
    found = jnp.dot(
        jnp.concatenate(three_parts(value), axis=1),
        jnp.concatenate([both] * 3, axis=0),
        preferred_element_type=F32,
    )
    return found[:, :128] + found[:, 128:]


def weighed_once(value, weights):
    weights = weights.astype(BF16)
    return jnp.dot(
        jnp.concatenate(three_parts(value), axis=1),
        jnp.concatenate([weights] * 3, axis=0),
        preferred_element_type=F32,
    )


def layered(found, slab, slabs, weights):
    total = None
    for ez in range(EZ):
        start = (ez * slabs + slab) * EDGE
        part = found[start : start + EDGE] * weights
        part = part[:8] + part[8:]
        part = pltpu.roll(part, ez * EYD, 1) if ez else part
        total = part if total is None else total + part
    return jnp.sum(total, axis=0, keepdims=True)


def lanes(shape):
    return lax.broadcasted_iota(jnp.int32, shape, len(shape) - 1)


def rows_of(shape):
    return lax.broadcasted_iota(jnp.int32, shape, len(shape) - 2)


def even(value):
    return lax.rem(value, 2) == 0


def takes(microseconds):
    return pl.CostEstimate(flops=0, bytes_accessed=int(microseconds * 3.69e6), transcendentals=0)


def ask_kernel(gx_count, route, within, xshift, ref, deformed, m0, m1, m2, m3, thick, own, place):
    gx, gy = lax.axis_index("gx"), lax.axis_index("gy")
    gx_even, gy_even, half_even = even(gx), even(gy), even(gy // 2)
    row, lane = rows_of((8, 128)), lanes((8, 128))
    wide = (8, NEL)
    offset = jnp.broadcast_to(route[...], wide) - SPAN
    moved = jnp.clip(gx + jnp.broadcast_to(xshift[...], wide) - 1, 0, gx_count - 1) - gx
    ahead = jnp.where(gx_even, 1, 2)
    bank = jnp.where(moved == 0, 0, jnp.where(moved == 1, ahead, 3 - ahead))
    code = bank * NEL + lanes(wide) // EYD * EYD + jnp.broadcast_to(within[...], wide)
    plus = jnp.where(gy_even, 0, 1)
    twice = jnp.where(half_even, 2, 3)
    j = jnp.where(offset == 1, plus, jnp.where(offset == -1, 1 - plus, jnp.where(offset == 2, twice, 5 - twice)))
    j = jnp.where(offset == 0, 4, j)
    mine = (rows_of(wide) == j).astype(F32)
    square = (NEL, NEL)
    earlier = (rows_of(square) < lanes(square)).astype(F32).astype(BF16)
    ahead_of = jnp.dot(mine.astype(BF16), earlier, preferred_element_type=F32)
    slot = jnp.sum(mine * ahead_of, axis=0, keepdims=True)
    order = jnp.full(wide, 4, jnp.int32)
    for at, kind in enumerate(KINDS):
        order = jnp.where(j == kind, at, order)
    found = jnp.where(rows_of(wide) == lanes(wide) // EYD, order.astype(F32) * 8.0 + slot, 0.0)
    long = (NEL, 128)
    widen = (lax.rem(rows_of(long), EYD) == lanes(long) // EDGE).astype(F32).astype(BF16)
    found = jnp.dot(found.astype(BF16), widen, preferred_element_type=F32)
    place[...] = found.astype(jnp.int32) * EDGE + lax.rem(lane, EDGE)
    tall = (128, NEL)
    taken = (rows_of(tall) == jnp.broadcast_to(slot, tall).astype(jnp.int32)).astype(F32).astype(BF16)
    asked = lax.dot_general(
        (mine * code.astype(F32)).astype(BF16), taken, (((1,), (1,)), ((), ())), preferred_element_type=F32
    )
    own[...] = asked
    m2[...] = asked
    m3[...] = asked
    m0[8:, :] = asked
    m1[8:, :] = asked
    image = ref[...]
    first = jnp.where(gy_even, NY - 1, 0)
    wanted = jnp.where(row == 0, first, jnp.where(row == 1, NY - 1 - first, -1))
    pick = (lane == wanted).astype(F32).astype(BF16)
    columns = lax.dot_general(pick, image.reshape(NZ * EDGE, NY), (((1,), (1,)), ((), ())), preferred_element_type=F32)
    for i in range(8):
        m0[i : i + 1, :] = columns[0:1, i * 128 : (i + 1) * 128]
        m1[i : i + 1, :] = columns[1:2, i * 128 : (i + 1) * 128]
    thick[0:NZ] = deformed[...]
    image = image.astype(F32)
    for k, face in enumerate((image[:, 0, :], image[:, EDGE - 1, :])):
        thick[NZ + k * EZ : NZ + (k + 1) * EZ] = face.astype(BF16).reshape(EZ, EDGE, NY)


def ask(route, within, xshift, ref, deformed):
    smem = pl.BlockSpec(memory_space=pltpu.SMEM)
    vmem = pl.BlockSpec(memory_space=pltpu.VMEM)
    return pl.pallas_call(
        functools.partial(ask_kernel, lax.axis_size("gx")),
        out_shape=(
            jax.ShapeDtypeStruct((16, 128), F32),
            jax.ShapeDtypeStruct((16, 128), F32),
            jax.ShapeDtypeStruct((8, 128), F32),
            jax.ShapeDtypeStruct((8, 128), F32),
            jax.ShapeDtypeStruct((NZ + 2 * EZ, EDGE, NY), BF16),
            jax.ShapeDtypeStruct((8, 128), F32),
            jax.ShapeDtypeStruct((8, 128), jnp.int32),
        ),
        in_specs=[vmem] * 5,
        out_specs=(vmem,) * 7,
        cost_estimate=takes(2.0),
        name="ask",
    )(route, within, xshift, ref, deformed)


def gather_columns(table, slabs, sources, places):
    table[...] = jnp.zeros_like(table)
    shape = (EDGE, NY)
    row, lane = rows_of(shape), lanes(shape)
    for i, (source, place) in enumerate(zip(sources, places)):
        start = pl.multiple_of(i * NY + source * EDGE, EDGE)
        table[pl.ds(start, EDGE), :] = (lane == row + place * EDGE).astype(F32).astype(BF16)
    return jnp.dot(jnp.concatenate(slabs, axis=1), table[...], preferred_element_type=F32)


def serve_kernel(lines, *refs):
    count = len(lines)
    asked, outs = refs[3 : 3 + count], refs[3 + count : 3 + 2 * count]
    banks, tables, codes, scalars, sem = refs[3 + 2 * count :]
    for j in range(count):
        codes[j] = asked[j][lines[j] // 8 * 8 : lines[j] // 8 * 8 + 8].astype(jnp.int32)
    copy = pltpu.make_async_copy(codes, scalars, sem)
    copy.start()
    for i in range(3):
        banks[i] = refs[i][0:NZ]
    copy.wait()
    for j in range(count):
        slabs, columns = [], []
        for slot in range(8):
            code = scalars[j, lines[j] % 8, slot]
            start = jnp.bitwise_and(code, NEL - EYD) * (EDGE // EYD)
            slab = banks[lax.shift_right_logical(code, 5), pl.ds(start, EDGE)]
            slabs.append(slab.reshape(EDGE * EDGE, NY))
            columns.append(jnp.bitwise_and(code, EYD - 1))
        packed = gather_columns(tables.at[j], slabs, columns, range(8))
        outs[j][...] = packed.reshape(EDGE, EDGE, NY).astype(BF16)


def serve(own, d0, d1, asked, lines):
    vmem = pl.BlockSpec(memory_space=pltpu.VMEM)
    count = len(lines)
    return pl.pallas_call(
        functools.partial(serve_kernel, lines),
        out_shape=(jax.ShapeDtypeStruct((EDGE, EDGE, NY), BF16),) * count,
        in_specs=[vmem] * 3 + [vmem] * count,
        out_specs=(vmem,) * count,
        scratch_shapes=[
            pltpu.VMEM((3, NZ, EDGE, NY), BF16),
            pltpu.VMEM((count, 8 * NY, NY), BF16),
            pltpu.VMEM((count, 8, 128), jnp.int32),
            pltpu.SMEM((count, 8, 128), jnp.int32),
            pltpu.SemaphoreType.DMA,
        ],
        compiler_params=pltpu.CompilerParams(vmem_limit_bytes=LIMIT),
        cost_estimate=takes(1.0 + 0.2 * count),
        name="serve",
    )(own, d0, d1, *asked)


def moments_kernel(gy_count, r0, r1, a1, a0, ref, frac, grad, packed, extra, portions, side, slabs):
    gx, gy = lax.axis_index("gx"), lax.axis_index("gy")
    gx_even, gy_even = even(gx), even(gy)
    side[...] = jnp.zeros((8, NZ * EDGE), F32)
    keep0 = jnp.where(gy_even, gy < gy_count - 1, gy > 0).astype(F32)
    keep1 = jnp.where(gy_even, gy > 0, gy < gy_count - 1).astype(F32)
    for i in range(8):
        side[0:1, i * 128 : (i + 1) * 128] = r0[i : i + 1, :] * keep0
        side[1:2, i * 128 : (i + 1) * 128] = r1[i : i + 1, :] * keep1
    row, lane = rows_of((8, 128)), lanes((8, 128))
    target0 = jnp.where(gy_even, NY - 1, 0)
    spot = jnp.where(row == 0, target0, jnp.where(row == 1, NY - 1 - target0, -1))
    spread = (lane == spot).astype(F32).astype(BF16)
    rim = lax.dot_general(
        side[...].astype(BF16), spread, (((0,), (0,)), ((), ())), preferred_element_type=F32
    ).reshape(NZ, EDGE, NY)
    low0, high0, low1, high1 = (
        thick[NZ + k * EZ : NZ + (k + 1) * EZ].astype(F32).reshape(NZ, NY) for thick in (a0, a1) for k in range(2)
    )
    before = jnp.where(gx_even, high1, high0)
    after = jnp.where(gx_even, low0, low1)
    lane2, row2 = lanes((EDGE, NY)), rows_of((EDGE, NY))
    for ez in range(EZ):
        collected = [[jnp.zeros((EDGE, NY), F32) for _ in range(3)] for _ in PAIRS]
        for k in range(EDGE):
            z = ez * EDGE + k
            plane = ref[z].astype(F32)
            below = ref[z - 1].astype(F32) if z > 0 else jnp.zeros((EDGE, NY), F32)
            above = ref[z + 1].astype(F32) if z + 1 < NZ else jnp.zeros((EDGE, NY), F32)
            rim_z = rim[z]
            nxt = jnp.where(row2 == EDGE - 1, after[z : z + 1, :], pltpu.roll(plane, EDGE - 1, 0))
            prv = jnp.where(row2 == 0, before[z : z + 1, :], pltpu.roll(plane, 1, 0))
            right = jnp.where(lane2 == NY - 1, rim_z, pltpu.roll(plane, NY - 1, 1))
            left = jnp.where(lane2 == 0, rim_z, pltpu.roll(plane, 1, 1))
            rounded = [((above - below) * 0.5).astype(BF16), ((nxt - prv) * 0.5).astype(BF16), ((right - left) * 0.5).astype(BF16)]
            for c in range(3):
                grad[c, z] = rounded[c]
            g = [value.astype(F32) for value in rounded]
            for p, (c, d) in enumerate(PAIRS):
                product = g[c] * g[d]
                for w in range(3):
                    collected[p][w] = collected[p][w] + float(PRODUCTS[w, k]) * product
        for p in range(len(PAIRS)):
            for w in range(3):
                start = (ez * 18 + p * 3 + w) * EDGE
                slabs[start : start + EDGE, :] = collected[p][w]
    found = weighed(slabs[...], along_y(hat_product, (0, 1, 2)))
    across = [hat_product(w, row2) for w in range(3)]
    row8, group8 = rows_of((8, 128)), lanes((8, 128)) // NEL
    tiles = [jnp.zeros((8, 128), F32) for _ in range(HROWS // 8 + 1)]
    for slab in range(18):
        for w in range(3):
            line = layered(found, slab, 18, across[w])
            source = slab * 3 + w
            if source < HROWS:
                tiles[source // 8] = jnp.where((row8 == source % 8) & (group8 < 3), line, tiles[source // 8])
            else:
                for wy in range(3):
                    spare = wy * 14 + source - HROWS
                    turned = pltpu.roll(line, (3 - wy) * NEL, 1)
                    tiles[spare // 8] = jnp.where((row8 == spare % 8) & (group8 == 3), turned, tiles[spare // 8])
    total = jnp.concatenate(tiles, axis=0)
    total = pltpu.roll(total, lax.rem(gx, 4) * NEL, 1)
    packed[...] = total[:HROWS]
    line = pltpu.roll(total[HROWS:], NEL, 1)[0:1] + pltpu.roll(total[HROWS:], 2 * NEL, 1)[1:2]
    extra[...] = jnp.where(row == 3, line, 0.0)
    element, lane_e = rows_of((EYD, 128)), lanes((EYD, 128))
    unfold = (lane_e // EDGE == element).astype(F32).astype(BF16)
    for ez in range(EZ):
        tenths = frac[ez * EYD : (ez + 1) * EYD, :].astype(F32).astype(BF16)
        wide = lax.dot_general(tenths, unfold, (((0,), (0,)), ((), ())), preferred_element_type=F32)
        portions[ez, 0:3, :] = wide * (1.0 / EDGE)


def moments(ref, faces_x, faces_y, fractions):
    vmem = pl.BlockSpec(memory_space=pltpu.VMEM)
    return pl.pallas_call(
        functools.partial(moments_kernel, lax.axis_size("gy")),
        out_shape=(
            jax.ShapeDtypeStruct((3, NZ, EDGE, NY), BF16),
            jax.ShapeDtypeStruct((HROWS, 128), F32),
            jax.ShapeDtypeStruct((8, 128), F32),
            jax.ShapeDtypeStruct((EZ, 8, 128), F32),
        ),
        in_specs=[vmem] * 6,
        out_specs=(vmem,) * 4,
        scratch_shapes=[pltpu.VMEM((8, NZ * EDGE), F32), pltpu.VMEM((EZ * 18 * EDGE, NY), F32)],
        compiler_params=pltpu.CompilerParams(vmem_limit_bytes=LIMIT),
        cost_estimate=takes(2.2),
        name="moments",
    )(faces_y[0], faces_y[1], faces_x[1], faces_x[0], ref, fractions)


def warp_kernel(b0, b1, b2, b3, b4, place, ref, grad, portions, extra, mismatch, packed, slabs):
    gx = lax.axis_index("gx")
    flat = (EDGE * EDGE, NY)
    lane = lanes(flat)
    at_x_rim = lax.rem(lax.broadcasted_iota(jnp.int32, flat, 0), EDGE) == EDGE - 1
    at_y_rim = lax.rem(lane, EDGE) == EDGE - 1
    came = jnp.concatenate([block[...].reshape(flat) for block in (b0, b1, b2, b3, b4)], axis=1)
    table = (5 * NY, NY)
    fetched = []
    for half in range(2):
        spots = [jnp.broadcast_to(place[ez : ez + 1, :], table) for ez in (2 * half, 2 * half + 1)]
        moves = [(rows_of(table) == spot).astype(F32).astype(BF16) for spot in spots]
        fetched.append(jnp.dot(came, jnp.concatenate(moves, axis=1), preferred_element_type=F32))
    for ez in range(EZ):
        blended = fetched[ez // 2][:, ez % 2 * NY : (ez % 2 + 1) * NY]
        portion = portions[ez]
        ty, tx, tz = portion[2:3, :], portion[1:2, :], portion[0:1, :]
        shifted = jnp.where(at_y_rim, blended, pltpu.roll(blended, NY - 1, 1))
        blended = (1.0 - ty) * blended + ty * shifted
        shifted = jnp.where(at_x_rim, blended, pltpu.roll(blended, EDGE * EDGE - 1, 0))
        blended = (1.0 - tx) * blended + tx * shifted
        shifted = jnp.concatenate([blended[EDGE:], blended[-EDGE:]], axis=0)
        blended = (1.0 - tz) * blended + tz * shifted
        blended = blended.reshape(EDGE, EDGE, NY)
        collected = [[jnp.zeros((EDGE, NY), F32) for _ in range(2)] for _ in range(3)]
        for k in range(EDGE):
            z = ez * EDGE + k
            apart = ref[z].astype(F32) - blended[k]
            mismatch[z] = apart
            for c in range(3):
                term = grad[c, z].astype(F32) * apart
                for a in range(2):
                    collected[c][a] = collected[c][a] + float(HAT[a, k]) * term
        for c in range(3):
            for a in range(2):
                start = (ez * 6 + c * 2 + a) * EDGE
                slabs[start : start + EDGE, :] = collected[c][a]
    found = weighed_once(slabs[...], along_y(lambda group, at: hat_weight(lax.rem(group, 2), at), (0, 1, 2, 3)))
    across = hat_weight(lanes((EDGE, 128)) // (2 * NEL), rows_of((EDGE, 128)))
    row, lane = rows_of((8, 128)), lanes((8, 128))
    group, in_z, in_y = lane // NEL, lax.rem(lane, NEL) // EYD, lax.rem(lane, EYD)
    total = jnp.zeros((8, 128), F32)
    for c in range(3):
        lower, upper = (layered(found, c * 2 + a, 6, across) for a in range(2))
        lower, upper = (jnp.broadcast_to(line, (8, 128)) for line in (lower, upper))
        level = lower + jnp.where(in_z > 0, pltpu.roll(upper, EYD, 1), 0.0)
        top = jnp.where(in_z == EZ - 1, upper, 0.0)

        def joined(line):
            return line + jnp.where(in_y > 0, pltpu.roll(line, 128 - NEL + 1, 1), 0.0)

        rim = jnp.where(in_y == EYD - 1, level, 0.0) + jnp.where(in_y == EYD - 2, pltpu.roll(top, 127, 1), 0.0)
        main = jnp.where(lax.rem(group, 2) == 0, joined(level), rim)
        total = jnp.where(row == c, main, total)
        top = joined(top)
        for bx in range(2):
            start = 2 * NEL + (c * 2 + bx) * EYD
            moved = pltpu.roll(top, (start - (bx * 2 * NEL + (EZ - 1) * EYD)) % 128, 1)
            total = jnp.where((row == 3) & (lane // EYD == start // EYD), moved, total)
    total = pltpu.roll(total, lax.rem(gx, 4) * NEL, 1) + extra[...]
    packed[...] = jnp.broadcast_to(total[0:4], packed.shape)


def warp(place, bricks, ref, grad, portions, extra):
    vmem = pl.BlockSpec(memory_space=pltpu.VMEM)
    devices = lax.axis_size("gx") * lax.axis_size("gy")
    return pl.pallas_call(
        warp_kernel,
        out_shape=(jax.ShapeDtypeStruct((NZ, EDGE, NY), F32), jax.ShapeDtypeStruct((devices, 4, 128), F32)),
        in_specs=[vmem] * 10,
        out_specs=(vmem, vmem),
        scratch_shapes=[
            pltpu.VMEM((EZ * 6 * EDGE, NY), F32),
        ],
        compiler_params=pltpu.CompilerParams(vmem_limit_bytes=LIMIT),
        cost_estimate=takes(4.0),
        name="warp",
    )(*bricks, place, ref, grad, portions, extra)


def spread_groups(block_of, groups, gx_count, store):
    tiles = -(-gx_count // 4)
    for tile in range(tiles):
        members = range(4 * tile, min(4 * tile + 4, gx_count))
        blocks = {gx: block_of(gx) for gx in members}
        for group in range(groups):
            merged = jnp.zeros_like(blocks[members[0]])
            lane = lanes(merged.shape)
            for gx in members:
                merged = jnp.where(lane // NEL == (group + gx) % 4, blocks[gx], merged)
            store(group, tile, pltpu.roll(merged, (128 - NEL * group) % 128, 1) if group else merged)


def solve_kernel(gx_count, gy_count, hess, load, out, coef, rhs):
    gx, gy = lax.axis_index("gx"), lax.axis_index("gy")
    steps = gather_steps(gx_count, gy_count)
    tiles = -(-gx_count // 4)
    width = 128 * tiles

    def unpack(row, _):
        def hess_block(column):
            relative = dict(gx=jnp.bitwise_xor(gx, column), gy=jnp.bitwise_xor(gy, row))
            return hess[block_index(steps, relative)]

        def store_hess(group, tile, value):
            coef[tile, pl.ds(group * HROWS * gy_count + row, HROWS, stride=gy_count), :] = value

        def load_block(column):
            return load[column * gy_count + row]

        def store_load(group, tile, value):
            rhs[tile, pl.ds(row * 16 + group * 4, 4), :] = value

        spread_groups(hess_block, 4, gx_count, store_hess)
        spread_groups(load_block, 4, gx_count, store_load)
        return 0

    lax.fori_loop(0, gy_count, unpack, 0, unroll=8)
    shape = (gy_count, width)
    lane, row = lanes(shape), rows_of(shape)
    in_z, in_y, in_x = lax.rem(lane, NEL) // EYD, lax.rem(lane, EYD), lane // NEL
    last_z, first_z = in_z == EZ - 1, in_z == 0
    last_x, first_x = in_x >= gx_count - 1, in_x == 0
    last_y, first_y = in_y == EYD - 1, in_y == 0
    end_y, begin_y = last_y & (row == gy_count - 1), first_y & (row == 0)

    bits = [(a, b, d) for a in range(2) for b in range(2) for d in range(2)]

    def turn(value, by, axis):
        size = shape[axis]
        by = by % size
        return pltpu.roll(value, by, axis) if by else value

    def corners(main, top):
        main_next, top_next = turn(main, -1, 0), turn(top, -1, 0)
        found = []
        for a, b, d in bits:

            def reached(main, top, by):
                value = turn(main, -(EYD * a + NEL * b + by), 1)
                return jnp.where(last_z, turn(top, -(NEL * b + by), 1), value) if a else value

            value = reached(main, top, d)
            if d:
                wrapped = jnp.where(end_y, 0.0, reached(main_next, top_next, 1 - EYD))
                value = jnp.where(last_y, wrapped, value)
            found.append(jnp.where(last_x, 0.0, value) if b else value)
        return found

    def settle(parts):
        main, top = None, None
        for (a, b, d), part in zip(bits, parts):
            before = turn(part, 1, 0) if d else None

            def given(by):
                value = turn(part, by + d, 1)
                if d:
                    wrapped = jnp.where(begin_y, 0.0, turn(before, by + 1 - EYD, 1))
                    value = jnp.where(first_y, wrapped, value)
                return jnp.where(first_x, 0.0, value) if b else value

            value = given(EYD * a + NEL * b)
            value = jnp.where(first_z, 0.0, value) if a else value
            main = value if main is None else main + value
            if a:
                value = given(NEL * b)
                top = value if top is None else top + value
        return main, jnp.where(last_z, top, 0.0)

    def strided(ref, start, stride):
        found = [ref[tile, pl.ds(start, gy_count, stride=stride), :] for tile in range(tiles)]
        return found[0] if tiles == 1 else jnp.concatenate(found, axis=1)

    def held(ref, index):
        found = [ref[tile, index * gy_count : (index + 1) * gy_count, :] for tile in range(tiles)]
        return found[0] if tiles == 1 else jnp.concatenate(found, axis=1)

    def channel(p, wz, wx, wy):
        source = (p * 3 + wz) * 3 + wx
        if source < HROWS:
            return held(coef, wy * HROWS + source)
        spare = wy * 14 + source - HROWS
        if spare < HROWS:
            return held(coef, 3 * HROWS + spare)
        return strided(rhs, (spare - HROWS) * 4 + 3, 16)

    pair_of = {}
    for p, (c, d) in enumerate(PAIRS):
        pair_of[c, d] = pair_of[d, c] = p

    def curved_by(vector):
        known = [corners(main, top) for main, top in vector]
        sums = [[None] * 8 for _ in range(3)]

        def add(c, n, term):
            sums[c][n] = term if sums[c][n] is None else sums[c][n] + term

        for p, (c, d) in enumerate(PAIRS):
            for wz in range(3):
                for wx in range(3):
                    for wy in range(3):
                        factor = channel(p, wz, wx, wy)
                        for n, low in enumerate(bits):
                            for m, high in enumerate(bits):
                                if (low[0] + high[0], low[1] + high[1], low[2] + high[2]) == (wz, wx, wy):
                                    add(c, n, factor * known[d][m])
                                    if c != d:
                                        add(d, n, factor * known[c][m])
        result = []
        for c in range(3):
            main, top = settle(sums[c])
            result.append((main + LAMBDA * vector[c][0], top + LAMBDA * vector[c][1]))
        bent = sum(known[c][n] * sums[c][n] for c in range(3) for n in range(8))
        return result, total(bent) + LAMBDA * inner(vector, vector)

    def total(value):
        return jnp.sum(jnp.sum(value, axis=0, keepdims=True), axis=1, keepdims=True)

    def inner(one, two):
        return total(sum(a[0] * b[0] + a[1] * b[1] for a, b in zip(one, two)))

    def combine(one, factor, two):
        return [(a[0] + factor * b[0], a[1] + factor * b[1]) for a, b in zip(one, two)]

    residual = []
    for c in range(3):
        main, top = None, None
        for bx in range(2):
            inside = strided(rhs, 2 * bx * 4 + c, 16)
            rim = turn(strided(rhs, (2 * bx + 1) * 4 + c, 16), 1, 0)
            spot = c * 2 + bx
            upper = strided(rhs, (2 + spot // 4) * 4 + 3, 16)
            upper = jnp.where(last_z, turn(upper, (EZ - 1 - spot % 4) * EYD, 1), 0.0)
            reached = first_y & (row > 0)
            inside = inside + jnp.where(reached, turn(rim, 1 - EYD, 1), 0.0)
            upper = upper + jnp.where(reached & last_z, turn(rim, 2 - EYD, 1), 0.0)
            if bx:
                main = main + jnp.where(first_x, 0.0, turn(inside, NEL, 1))
                top = top + jnp.where(first_x, 0.0, turn(upper, NEL, 1))
            else:
                main, top = inside, upper
        residual.append((main, top))
    direction = residual
    increment = None
    norm_now = inner(residual, residual)
    for iteration in range(ITERS):
        curved, bent = curved_by(direction)
        step = norm_now / bent
        if increment is None:
            increment = [(step * a, step * b) for a, b in direction]
        else:
            increment = combine(increment, step, direction)
        if iteration + 1 < ITERS:
            residual = combine(residual, -step, curved)
            norm_next = inner(residual, residual)
            direction = combine(residual, norm_next / norm_now, direction)
            norm_now = norm_next
    mine = (row == gy) & (in_x == gx)
    for c in range(3):
        for part, levels in ((increment[c][0], range(EZ)), (increment[c][1], [EZ])):
            line = jnp.sum(jnp.where(mine, part, 0.0), axis=0, keepdims=True)
            short = line[:, 0:128]
            for tile in range(1, tiles):
                short = short + line[:, tile * 128 : (tile + 1) * 128]
            short = pltpu.roll(jnp.broadcast_to(short, (8, 128)), lax.rem(128 - lax.rem(gx, 4) * NEL, 128), 1)
            for level in levels:
                start = min(level, EZ - 1) * EYD
                out[c, level] = short[0:1, start : start + EYD]


def solve(hess, load):
    gx_count, gy_count = lax.axis_size("gx"), lax.axis_size("gy")
    tiles = -(-gx_count // 4)
    vmem = pl.BlockSpec(memory_space=pltpu.VMEM)
    return pl.pallas_call(
        functools.partial(solve_kernel, gx_count, gy_count),
        out_shape=jax.ShapeDtypeStruct((3, EZ + 1, 1, EYD), F32),
        in_specs=[vmem] * 2,
        out_specs=vmem,
        scratch_shapes=[
            pltpu.VMEM((tiles, gy_count * 4 * HROWS, 128), F32),
            pltpu.VMEM((tiles, gy_count * 16, 128), F32),
        ],
        compiler_params=pltpu.CompilerParams(vmem_limit_bytes=LIMIT),
        cost_estimate=takes(3.5),
        name="solve",
    )(hess, load)


def swap(array, axis, partner):
    size = lax.axis_size(axis)
    pairs = [(i, partner(i)) for i in range(size)]
    return lax.ppermute(array, axis, [(i, j) for i, j in pairs if 0 <= j < size])


def swap_x(array, kind):
    if kind == 0:
        return swap(array, "gx", lambda i: i ^ 1)
    return swap(array, "gx", lambda i: i + 1 if i % 2 else i - 1)


def swap_y(array, kind):
    size = lax.axis_size("gy")
    partner = (
        lambda i: i ^ 1,
        lambda i: (i + 1 if i % 2 else i - 1) % size,
        lambda i: i ^ 2,
        lambda i: (i + 2 if i // 2 % 2 else i - 2) % size,
    )[kind]
    return swap(array, "gy", partner)


def gather_steps(gx_count, gy_count):
    far = [("gy", 1 << k) for k in range(1, gy_count.bit_length() - 1)]
    return [*far, ("gy", 1), *[("gx", 1 << k) for k in reversed(range(gx_count.bit_length() - 1))]]


def block_index(steps, relative):
    found = 0
    for k, (axis, bit) in enumerate(steps):
        found = found + jnp.where(jnp.bitwise_and(relative[axis], bit) != 0, 1 << k, 0)
    return found


def swapped(known, step):
    axis, bit = step
    return swap(known, axis, lambda j: j ^ bit)


def doubled(known, step):
    return jnp.concatenate([known, swapped(known, step)], axis=0)


def body(reference_image, deformed_image, route, within, xshift, fractions):
    m0, m1, m2, m3, thick, own, place = ask(
        route.reshape(1, NEL), within.reshape(1, NEL), xshift.reshape(1, NEL), reference_image, deformed_image
    )
    asks = (m0, m1, m2, m3)
    q = {kind: swap_y(asks[kind], kind) for kind in KINDS}
    d1, d0 = swap_x(thick, 1), swap_x(thick, 0)
    grad, packed, extra, portions = moments(reference_image, (d0, d1), (q[0], q[1]), fractions.reshape(NEL, 3))
    q[3], q[0], q[1], q[2], packed = lax.optimization_barrier((q[3], q[0], q[1], q[2], packed))
    *served, at_home = serve(deformed_image, d0, d1, [q[kind] for kind in KINDS] + [own], [8 * (k < 2) + k for k in KINDS] + [4])
    known = packed[None]
    bricks = [swap_y(block, kind) for kind, block in zip(KINDS, served)] + [at_home]
    steps = gather_steps(lax.axis_size("gx"), lax.axis_size("gy"))
    for k, step in enumerate(steps[:-3]):
        if k == 1:
            known, at_home = lax.optimization_barrier((known, at_home))
        known = doubled(known, step)
    bricks[-1] = at_home
    bricks, known = lax.optimization_barrier((bricks, known))
    mismatch, part = warp(place, bricks, reference_image, grad, portions, extra)
    beside, across = swapped(known, steps[-3]), swapped(known, steps[-2])
    known, beside, across, _ = lax.optimization_barrier((known, beside, across, part))
    load = lax.all_to_all(part, ("gx", "gy"), 0, 0)
    blocks = [known, beside, across, swapped(beside, steps[-2])]
    blocks = blocks + [swapped(block, steps[-1]) for block in blocks]
    return solve(jnp.concatenate(blocks, axis=0), load), mismatch


def solution(mesh):
    placed = (
        P(None, "gx", "gy"),
        P(None, "gx", "gy"),
        P("gx", "gy", None, None),
        P("gx", "gy", None),
        P("gx", "gy", None),
        P("gx", "gy", None, None),
    )
    return jax.shard_map(
        body,
        mesh=mesh,
        in_specs=placed,
        out_specs=(P(None, None, "gx", "gy"), P(None, "gx", "gy")),
        check_vma=False,
    )
```

```python
import functools

import jax
import jax.numpy as jnp
import numpy as np
from jax import lax
from jax.experimental import pallas as pl
from jax.experimental.pallas import tpu as pltpu
from jax.sharding import PartitionSpec as P

EDGE = 16
EZ = 4
EYD = 8
SPAN = 2
ITERS = 3
NEL = 32
VOL = 4096
NZ = EZ * EDGE
NY = EYD * EDGE
LAMBDA = 0.05

PAIRS = ((0, 0), (0, 1), (0, 2), (1, 1), (1, 2), (2, 2))
HROWS = 40
KINDS = (3, 0, 1, 2)
LIMIT = 32 * 1024 * 1024

F32 = jnp.float32
BF16 = jnp.bfloat16

UPPER = (np.arange(EDGE) + 0.5) / EDGE
HAT = np.stack([1.0 - UPPER, UPPER])
PRODUCTS = np.stack([HAT[0] * HAT[0], HAT[0] * HAT[1], HAT[1] * HAT[1]])


def hat_product(which, position):
    upper = (position.astype(F32) + 0.5) * (1.0 / EDGE)
    lower = 1.0 - upper
    return jnp.where(which == 0, lower * lower, jnp.where(which == 1, lower * upper, upper * upper))


def hat_weight(which, position):
    upper = (position.astype(F32) + 0.5) * (1.0 / EDGE)
    return jnp.where(which == 0, 1.0 - upper, upper)


def along_y(weight, groups):
    shape = (NY, 128)
    row, lane = rows_of(shape), lanes(shape)
    group = lane // NEL
    inside = (row // EDGE == lax.rem(lane, NEL)) & (group >= groups[0]) & (group <= groups[-1])
    return jnp.where(inside, weight(group, lax.rem(row, EDGE)) * (1.0 / VOL), 0.0)


def three_parts(value):
    high = value.astype(BF16)
    rest = value - high.astype(F32)
    middle = rest.astype(BF16)
    return [high, middle, (rest - middle.astype(F32)).astype(BF16)]


def weighed(value, weights):
    high = weights.astype(BF16)
    both = jnp.concatenate([high, (weights - high.astype(F32)).astype(BF16)], axis=1)
    found = jnp.dot(
        jnp.concatenate(three_parts(value), axis=1),
        jnp.concatenate([both] * 3, axis=0),
        preferred_element_type=F32,
    )
    return found[:, :128] + found[:, 128:]


def weighed_once(value, weights):
    weights = weights.astype(BF16)
    return jnp.dot(
        jnp.concatenate(three_parts(value), axis=1),
        jnp.concatenate([weights] * 3, axis=0),
        preferred_element_type=F32,
    )


def layered(found, slab, slabs, weights):
    total = None
    for ez in range(EZ):
        start = (ez * slabs + slab) * EDGE
        part = found[start : start + EDGE] * weights
        part = part[:8] + part[8:]
        part = pltpu.roll(part, ez * EYD, 1) if ez else part
        total = part if total is None else total + part
    return jnp.sum(total, axis=0, keepdims=True)


def lanes(shape):
    return lax.broadcasted_iota(jnp.int32, shape, len(shape) - 1)


def rows_of(shape):
    return lax.broadcasted_iota(jnp.int32, shape, len(shape) - 2)


def even(value):
    return lax.rem(value, 2) == 0


def takes(microseconds):
    return pl.CostEstimate(flops=0, bytes_accessed=int(microseconds * 3.69e6), transcendentals=0)


def ask_kernel(gx_count, route, within, xshift, ref, deformed, m0, m1, m2, m3, thick, own, place):
    gx, gy = lax.axis_index("gx"), lax.axis_index("gy")
    gx_even, gy_even, half_even = even(gx), even(gy), even(gy // 2)
    row, lane = rows_of((8, 128)), lanes((8, 128))
    wide = (8, NEL)
    offset = jnp.broadcast_to(route[...], wide) - SPAN
    moved = jnp.clip(gx + jnp.broadcast_to(xshift[...], wide) - 1, 0, gx_count - 1) - gx
    ahead = jnp.where(gx_even, 1, 2)
    bank = jnp.where(moved == 0, 0, jnp.where(moved == 1, ahead, 3 - ahead))
    code = bank * NEL + lanes(wide) // EYD * EYD + jnp.broadcast_to(within[...], wide)
    plus = jnp.where(gy_even, 0, 1)
    twice = jnp.where(half_even, 2, 3)
    j = jnp.where(offset == 1, plus, jnp.where(offset == -1, 1 - plus, jnp.where(offset == 2, twice, 5 - twice)))
    j = jnp.where(offset == 0, 4, j)
    mine = (rows_of(wide) == j).astype(F32)
    square = (NEL, NEL)
    earlier = (rows_of(square) < lanes(square)).astype(F32).astype(BF16)
    ahead_of = jnp.dot(mine.astype(BF16), earlier, preferred_element_type=F32)
    slot = jnp.sum(mine * ahead_of, axis=0, keepdims=True)
    order = jnp.full(wide, 4, jnp.int32)
    for at, kind in enumerate(KINDS):
        order = jnp.where(j == kind, at, order)
    found = jnp.where(rows_of(wide) == lanes(wide) // EYD, order.astype(F32) * 8.0 + slot, 0.0)
    long = (NEL, 128)
    widen = (lax.rem(rows_of(long), EYD) == lanes(long) // EDGE).astype(F32).astype(BF16)
    found = jnp.dot(found.astype(BF16), widen, preferred_element_type=F32)
    place[...] = found.astype(jnp.int32) * EDGE + lax.rem(lane, EDGE)
    tall = (128, NEL)
    taken = (rows_of(tall) == jnp.broadcast_to(slot, tall).astype(jnp.int32)).astype(F32).astype(BF16)
    asked = lax.dot_general(
        (mine * code.astype(F32)).astype(BF16), taken, (((1,), (1,)), ((), ())), preferred_element_type=F32
    )
    own[...] = asked
    m2[...] = asked
    m3[...] = asked
    m0[8:, :] = asked
    m1[8:, :] = asked
    image = ref[...]
    first = jnp.where(gy_even, NY - 1, 0)
    wanted = jnp.where(row == 0, first, jnp.where(row == 1, NY - 1 - first, -1))
    pick = (lane == wanted).astype(F32).astype(BF16)
    columns = lax.dot_general(pick, image.reshape(NZ * EDGE, NY), (((1,), (1,)), ((), ())), preferred_element_type=F32)
    for i in range(8):
        m0[i : i + 1, :] = columns[0:1, i * 128 : (i + 1) * 128]
        m1[i : i + 1, :] = columns[1:2, i * 128 : (i + 1) * 128]
    thick[0:NZ] = deformed[...]
    image = image.astype(F32)
    for k, face in enumerate((image[:, 0, :], image[:, EDGE - 1, :])):
        thick[NZ + k * EZ : NZ + (k + 1) * EZ] = face.astype(BF16).reshape(EZ, EDGE, NY)


def ask(route, within, xshift, ref, deformed):
    smem = pl.BlockSpec(memory_space=pltpu.SMEM)
    vmem = pl.BlockSpec(memory_space=pltpu.VMEM)
    return pl.pallas_call(
        functools.partial(ask_kernel, lax.axis_size("gx")),
        out_shape=(
            jax.ShapeDtypeStruct((16, 128), F32),
            jax.ShapeDtypeStruct((16, 128), F32),
            jax.ShapeDtypeStruct((8, 128), F32),
            jax.ShapeDtypeStruct((8, 128), F32),
            jax.ShapeDtypeStruct((NZ + 2 * EZ, EDGE, NY), BF16),
            jax.ShapeDtypeStruct((8, 128), F32),
            jax.ShapeDtypeStruct((8, 128), jnp.int32),
        ),
        in_specs=[vmem] * 5,
        out_specs=(vmem,) * 7,
        cost_estimate=takes(2.0),
        name="ask",
    )(route, within, xshift, ref, deformed)


def gather_columns(table, slabs, sources, places):
    table[...] = jnp.zeros_like(table)
    shape = (EDGE, NY)
    row, lane = rows_of(shape), lanes(shape)
    for i, (source, place) in enumerate(zip(sources, places)):
        start = pl.multiple_of(i * NY + source * EDGE, EDGE)
        table[pl.ds(start, EDGE), :] = (lane == row + place * EDGE).astype(F32).astype(BF16)
    return jnp.dot(jnp.concatenate(slabs, axis=1), table[...], preferred_element_type=F32)


def serve_kernel(lines, *refs):
    count = len(lines)
    asked, outs = refs[3 : 3 + count], refs[3 + count : 3 + 2 * count]
    banks, tables, codes, scalars, sem = refs[3 + 2 * count :]
    for j in range(count):
        codes[j] = asked[j][lines[j] // 8 * 8 : lines[j] // 8 * 8 + 8].astype(jnp.int32)
    copy = pltpu.make_async_copy(codes, scalars, sem)
    copy.start()
    for i in range(3):
        banks[i] = refs[i][0:NZ]
    copy.wait()
    for j in range(count):
        slabs, columns = [], []
        for slot in range(8):
            code = scalars[j, lines[j] % 8, slot]
            start = jnp.bitwise_and(code, NEL - EYD) * (EDGE // EYD)
            slab = banks[lax.shift_right_logical(code, 5), pl.ds(start, EDGE)]
            slabs.append(slab.reshape(EDGE * EDGE, NY))
            columns.append(jnp.bitwise_and(code, EYD - 1))
        packed = gather_columns(tables.at[j], slabs, columns, range(8))
        outs[j][...] = packed.reshape(EDGE, EDGE, NY).astype(BF16)


def serve(own, d0, d1, asked, lines):
    vmem = pl.BlockSpec(memory_space=pltpu.VMEM)
    count = len(lines)
    return pl.pallas_call(
        functools.partial(serve_kernel, lines),
        out_shape=(jax.ShapeDtypeStruct((EDGE, EDGE, NY), BF16),) * count,
        in_specs=[vmem] * 3 + [vmem] * count,
        out_specs=(vmem,) * count,
        scratch_shapes=[
            pltpu.VMEM((3, NZ, EDGE, NY), BF16),
            pltpu.VMEM((count, 8 * NY, NY), BF16),
            pltpu.VMEM((count, 8, 128), jnp.int32),
            pltpu.SMEM((count, 8, 128), jnp.int32),
            pltpu.SemaphoreType.DMA,
        ],
        compiler_params=pltpu.CompilerParams(vmem_limit_bytes=LIMIT),
        cost_estimate=takes(1.0 + 0.2 * count),
        name="serve",
    )(own, d0, d1, *asked)


def moments_kernel(gy_count, r0, r1, a1, a0, ref, frac, grad, packed, extra, portions, side, slabs):
    gx, gy = lax.axis_index("gx"), lax.axis_index("gy")
    gx_even, gy_even = even(gx), even(gy)
    side[...] = jnp.zeros((8, NZ * EDGE), F32)
    keep0 = jnp.where(gy_even, gy < gy_count - 1, gy > 0).astype(F32)
    keep1 = jnp.where(gy_even, gy > 0, gy < gy_count - 1).astype(F32)
    for i in range(8):
        side[0:1, i * 128 : (i + 1) * 128] = r0[i : i + 1, :] * keep0
        side[1:2, i * 128 : (i + 1) * 128] = r1[i : i + 1, :] * keep1
    row, lane = rows_of((8, 128)), lanes((8, 128))
    target0 = jnp.where(gy_even, NY - 1, 0)
    spot = jnp.where(row == 0, target0, jnp.where(row == 1, NY - 1 - target0, -1))
    spread = (lane == spot).astype(F32).astype(BF16)
    rim = lax.dot_general(
        side[...].astype(BF16), spread, (((0,), (0,)), ((), ())), preferred_element_type=F32
    ).reshape(NZ, EDGE, NY)
    low0, high0, low1, high1 = (
        thick[NZ + k * EZ : NZ + (k + 1) * EZ].astype(F32).reshape(NZ, NY) for thick in (a0, a1) for k in range(2)
    )
    before = jnp.where(gx_even, high1, high0)
    after = jnp.where(gx_even, low0, low1)
    lane2, row2 = lanes((EDGE, NY)), rows_of((EDGE, NY))

    def slopes(z):
        plane = ref[z].astype(F32)
        below = ref[z - 1].astype(F32) if z > 0 else jnp.zeros((EDGE, NY), F32)
        above = ref[z + 1].astype(F32) if z + 1 < NZ else jnp.zeros((EDGE, NY), F32)
        rim_z = rim[z]
        nxt = jnp.where(row2 == EDGE - 1, after[z : z + 1, :], pltpu.roll(plane, EDGE - 1, 0))
        prv = jnp.where(row2 == 0, before[z : z + 1, :], pltpu.roll(plane, 1, 0))
        right = jnp.where(lane2 == NY - 1, rim_z, pltpu.roll(plane, NY - 1, 1))
        left = jnp.where(lane2 == 0, rim_z, pltpu.roll(plane, 1, 1))
        rounded = [(value * 0.5).astype(BF16) for value in (above - below, nxt - prv, right - left)]
        for c in range(3):
            grad[c, z] = rounded[c]
        return [value.astype(F32) for value in rounded]

    for ez in range(EZ):
        sums = [[jnp.zeros((EDGE, NY), F32) for _ in range(3)] for _ in PAIRS]
        for k in range(EDGE // 2):
            both = [slopes(ez * EDGE + k), slopes(ez * EDGE + EDGE - 1 - k)]
            away = float(0.5 - UPPER[k])
            for p, (c, d) in enumerate(PAIRS):
                low, high = (g[c] * g[d] for g in both)
                even_part, odd_part = low + high, high - low
                sums[p][0] = sums[p][0] + even_part
                sums[p][1] = sums[p][1] + away * odd_part
                sums[p][2] = sums[p][2] + (away * away) * even_part
        for p in range(len(PAIRS)):
            quarter, first, second = sums[p][0] * 0.25, sums[p][1], sums[p][2]
            for w, value in enumerate((quarter - first + second, quarter - second, quarter + first + second)):
                start = (ez * 18 + p * 3 + w) * EDGE
                slabs[start : start + EDGE, :] = value
    found = weighed(slabs[...], along_y(hat_product, (0, 1, 2)))
    across = [hat_product(w, row2) for w in range(3)]
    row8, group8 = rows_of((8, 128)), lanes((8, 128)) // NEL
    tiles = [jnp.zeros((8, 128), F32) for _ in range(HROWS // 8 + 1)]
    for slab in range(18):
        for w in range(3):
            line = layered(found, slab, 18, across[w])
            source = slab * 3 + w
            if source < HROWS:
                tiles[source // 8] = jnp.where((row8 == source % 8) & (group8 < 3), line, tiles[source // 8])
            else:
                for wy in range(3):
                    spare = wy * 14 + source - HROWS
                    turned = pltpu.roll(line, (3 - wy) * NEL, 1)
                    tiles[spare // 8] = jnp.where((row8 == spare % 8) & (group8 == 3), turned, tiles[spare // 8])
    total = jnp.concatenate(tiles, axis=0)
    total = pltpu.roll(total, lax.rem(gx, 4) * NEL, 1)
    packed[...] = total[:HROWS]
    line = pltpu.roll(total[HROWS:], NEL, 1)[0:1] + pltpu.roll(total[HROWS:], 2 * NEL, 1)[1:2]
    extra[...] = jnp.where(row == 3, line, 0.0)
    element, lane_e = rows_of((EYD, 128)), lanes((EYD, 128))
    unfold = (lane_e // EDGE == element).astype(F32).astype(BF16)
    for ez in range(EZ):
        tenths = frac[ez * EYD : (ez + 1) * EYD, :].astype(F32).astype(BF16)
        wide = lax.dot_general(tenths, unfold, (((0,), (0,)), ((), ())), preferred_element_type=F32)
        portions[ez, 0:3, :] = wide * (1.0 / EDGE)


def moments(ref, faces_x, faces_y, fractions):
    vmem = pl.BlockSpec(memory_space=pltpu.VMEM)
    return pl.pallas_call(
        functools.partial(moments_kernel, lax.axis_size("gy")),
        out_shape=(
            jax.ShapeDtypeStruct((3, NZ, EDGE, NY), BF16),
            jax.ShapeDtypeStruct((HROWS, 128), F32),
            jax.ShapeDtypeStruct((8, 128), F32),
            jax.ShapeDtypeStruct((EZ, 8, 128), F32),
        ),
        in_specs=[vmem] * 6,
        out_specs=(vmem,) * 4,
        scratch_shapes=[pltpu.VMEM((8, NZ * EDGE), F32), pltpu.VMEM((EZ * 18 * EDGE, NY), F32)],
        compiler_params=pltpu.CompilerParams(vmem_limit_bytes=LIMIT),
        cost_estimate=takes(2.2),
        name="moments",
    )(faces_y[0], faces_y[1], faces_x[1], faces_x[0], ref, fractions)


def warp_kernel(b0, b1, b2, b3, b4, place, ref, grad, portions, extra, mismatch, packed, slabs):
    gx = lax.axis_index("gx")
    flat = (EDGE * EDGE, NY)
    lane = lanes(flat)
    at_x_rim = lax.rem(lax.broadcasted_iota(jnp.int32, flat, 0), EDGE) == EDGE - 1
    at_y_rim = lax.rem(lane, EDGE) == EDGE - 1
    came = jnp.concatenate([block[...].reshape(flat) for block in (b0, b1, b2, b3, b4)], axis=1)
    table = (5 * NY, NY)
    fetched = []
    for half in range(2):
        spots = [jnp.broadcast_to(place[ez : ez + 1, :], table) for ez in (2 * half, 2 * half + 1)]
        moves = [(rows_of(table) == spot).astype(F32).astype(BF16) for spot in spots]
        fetched.append(jnp.dot(came, jnp.concatenate(moves, axis=1), preferred_element_type=F32))
    for ez in range(EZ):
        blended = fetched[ez // 2][:, ez % 2 * NY : (ez % 2 + 1) * NY]
        portion = portions[ez]
        ty, tx, tz = portion[2:3, :], portion[1:2, :], portion[0:1, :]
        shifted = jnp.where(at_y_rim, blended, pltpu.roll(blended, NY - 1, 1))
        blended = (1.0 - ty) * blended + ty * shifted
        shifted = jnp.where(at_x_rim, blended, pltpu.roll(blended, EDGE * EDGE - 1, 0))
        blended = (1.0 - tx) * blended + tx * shifted
        shifted = jnp.concatenate([blended[EDGE:], blended[-EDGE:]], axis=0)
        blended = (1.0 - tz) * blended + tz * shifted
        blended = blended.reshape(EDGE, EDGE, NY)
        sums = [[jnp.zeros((EDGE, NY), F32) for _ in range(2)] for _ in range(3)]
        for k in range(EDGE // 2):
            planes = (ez * EDGE + k, ez * EDGE + EDGE - 1 - k)
            aparts = [ref[z].astype(F32) - blended[z - ez * EDGE] for z in planes]
            for z, apart in zip(planes, aparts):
                mismatch[z] = apart
            for c in range(3):
                low, high = (grad[c, z].astype(F32) * apart for z, apart in zip(planes, aparts))
                sums[c][0] = sums[c][0] + (low + high)
                sums[c][1] = sums[c][1] + float(0.5 - UPPER[k]) * (high - low)
        for c in range(3):
            half, first = sums[c][0] * 0.5, sums[c][1]
            for a, value in enumerate((half - first, half + first)):
                start = (ez * 6 + c * 2 + a) * EDGE
                slabs[start : start + EDGE, :] = value
    found = weighed_once(slabs[...], along_y(lambda group, at: hat_weight(lax.rem(group, 2), at), (0, 1, 2, 3)))
    across = hat_weight(lanes((EDGE, 128)) // (2 * NEL), rows_of((EDGE, 128)))
    row, lane = rows_of((8, 128)), lanes((8, 128))
    group, in_z, in_y = lane // NEL, lax.rem(lane, NEL) // EYD, lax.rem(lane, EYD)
    total = jnp.zeros((8, 128), F32)
    for c in range(3):
        lower, upper = (layered(found, c * 2 + a, 6, across) for a in range(2))
        lower, upper = (jnp.broadcast_to(line, (8, 128)) for line in (lower, upper))
        level = lower + jnp.where(in_z > 0, pltpu.roll(upper, EYD, 1), 0.0)
        top = jnp.where(in_z == EZ - 1, upper, 0.0)

        def joined(line):
            return line + jnp.where(in_y > 0, pltpu.roll(line, 128 - NEL + 1, 1), 0.0)

        rim = jnp.where(in_y == EYD - 1, level, 0.0) + jnp.where(in_y == EYD - 2, pltpu.roll(top, 127, 1), 0.0)
        main = jnp.where(lax.rem(group, 2) == 0, joined(level), rim)
        total = jnp.where(row == c, main, total)
        top = joined(top)
        for bx in range(2):
            start = 2 * NEL + (c * 2 + bx) * EYD
            moved = pltpu.roll(top, (start - (bx * 2 * NEL + (EZ - 1) * EYD)) % 128, 1)
            total = jnp.where((row == 3) & (lane // EYD == start // EYD), moved, total)
    total = pltpu.roll(total, lax.rem(gx, 4) * NEL, 1) + extra[...]
    packed[...] = jnp.broadcast_to(total[0:4], packed.shape)


def warp(place, bricks, ref, grad, portions, extra):
    vmem = pl.BlockSpec(memory_space=pltpu.VMEM)
    devices = lax.axis_size("gx") * lax.axis_size("gy")
    return pl.pallas_call(
        warp_kernel,
        out_shape=(jax.ShapeDtypeStruct((NZ, EDGE, NY), F32), jax.ShapeDtypeStruct((devices, 4, 128), F32)),
        in_specs=[vmem] * 10,
        out_specs=(vmem, vmem),
        scratch_shapes=[
            pltpu.VMEM((EZ * 6 * EDGE, NY), F32),
        ],
        compiler_params=pltpu.CompilerParams(vmem_limit_bytes=LIMIT),
        cost_estimate=takes(4.0),
        name="warp",
    )(*bricks, place, ref, grad, portions, extra)


def spread_groups(block_of, groups, gx_count, store):
    tiles = -(-gx_count // 4)
    for tile in range(tiles):
        members = range(4 * tile, min(4 * tile + 4, gx_count))
        blocks = {gx: block_of(gx) for gx in members}
        for group in range(groups):
            merged = jnp.zeros_like(blocks[members[0]])
            lane = lanes(merged.shape)
            for gx in members:
                merged = jnp.where(lane // NEL == (group + gx) % 4, blocks[gx], merged)
            store(group, tile, pltpu.roll(merged, (128 - NEL * group) % 128, 1) if group else merged)


def solve_kernel(gx_count, gy_count, hess, load, out, coef, rhs):
    gx, gy = lax.axis_index("gx"), lax.axis_index("gy")
    steps = gather_steps(gx_count, gy_count)
    tiles = -(-gx_count // 4)
    width = 128 * tiles

    def unpack(row, _):
        def hess_block(column):
            relative = dict(gx=jnp.bitwise_xor(gx, column), gy=jnp.bitwise_xor(gy, row))
            return hess[block_index(steps, relative)]

        def store_hess(group, tile, value):
            coef[tile, pl.ds(group * HROWS * gy_count + row, HROWS, stride=gy_count), :] = value

        def load_block(column):
            return load[column * gy_count + row]

        def store_load(group, tile, value):
            rhs[tile, pl.ds(row * 16 + group * 4, 4), :] = value

        spread_groups(hess_block, 4, gx_count, store_hess)
        spread_groups(load_block, 4, gx_count, store_load)
        return 0

    lax.fori_loop(0, gy_count, unpack, 0, unroll=8)
    shape = (gy_count, width)
    lane, row = lanes(shape), rows_of(shape)
    in_z, in_y, in_x = lax.rem(lane, NEL) // EYD, lax.rem(lane, EYD), lane // NEL
    last_z, first_z = in_z == EZ - 1, in_z == 0
    last_x, first_x = in_x >= gx_count - 1, in_x == 0
    last_y, first_y = in_y == EYD - 1, in_y == 0
    end_y, begin_y = last_y & (row == gy_count - 1), first_y & (row == 0)

    bits = [(a, b, d) for a in range(2) for b in range(2) for d in range(2)]

    def turn(value, by, axis):
        size = shape[axis]
        by = by % size
        return pltpu.roll(value, by, axis) if by else value

    def corners(main, top):
        main_next, top_next = turn(main, -1, 0), turn(top, -1, 0)
        found = []
        for a, b, d in bits:

            def reached(main, top, by):
                value = turn(main, -(EYD * a + NEL * b + by), 1)
                return jnp.where(last_z, turn(top, -(NEL * b + by), 1), value) if a else value

            value = reached(main, top, d)
            if d:
                wrapped = jnp.where(end_y, 0.0, reached(main_next, top_next, 1 - EYD))
                value = jnp.where(last_y, wrapped, value)
            found.append(jnp.where(last_x, 0.0, value) if b else value)
        return found

    def settle(parts):
        main, top = None, None
        for (a, b, d), part in zip(bits, parts):
            before = turn(part, 1, 0) if d else None

            def given(by):
                value = turn(part, by + d, 1)
                if d:
                    wrapped = jnp.where(begin_y, 0.0, turn(before, by + 1 - EYD, 1))
                    value = jnp.where(first_y, wrapped, value)
                return jnp.where(first_x, 0.0, value) if b else value

            value = given(EYD * a + NEL * b)
            value = jnp.where(first_z, 0.0, value) if a else value
            main = value if main is None else main + value
            if a:
                value = given(NEL * b)
                top = value if top is None else top + value
        return main, jnp.where(last_z, top, 0.0)

    def strided(ref, start, stride):
        found = [ref[tile, pl.ds(start, gy_count, stride=stride), :] for tile in range(tiles)]
        return found[0] if tiles == 1 else jnp.concatenate(found, axis=1)

    def held(ref, index):
        found = [ref[tile, index * gy_count : (index + 1) * gy_count, :] for tile in range(tiles)]
        return found[0] if tiles == 1 else jnp.concatenate(found, axis=1)

    def channel(p, wz, wx, wy):
        source = (p * 3 + wz) * 3 + wx
        if source < HROWS:
            return held(coef, wy * HROWS + source)
        spare = wy * 14 + source - HROWS
        if spare < HROWS:
            return held(coef, 3 * HROWS + spare)
        return strided(rhs, (spare - HROWS) * 4 + 3, 16)

    pair_of = {}
    for p, (c, d) in enumerate(PAIRS):
        pair_of[c, d] = pair_of[d, c] = p

    def curved_by(vector):
        known = [corners(main, top) for main, top in vector]
        sums = [[None] * 8 for _ in range(3)]

        def add(c, n, term):
            sums[c][n] = term if sums[c][n] is None else sums[c][n] + term

        for p, (c, d) in enumerate(PAIRS):
            for wz in range(3):
                for wx in range(3):
                    for wy in range(3):
                        factor = channel(p, wz, wx, wy)
                        for n, low in enumerate(bits):
                            for m, high in enumerate(bits):
                                if (low[0] + high[0], low[1] + high[1], low[2] + high[2]) == (wz, wx, wy):
                                    add(c, n, factor * known[d][m])
                                    if c != d:
                                        add(d, n, factor * known[c][m])
        result = []
        for c in range(3):
            main, top = settle(sums[c])
            result.append((main + LAMBDA * vector[c][0], top + LAMBDA * vector[c][1]))
        bent = sum(known[c][n] * sums[c][n] for c in range(3) for n in range(8))
        return result, total(bent) + LAMBDA * inner(vector, vector)

    def total(value):
        return jnp.sum(jnp.sum(value, axis=0, keepdims=True), axis=1, keepdims=True)

    def inner(one, two):
        return total(sum(a[0] * b[0] + a[1] * b[1] for a, b in zip(one, two)))

    def combine(one, factor, two):
        return [(a[0] + factor * b[0], a[1] + factor * b[1]) for a, b in zip(one, two)]

    residual = []
    for c in range(3):
        main, top = None, None
        for bx in range(2):
            inside = strided(rhs, 2 * bx * 4 + c, 16)
            rim = turn(strided(rhs, (2 * bx + 1) * 4 + c, 16), 1, 0)
            spot = c * 2 + bx
            upper = strided(rhs, (2 + spot // 4) * 4 + 3, 16)
            upper = jnp.where(last_z, turn(upper, (EZ - 1 - spot % 4) * EYD, 1), 0.0)
            reached = first_y & (row > 0)
            inside = inside + jnp.where(reached, turn(rim, 1 - EYD, 1), 0.0)
            upper = upper + jnp.where(reached & last_z, turn(rim, 2 - EYD, 1), 0.0)
            if bx:
                main = main + jnp.where(first_x, 0.0, turn(inside, NEL, 1))
                top = top + jnp.where(first_x, 0.0, turn(upper, NEL, 1))
            else:
                main, top = inside, upper
        residual.append((main, top))
    direction = residual
    increment = None
    norm_now = inner(residual, residual)
    for iteration in range(ITERS):
        curved, bent = curved_by(direction)
        step = norm_now / bent
        if increment is None:
            increment = [(step * a, step * b) for a, b in direction]
        else:
            increment = combine(increment, step, direction)
        if iteration + 1 < ITERS:
            residual = combine(residual, -step, curved)
            norm_next = inner(residual, residual)
            direction = combine(residual, norm_next / norm_now, direction)
            norm_now = norm_next
    mine = (row == gy) & (in_x == gx)
    for c in range(3):
        for part, levels in ((increment[c][0], range(EZ)), (increment[c][1], [EZ])):
            line = jnp.sum(jnp.where(mine, part, 0.0), axis=0, keepdims=True)
            short = line[:, 0:128]
            for tile in range(1, tiles):
                short = short + line[:, tile * 128 : (tile + 1) * 128]
            short = pltpu.roll(jnp.broadcast_to(short, (8, 128)), lax.rem(128 - lax.rem(gx, 4) * NEL, 128), 1)
            for level in levels:
                start = min(level, EZ - 1) * EYD
                out[c, level] = short[0:1, start : start + EYD]


def solve(hess, load):
    gx_count, gy_count = lax.axis_size("gx"), lax.axis_size("gy")
    tiles = -(-gx_count // 4)
    vmem = pl.BlockSpec(memory_space=pltpu.VMEM)
    return pl.pallas_call(
        functools.partial(solve_kernel, gx_count, gy_count),
        out_shape=jax.ShapeDtypeStruct((3, EZ + 1, 1, EYD), F32),
        in_specs=[vmem] * 2,
        out_specs=vmem,
        scratch_shapes=[
            pltpu.VMEM((tiles, gy_count * 4 * HROWS, 128), F32),
            pltpu.VMEM((tiles, gy_count * 16, 128), F32),
        ],
        compiler_params=pltpu.CompilerParams(vmem_limit_bytes=LIMIT),
        cost_estimate=takes(3.5),
        name="solve",
    )(hess, load)


def swap(array, axis, partner):
    size = lax.axis_size(axis)
    pairs = [(i, partner(i)) for i in range(size)]
    return lax.ppermute(array, axis, [(i, j) for i, j in pairs if 0 <= j < size])


def swap_x(array, kind):
    if kind == 0:
        return swap(array, "gx", lambda i: i ^ 1)
    return swap(array, "gx", lambda i: i + 1 if i % 2 else i - 1)


def swap_y(array, kind):
    size = lax.axis_size("gy")
    partner = (
        lambda i: i ^ 1,
        lambda i: (i + 1 if i % 2 else i - 1) % size,
        lambda i: i ^ 2,
        lambda i: (i + 2 if i // 2 % 2 else i - 2) % size,
    )[kind]
    return swap(array, "gy", partner)


def gather_steps(gx_count, gy_count):
    far = [("gy", 1 << k) for k in range(1, gy_count.bit_length() - 1)]
    return [*far, ("gy", 1), *[("gx", 1 << k) for k in reversed(range(gx_count.bit_length() - 1))]]


def block_index(steps, relative):
    found = 0
    for k, (axis, bit) in enumerate(steps):
        found = found + jnp.where(jnp.bitwise_and(relative[axis], bit) != 0, 1 << k, 0)
    return found


def swapped(known, step):
    axis, bit = step
    return swap(known, axis, lambda j: j ^ bit)


def doubled(known, step):
    return jnp.concatenate([known, swapped(known, step)], axis=0)


def body(reference_image, deformed_image, route, within, xshift, fractions):
    m0, m1, m2, m3, thick, own, place = ask(
        route.reshape(1, NEL), within.reshape(1, NEL), xshift.reshape(1, NEL), reference_image, deformed_image
    )
    asks = (m0, m1, m2, m3)
    q = {kind: swap_y(asks[kind], kind) for kind in KINDS}
    d1, d0 = swap_x(thick, 1), swap_x(thick, 0)
    grad, packed, extra, portions = moments(reference_image, (d0, d1), (q[0], q[1]), fractions.reshape(NEL, 3))
    q[3], q[0], q[1], q[2], packed = lax.optimization_barrier((q[3], q[0], q[1], q[2], packed))
    *served, at_home = serve(deformed_image, d0, d1, [q[kind] for kind in KINDS] + [own], [8 * (k < 2) + k for k in KINDS] + [4])
    known = packed[None]
    bricks = [swap_y(block, kind) for kind, block in zip(KINDS, served)] + [at_home]
    steps = gather_steps(lax.axis_size("gx"), lax.axis_size("gy"))
    for k, step in enumerate(steps[:-3]):
        if k == 1:
            known, at_home = lax.optimization_barrier((known, at_home))
        known = doubled(known, step)
    bricks[-1] = at_home
    bricks, known = lax.optimization_barrier((bricks, known))
    mismatch, part = warp(place, bricks, reference_image, grad, portions, extra)
    beside, across = swapped(known, steps[-3]), swapped(known, steps[-2])
    known, beside, across, _ = lax.optimization_barrier((known, beside, across, part))
    load = lax.all_to_all(part, ("gx", "gy"), 0, 0)
    blocks = [known, beside, across, swapped(beside, steps[-2])]
    blocks = blocks + [swapped(block, steps[-1]) for block in blocks]
    return solve(jnp.concatenate(blocks, axis=0), load), mismatch


def solution(mesh):
    placed = (
        P(None, "gx", "gy"),
        P(None, "gx", "gy"),
        P("gx", "gy", None, None),
        P("gx", "gy", None),
        P("gx", "gy", None),
        P("gx", "gy", None, None),
    )
    return jax.shard_map(
        body,
        mesh=mesh,
        in_specs=placed,
        out_specs=(P(None, None, "gx", "gy"), P(None, "gx", "gy")),
        check_vma=False,
    )
```

```python
import functools

import jax
import jax.numpy as jnp
import numpy as np
from jax import lax
from jax.experimental import pallas as pl
from jax.experimental.pallas import tpu as pltpu
from jax.sharding import PartitionSpec as P

EDGE = 16
EZ = 4
EYD = 8
SPAN = 2
ITERS = 3
NEL = 32
VOL = 4096
NZ = EZ * EDGE
NY = EYD * EDGE
LAMBDA = 0.05

PAIRS = ((0, 0), (0, 1), (0, 2), (1, 1), (1, 2), (2, 2))
HROWS = 40
KINDS = (3, 0, 1, 2)
LIMIT = 32 * 1024 * 1024

F32 = jnp.float32
BF16 = jnp.bfloat16

UPPER = (np.arange(EDGE) + 0.5) / EDGE
HAT = np.stack([1.0 - UPPER, UPPER])
PRODUCTS = np.stack([HAT[0] * HAT[0], HAT[0] * HAT[1], HAT[1] * HAT[1]])


def hat_product(which, position):
    upper = (position.astype(F32) + 0.5) * (1.0 / EDGE)
    lower = 1.0 - upper
    return jnp.where(which == 0, lower * lower, jnp.where(which == 1, lower * upper, upper * upper))


def hat_weight(which, position):
    upper = (position.astype(F32) + 0.5) * (1.0 / EDGE)
    return jnp.where(which == 0, 1.0 - upper, upper)


def along_y(weight, groups):
    shape = (NY, 128)
    row, lane = rows_of(shape), lanes(shape)
    group = lane // NEL
    inside = (row // EDGE == lax.rem(lane, NEL)) & (group >= groups[0]) & (group <= groups[-1])
    return jnp.where(inside, weight(group, lax.rem(row, EDGE)) * (1.0 / VOL), 0.0)


def three_parts(value):
    high = value.astype(BF16)
    rest = value - high.astype(F32)
    middle = rest.astype(BF16)
    return [high, middle, (rest - middle.astype(F32)).astype(BF16)]


def weighed(value, weights):
    high = weights.astype(BF16)
    both = jnp.concatenate([high, (weights - high.astype(F32)).astype(BF16)], axis=1)
    found = jnp.dot(
        jnp.concatenate(three_parts(value), axis=1),
        jnp.concatenate([both] * 3, axis=0),
        preferred_element_type=F32,
    )
    return found[:, :128] + found[:, 128:]


def weighed_once(value, weights):
    weights = weights.astype(BF16)
    return jnp.dot(
        jnp.concatenate(three_parts(value), axis=1),
        jnp.concatenate([weights] * 3, axis=0),
        preferred_element_type=F32,
    )


def layered(found, slab, slabs, weights):
    total = None
    for ez in range(EZ):
        start = (ez * slabs + slab) * EDGE
        part = found[start : start + EDGE] * weights
        part = part[:8] + part[8:]
        part = pltpu.roll(part, ez * EYD, 1) if ez else part
        total = part if total is None else total + part
    return jnp.sum(total, axis=0, keepdims=True)


def lanes(shape):
    return lax.broadcasted_iota(jnp.int32, shape, len(shape) - 1)


def rows_of(shape):
    return lax.broadcasted_iota(jnp.int32, shape, len(shape) - 2)


def even(value):
    return lax.rem(value, 2) == 0


def takes(microseconds):
    return pl.CostEstimate(flops=0, bytes_accessed=int(microseconds * 3.69e6), transcendentals=0)


def ask_kernel(gx_count, route, within, xshift, ref, deformed, m0, m1, m2, m3, thick, own, place):
    gx, gy = lax.axis_index("gx"), lax.axis_index("gy")
    gx_even, gy_even, half_even = even(gx), even(gy), even(gy // 2)
    row, lane = rows_of((8, 128)), lanes((8, 128))
    wide = (8, NEL)
    offset = jnp.broadcast_to(route[...], wide) - SPAN
    moved = jnp.clip(gx + jnp.broadcast_to(xshift[...], wide) - 1, 0, gx_count - 1) - gx
    ahead = jnp.where(gx_even, 1, 2)
    bank = jnp.where(moved == 0, 0, jnp.where(moved == 1, ahead, 3 - ahead))
    code = bank * NEL + lanes(wide) // EYD * EYD + jnp.broadcast_to(within[...], wide)
    plus = jnp.where(gy_even, 0, 1)
    twice = jnp.where(half_even, 2, 3)
    j = jnp.where(offset == 1, plus, jnp.where(offset == -1, 1 - plus, jnp.where(offset == 2, twice, 5 - twice)))
    j = jnp.where(offset == 0, 4, j)
    mine = (rows_of(wide) == j).astype(F32)
    square = (NEL, NEL)
    earlier = (rows_of(square) < lanes(square)).astype(F32).astype(BF16)
    ahead_of = jnp.dot(mine.astype(BF16), earlier, preferred_element_type=F32)
    slot = jnp.sum(mine * ahead_of, axis=0, keepdims=True)
    order = jnp.full(wide, 4, jnp.int32)
    for at, kind in enumerate(KINDS):
        order = jnp.where(j == kind, at, order)
    found = jnp.where(rows_of(wide) == lanes(wide) // EYD, order.astype(F32) * 8.0 + slot, 0.0)
    long = (NEL, 128)
    widen = (lax.rem(rows_of(long), EYD) == lanes(long) // EDGE).astype(F32).astype(BF16)
    found = jnp.dot(found.astype(BF16), widen, preferred_element_type=F32)
    place[...] = found.astype(jnp.int32) * EDGE + lax.rem(lane, EDGE)
    tall = (128, NEL)
    taken = (rows_of(tall) == jnp.broadcast_to(slot, tall).astype(jnp.int32)).astype(F32).astype(BF16)
    asked = lax.dot_general(
        (mine * code.astype(F32)).astype(BF16), taken, (((1,), (1,)), ((), ())), preferred_element_type=F32
    )
    own[...] = asked
    m2[...] = asked
    m3[...] = asked
    m0[8:, :] = asked
    m1[8:, :] = asked
    image = ref[...]
    first = jnp.where(gy_even, NY - 1, 0)
    wanted = jnp.where(row == 0, first, jnp.where(row == 1, NY - 1 - first, -1))
    pick = (lane == wanted).astype(F32).astype(BF16)
    columns = lax.dot_general(pick, image.reshape(NZ * EDGE, NY), (((1,), (1,)), ((), ())), preferred_element_type=F32)
    for i in range(8):
        m0[i : i + 1, :] = columns[0:1, i * 128 : (i + 1) * 128]
        m1[i : i + 1, :] = columns[1:2, i * 128 : (i + 1) * 128]
    thick[0:NZ] = deformed[...]
    image = image.astype(F32)
    for k, face in enumerate((image[:, 0, :], image[:, EDGE - 1, :])):
        thick[NZ + k * EZ : NZ + (k + 1) * EZ] = face.astype(BF16).reshape(EZ, EDGE, NY)


def ask(route, within, xshift, ref, deformed):
    smem = pl.BlockSpec(memory_space=pltpu.SMEM)
    vmem = pl.BlockSpec(memory_space=pltpu.VMEM)
    return pl.pallas_call(
        functools.partial(ask_kernel, lax.axis_size("gx")),
        out_shape=(
            jax.ShapeDtypeStruct((16, 128), F32),
            jax.ShapeDtypeStruct((16, 128), F32),
            jax.ShapeDtypeStruct((8, 128), F32),
            jax.ShapeDtypeStruct((8, 128), F32),
            jax.ShapeDtypeStruct((NZ + 2 * EZ, EDGE, NY), BF16),
            jax.ShapeDtypeStruct((8, 128), F32),
            jax.ShapeDtypeStruct((8, 128), jnp.int32),
        ),
        in_specs=[vmem] * 5,
        out_specs=(vmem,) * 7,
        cost_estimate=takes(2.0),
        name="ask",
    )(route, within, xshift, ref, deformed)


def gather_columns(table, slabs, sources, places):
    table[...] = jnp.zeros_like(table)
    shape = (EDGE, NY)
    row, lane = rows_of(shape), lanes(shape)
    for i, (source, place) in enumerate(zip(sources, places)):
        start = pl.multiple_of(i * NY + source * EDGE, EDGE)
        table[pl.ds(start, EDGE), :] = (lane == row + place * EDGE).astype(F32).astype(BF16)
    return jnp.dot(jnp.concatenate(slabs, axis=1), table[...], preferred_element_type=F32)


def serve_kernel(lines, *refs):
    count = len(lines)
    asked, outs = refs[3 : 3 + count], refs[3 + count : 3 + 2 * count]
    banks, tables, codes, scalars, sem = refs[3 + 2 * count :]
    for j in range(count):
        codes[j] = asked[j][lines[j] // 8 * 8 : lines[j] // 8 * 8 + 8].astype(jnp.int32)
    copy = pltpu.make_async_copy(codes, scalars, sem)
    copy.start()
    for i in range(3):
        banks[i] = refs[i][0:NZ]
    copy.wait()
    for j in range(count):
        slabs, columns = [], []
        for slot in range(8):
            code = scalars[j, lines[j] % 8, slot]
            start = jnp.bitwise_and(code, NEL - EYD) * (EDGE // EYD)
            slab = banks[lax.shift_right_logical(code, 5), pl.ds(start, EDGE)]
            slabs.append(slab.reshape(EDGE * EDGE, NY))
            columns.append(jnp.bitwise_and(code, EYD - 1))
        packed = gather_columns(tables.at[j], slabs, columns, range(8))
        outs[j][...] = packed.reshape(EDGE, EDGE, NY).astype(BF16)


def serve(own, d0, d1, asked, lines):
    vmem = pl.BlockSpec(memory_space=pltpu.VMEM)
    count = len(lines)
    return pl.pallas_call(
        functools.partial(serve_kernel, lines),
        out_shape=(jax.ShapeDtypeStruct((EDGE, EDGE, NY), BF16),) * count,
        in_specs=[vmem] * 3 + [vmem] * count,
        out_specs=(vmem,) * count,
        scratch_shapes=[
            pltpu.VMEM((3, NZ, EDGE, NY), BF16),
            pltpu.VMEM((count, 8 * NY, NY), BF16),
            pltpu.VMEM((count, 8, 128), jnp.int32),
            pltpu.SMEM((count, 8, 128), jnp.int32),
            pltpu.SemaphoreType.DMA,
        ],
        compiler_params=pltpu.CompilerParams(vmem_limit_bytes=LIMIT),
        cost_estimate=takes(1.0 + 0.2 * count),
        name="serve",
    )(own, d0, d1, *asked)


def moments_kernel(gy_count, r0, r1, a1, a0, ref, frac, grad, packed, extra, portions, side, slabs):
    gx, gy = lax.axis_index("gx"), lax.axis_index("gy")
    gx_even, gy_even = even(gx), even(gy)
    side[...] = jnp.zeros((8, NZ * EDGE), F32)
    keep0 = jnp.where(gy_even, gy < gy_count - 1, gy > 0).astype(F32)
    keep1 = jnp.where(gy_even, gy > 0, gy < gy_count - 1).astype(F32)
    for i in range(8):
        side[0:1, i * 128 : (i + 1) * 128] = r0[i : i + 1, :] * keep0
        side[1:2, i * 128 : (i + 1) * 128] = r1[i : i + 1, :] * keep1
    row, lane = rows_of((8, 128)), lanes((8, 128))
    target0 = jnp.where(gy_even, NY - 1, 0)
    spot = jnp.where(row == 0, target0, jnp.where(row == 1, NY - 1 - target0, -1))
    spread = (lane == spot).astype(F32).astype(BF16)
    rim = lax.dot_general(
        side[...].astype(BF16), spread, (((0,), (0,)), ((), ())), preferred_element_type=F32
    ).reshape(NZ, EDGE, NY)
    low0, high0, low1, high1 = (
        thick[NZ + k * EZ : NZ + (k + 1) * EZ].astype(F32).reshape(NZ, NY) for thick in (a0, a1) for k in range(2)
    )
    before = jnp.where(gx_even, high1, high0)
    after = jnp.where(gx_even, low0, low1)
    lane2, row2 = lanes((EDGE, NY)), rows_of((EDGE, NY))

    def slopes(z):
        plane = ref[z].astype(F32)
        below = ref[z - 1].astype(F32) if z > 0 else jnp.zeros((EDGE, NY), F32)
        above = ref[z + 1].astype(F32) if z + 1 < NZ else jnp.zeros((EDGE, NY), F32)
        rim_z = rim[z]
        nxt = jnp.where(row2 == EDGE - 1, after[z : z + 1, :], pltpu.roll(plane, EDGE - 1, 0))
        prv = jnp.where(row2 == 0, before[z : z + 1, :], pltpu.roll(plane, 1, 0))
        right = jnp.where(lane2 == NY - 1, rim_z, pltpu.roll(plane, NY - 1, 1))
        left = jnp.where(lane2 == 0, rim_z, pltpu.roll(plane, 1, 1))
        rounded = [(value * 0.5).astype(BF16) for value in (above - below, nxt - prv, right - left)]
        for c in range(3):
            grad[c, z] = rounded[c]
        return [value.astype(F32) for value in rounded]

    for ez in range(EZ):
        sums = [[jnp.zeros((EDGE, NY), F32) for _ in range(3)] for _ in PAIRS]
        for k in range(EDGE // 2):
            both = [slopes(ez * EDGE + k), slopes(ez * EDGE + EDGE - 1 - k)]
            away = float(0.5 - UPPER[k])
            for p, (c, d) in enumerate(PAIRS):
                low, high = (g[c] * g[d] for g in both)
                even_part, odd_part = low + high, high - low
                sums[p][0] = sums[p][0] + even_part
                sums[p][1] = sums[p][1] + away * odd_part
                sums[p][2] = sums[p][2] + (away * away) * even_part
        for p in range(len(PAIRS)):
            quarter, first, second = sums[p][0] * 0.25, sums[p][1], sums[p][2]
            for w, value in enumerate((quarter - first + second, quarter - second, quarter + first + second)):
                start = (ez * 18 + p * 3 + w) * EDGE
                slabs[start : start + EDGE, :] = value
    found = weighed(slabs[...], along_y(hat_product, (0, 1, 2)))
    across = [hat_product(w, row2) for w in range(3)]
    row8, group8 = rows_of((8, 128)), lanes((8, 128)) // NEL
    tiles = [jnp.zeros((8, 128), F32) for _ in range(HROWS // 8 + 1)]
    for slab in range(18):
        for w in range(3):
            line = layered(found, slab, 18, across[w])
            source = slab * 3 + w
            if source < HROWS:
                tiles[source // 8] = jnp.where((row8 == source % 8) & (group8 < 3), line, tiles[source // 8])
            else:
                for wy in range(3):
                    spare = wy * 14 + source - HROWS
                    turned = pltpu.roll(line, (3 - wy) * NEL, 1)
                    tiles[spare // 8] = jnp.where((row8 == spare % 8) & (group8 == 3), turned, tiles[spare // 8])
    total = jnp.concatenate(tiles, axis=0)
    total = pltpu.roll(total, lax.rem(gx, 4) * NEL, 1)
    packed[...] = total[:HROWS]
    line = pltpu.roll(total[HROWS:], NEL, 1)[0:1] + pltpu.roll(total[HROWS:], 2 * NEL, 1)[1:2]
    extra[...] = jnp.where(row == 3, line, 0.0)
    element, lane_e = rows_of((EYD, 128)), lanes((EYD, 128))
    unfold = (lane_e // EDGE == element).astype(F32).astype(BF16)
    for ez in range(EZ):
        tenths = frac[ez * EYD : (ez + 1) * EYD, :].astype(F32).astype(BF16)
        wide = lax.dot_general(tenths, unfold, (((0,), (0,)), ((), ())), preferred_element_type=F32)
        portions[ez, 0:3, :] = wide * (1.0 / EDGE)


def moments(ref, faces_x, faces_y, fractions):
    vmem = pl.BlockSpec(memory_space=pltpu.VMEM)
    return pl.pallas_call(
        functools.partial(moments_kernel, lax.axis_size("gy")),
        out_shape=(
            jax.ShapeDtypeStruct((3, NZ, EDGE, NY), BF16),
            jax.ShapeDtypeStruct((HROWS, 128), F32),
            jax.ShapeDtypeStruct((8, 128), F32),
            jax.ShapeDtypeStruct((EZ, 8, 128), F32),
        ),
        in_specs=[vmem] * 6,
        out_specs=(vmem,) * 4,
        scratch_shapes=[pltpu.VMEM((8, NZ * EDGE), F32), pltpu.VMEM((EZ * 18 * EDGE, NY), F32)],
        compiler_params=pltpu.CompilerParams(vmem_limit_bytes=LIMIT),
        cost_estimate=takes(2.2),
        name="moments",
    )(faces_y[0], faces_y[1], faces_x[1], faces_x[0], ref, fractions)


def warp_kernel(b0, b1, b2, b3, b4, place, ref, grad, portions, extra, mismatch, packed, slabs):
    gx = lax.axis_index("gx")
    flat = (EDGE * EDGE, NY)
    lane = lanes(flat)
    at_x_rim = lax.rem(lax.broadcasted_iota(jnp.int32, flat, 0), EDGE) == EDGE - 1
    at_y_rim = lax.rem(lane, EDGE) == EDGE - 1
    came = jnp.concatenate([block[...].reshape(flat) for block in (b0, b1, b2, b3, b4)], axis=1)
    table = (5 * NY, NY)
    fetched = []
    for half in range(2):
        spots = [jnp.broadcast_to(place[ez : ez + 1, :], table) for ez in (2 * half, 2 * half + 1)]
        moves = [(rows_of(table) == spot).astype(F32).astype(BF16) for spot in spots]
        fetched.append(jnp.dot(came, jnp.concatenate(moves, axis=1), preferred_element_type=F32))
    for ez in range(EZ):
        blended = fetched[ez // 2][:, ez % 2 * NY : (ez % 2 + 1) * NY]
        portion = portions[ez]
        ty, tx, tz = portion[2:3, :], portion[1:2, :], portion[0:1, :]
        shifted = jnp.where(at_y_rim, blended, pltpu.roll(blended, NY - 1, 1))
        blended = (1.0 - ty) * blended + ty * shifted
        shifted = jnp.where(at_x_rim, blended, pltpu.roll(blended, EDGE * EDGE - 1, 0))
        blended = (1.0 - tx) * blended + tx * shifted
        shifted = jnp.concatenate([blended[EDGE:], blended[-EDGE:]], axis=0)
        blended = (1.0 - tz) * blended + tz * shifted
        blended = blended.reshape(EDGE, EDGE, NY)
        sums = [[jnp.zeros((EDGE, NY), F32) for _ in range(2)] for _ in range(3)]
        for k in range(EDGE // 2):
            planes = (ez * EDGE + k, ez * EDGE + EDGE - 1 - k)
            aparts = [ref[z].astype(F32) - blended[z - ez * EDGE] for z in planes]
            for z, apart in zip(planes, aparts):
                mismatch[z] = apart
            for c in range(3):
                low, high = (grad[c, z].astype(F32) * apart for z, apart in zip(planes, aparts))
                sums[c][0] = sums[c][0] + (low + high)
                sums[c][1] = sums[c][1] + float(0.5 - UPPER[k]) * (high - low)
        for c in range(3):
            half, first = sums[c][0] * 0.5, sums[c][1]
            for a, value in enumerate((half - first, half + first)):
                start = (ez * 6 + c * 2 + a) * EDGE
                slabs[start : start + EDGE, :] = value
    found = weighed_once(slabs[...], along_y(lambda group, at: hat_weight(lax.rem(group, 2), at), (0, 1, 2, 3)))
    across = hat_weight(lanes((EDGE, 128)) // (2 * NEL), rows_of((EDGE, 128)))
    row, lane = rows_of((8, 128)), lanes((8, 128))
    group, in_z, in_y = lane // NEL, lax.rem(lane, NEL) // EYD, lax.rem(lane, EYD)
    total = jnp.zeros((8, 128), F32)
    for c in range(3):
        lower, upper = (layered(found, c * 2 + a, 6, across) for a in range(2))
        lower, upper = (jnp.broadcast_to(line, (8, 128)) for line in (lower, upper))
        level = lower + jnp.where(in_z > 0, pltpu.roll(upper, EYD, 1), 0.0)
        top = jnp.where(in_z == EZ - 1, upper, 0.0)

        def joined(line):
            return line + jnp.where(in_y > 0, pltpu.roll(line, 128 - NEL + 1, 1), 0.0)

        rim = jnp.where(in_y == EYD - 1, level, 0.0) + jnp.where(in_y == EYD - 2, pltpu.roll(top, 127, 1), 0.0)
        main = jnp.where(lax.rem(group, 2) == 0, joined(level), rim)
        total = jnp.where(row == c, main, total)
        top = joined(top)
        for bx in range(2):
            start = 2 * NEL + (c * 2 + bx) * EYD
            moved = pltpu.roll(top, (start - (bx * 2 * NEL + (EZ - 1) * EYD)) % 128, 1)
            total = jnp.where((row == 3) & (lane // EYD == start // EYD), moved, total)
    total = pltpu.roll(total, lax.rem(gx, 4) * NEL, 1) + extra[...]
    packed[...] = jnp.broadcast_to(total[0:4], packed.shape)


def warp(place, bricks, ref, grad, portions, extra):
    vmem = pl.BlockSpec(memory_space=pltpu.VMEM)
    devices = lax.axis_size("gx") * lax.axis_size("gy")
    return pl.pallas_call(
        warp_kernel,
        out_shape=(jax.ShapeDtypeStruct((NZ, EDGE, NY), F32), jax.ShapeDtypeStruct((devices, 4, 128), F32)),
        in_specs=[vmem] * 10,
        out_specs=(vmem, vmem),
        scratch_shapes=[
            pltpu.VMEM((EZ * 6 * EDGE, NY), F32),
        ],
        compiler_params=pltpu.CompilerParams(vmem_limit_bytes=LIMIT),
        cost_estimate=takes(4.0),
        name="warp",
    )(*bricks, place, ref, grad, portions, extra)


def spread_groups(block_of, groups, gx_count, store):
    tiles = -(-gx_count // 4)
    for tile in range(tiles):
        members = range(4 * tile, min(4 * tile + 4, gx_count))
        blocks = {gx: block_of(gx) for gx in members}
        for group in range(groups):
            merged = jnp.zeros_like(blocks[members[0]])
            lane = lanes(merged.shape)
            for gx in members:
                merged = jnp.where(lane // NEL == (group + gx) % 4, blocks[gx], merged)
            store(group, tile, pltpu.roll(merged, (128 - NEL * group) % 128, 1) if group else merged)


def solve_kernel(gx_count, gy_count, hess, load, out, coef, rhs):
    gx, gy = lax.axis_index("gx"), lax.axis_index("gy")
    steps = gather_steps(gx_count, gy_count)
    tiles = -(-gx_count // 4)
    width = 128 * tiles

    def unpack(row, _):
        def hess_block(column):
            relative = dict(gx=jnp.bitwise_xor(gx, column), gy=jnp.bitwise_xor(gy, row))
            return hess[block_index(steps, relative)]

        def store_hess(group, tile, value):
            coef[tile, pl.ds(group * HROWS * gy_count + row, HROWS, stride=gy_count), :] = value

        def load_block(column):
            return load[column * gy_count + row]

        def store_load(group, tile, value):
            rhs[tile, pl.ds(row * 16 + group * 4, 4), :] = value

        spread_groups(hess_block, 4, gx_count, store_hess)
        spread_groups(load_block, 4, gx_count, store_load)
        return 0

    lax.fori_loop(0, gy_count, unpack, 0, unroll=8)
    shape = (gy_count, width)
    lane, row = lanes(shape), rows_of(shape)
    in_z, in_y, in_x = lax.rem(lane, NEL) // EYD, lax.rem(lane, EYD), lane // NEL
    last_z, first_z = in_z == EZ - 1, in_z == 0
    last_x, first_x = in_x >= gx_count - 1, in_x == 0
    last_y, first_y = in_y == EYD - 1, in_y == 0
    end_y, begin_y = last_y & (row == gy_count - 1), first_y & (row == 0)

    bits = [(a, b, d) for a in range(2) for b in range(2) for d in range(2)]

    def turn(value, by, axis):
        size = shape[axis]
        by = by % size
        return pltpu.roll(value, by, axis) if by else value

    def corners(main, top):
        main_next, top_next = turn(main, -1, 0), turn(top, -1, 0)
        found = []
        for a, b, d in bits:

            def reached(main, top, by):
                value = turn(main, -(EYD * a + NEL * b + by), 1)
                return jnp.where(last_z, turn(top, -(NEL * b + by), 1), value) if a else value

            value = reached(main, top, d)
            if d:
                wrapped = jnp.where(end_y, 0.0, reached(main_next, top_next, 1 - EYD))
                value = jnp.where(last_y, wrapped, value)
            found.append(jnp.where(last_x, 0.0, value) if b else value)
        return found

    def settle(parts):
        main, top = None, None
        for (a, b, d), part in zip(bits, parts):
            before = turn(part, 1, 0) if d else None

            def given(by):
                value = turn(part, by + d, 1)
                if d:
                    wrapped = jnp.where(begin_y, 0.0, turn(before, by + 1 - EYD, 1))
                    value = jnp.where(first_y, wrapped, value)
                return jnp.where(first_x, 0.0, value) if b else value

            value = given(EYD * a + NEL * b)
            value = jnp.where(first_z, 0.0, value) if a else value
            main = value if main is None else main + value
            if a:
                value = given(NEL * b)
                top = value if top is None else top + value
        return main, jnp.where(last_z, top, 0.0)

    def strided(ref, start, stride):
        found = [ref[tile, pl.ds(start, gy_count, stride=stride), :] for tile in range(tiles)]
        return found[0] if tiles == 1 else jnp.concatenate(found, axis=1)

    def held(ref, index):
        found = [ref[tile, index * gy_count : (index + 1) * gy_count, :] for tile in range(tiles)]
        return found[0] if tiles == 1 else jnp.concatenate(found, axis=1)

    def channel(p, wz, wx, wy):
        source = (p * 3 + wz) * 3 + wx
        if source < HROWS:
            return held(coef, wy * HROWS + source)
        spare = wy * 14 + source - HROWS
        if spare < HROWS:
            return held(coef, 3 * HROWS + spare)
        return strided(rhs, (spare - HROWS) * 4 + 3, 16)

    pair_of = {}
    for p, (c, d) in enumerate(PAIRS):
        pair_of[c, d] = pair_of[d, c] = p

    def curved_by(vector):
        known = [corners(main, top) for main, top in vector]
        sums = [[None] * 8 for _ in range(3)]

        def add(c, n, term):
            sums[c][n] = term if sums[c][n] is None else sums[c][n] + term

        for p, (c, d) in enumerate(PAIRS):
            for wz in range(3):
                for wx in range(3):
                    for wy in range(3):
                        factor = channel(p, wz, wx, wy)
                        for n, low in enumerate(bits):
                            for m, high in enumerate(bits):
                                if (low[0] + high[0], low[1] + high[1], low[2] + high[2]) == (wz, wx, wy):
                                    add(c, n, factor * known[d][m])
                                    if c != d:
                                        add(d, n, factor * known[c][m])
        result = []
        for c in range(3):
            main, top = settle(sums[c])
            result.append((main + LAMBDA * vector[c][0], top + LAMBDA * vector[c][1]))
        terms = [known[c][n] * sums[c][n] for c in range(3) for n in range(8)]
        terms += [LAMBDA * (part * part) for pair in vector for part in pair]
        while len(terms) > 1:
            terms = [sum(terms[i : i + 2]) for i in range(0, len(terms), 2)]
        return result, total(terms[0])

    def total(value):
        return jnp.sum(jnp.sum(value, axis=0, keepdims=True), axis=1, keepdims=True)

    def inner(one, two):
        return total(sum(a[0] * b[0] + a[1] * b[1] for a, b in zip(one, two)))

    def combine(one, factor, two):
        return [(a[0] + factor * b[0], a[1] + factor * b[1]) for a, b in zip(one, two)]

    residual = []
    for c in range(3):
        main, top = None, None
        for bx in range(2):
            inside = strided(rhs, 2 * bx * 4 + c, 16)
            rim = turn(strided(rhs, (2 * bx + 1) * 4 + c, 16), 1, 0)
            spot = c * 2 + bx
            upper = strided(rhs, (2 + spot // 4) * 4 + 3, 16)
            upper = jnp.where(last_z, turn(upper, (EZ - 1 - spot % 4) * EYD, 1), 0.0)
            reached = first_y & (row > 0)
            inside = inside + jnp.where(reached, turn(rim, 1 - EYD, 1), 0.0)
            upper = upper + jnp.where(reached & last_z, turn(rim, 2 - EYD, 1), 0.0)
            if bx:
                main = main + jnp.where(first_x, 0.0, turn(inside, NEL, 1))
                top = top + jnp.where(first_x, 0.0, turn(upper, NEL, 1))
            else:
                main, top = inside, upper
        residual.append((main, top))
    direction = residual
    increment = None
    norm_now = inner(residual, residual)
    for iteration in range(ITERS):
        curved, bent = curved_by(direction)
        step = norm_now / bent
        if increment is None:
            increment = [(step * a, step * b) for a, b in direction]
        else:
            increment = combine(increment, step, direction)
        if iteration + 1 < ITERS:
            residual = combine(residual, -step, curved)
            norm_next = inner(residual, residual)
            direction = combine(residual, norm_next / norm_now, direction)
            norm_now = norm_next
    mine = (row == gy) & (in_x == gx)
    for c in range(3):
        for part, levels in ((increment[c][0], range(EZ)), (increment[c][1], [EZ])):
            line = jnp.sum(jnp.where(mine, part, 0.0), axis=0, keepdims=True)
            short = line[:, 0:128]
            for tile in range(1, tiles):
                short = short + line[:, tile * 128 : (tile + 1) * 128]
            short = pltpu.roll(jnp.broadcast_to(short, (8, 128)), lax.rem(128 - lax.rem(gx, 4) * NEL, 128), 1)
            for level in levels:
                start = min(level, EZ - 1) * EYD
                out[c, level] = short[0:1, start : start + EYD]


def solve(hess, load):
    gx_count, gy_count = lax.axis_size("gx"), lax.axis_size("gy")
    tiles = -(-gx_count // 4)
    vmem = pl.BlockSpec(memory_space=pltpu.VMEM)
    return pl.pallas_call(
        functools.partial(solve_kernel, gx_count, gy_count),
        out_shape=jax.ShapeDtypeStruct((3, EZ + 1, 1, EYD), F32),
        in_specs=[vmem] * 2,
        out_specs=vmem,
        scratch_shapes=[
            pltpu.VMEM((tiles, gy_count * 4 * HROWS, 128), F32),
            pltpu.VMEM((tiles, gy_count * 16, 128), F32),
        ],
        compiler_params=pltpu.CompilerParams(vmem_limit_bytes=LIMIT),
        cost_estimate=takes(3.5),
        name="solve",
    )(hess, load)


def swap(array, axis, partner):
    size = lax.axis_size(axis)
    pairs = [(i, partner(i)) for i in range(size)]
    return lax.ppermute(array, axis, [(i, j) for i, j in pairs if 0 <= j < size])


def swap_x(array, kind):
    if kind == 0:
        return swap(array, "gx", lambda i: i ^ 1)
    return swap(array, "gx", lambda i: i + 1 if i % 2 else i - 1)


def swap_y(array, kind):
    size = lax.axis_size("gy")
    partner = (
        lambda i: i ^ 1,
        lambda i: (i + 1 if i % 2 else i - 1) % size,
        lambda i: i ^ 2,
        lambda i: (i + 2 if i // 2 % 2 else i - 2) % size,
    )[kind]
    return swap(array, "gy", partner)


def gather_steps(gx_count, gy_count):
    far = [("gy", 1 << k) for k in range(1, gy_count.bit_length() - 1)]
    return [*far, ("gy", 1), *[("gx", 1 << k) for k in reversed(range(gx_count.bit_length() - 1))]]


def block_index(steps, relative):
    found = 0
    for k, (axis, bit) in enumerate(steps):
        found = found + jnp.where(jnp.bitwise_and(relative[axis], bit) != 0, 1 << k, 0)
    return found


def swapped(known, step):
    axis, bit = step
    return swap(known, axis, lambda j: j ^ bit)


def doubled(known, step):
    return jnp.concatenate([known, swapped(known, step)], axis=0)


def body(reference_image, deformed_image, route, within, xshift, fractions):
    m0, m1, m2, m3, thick, own, place = ask(
        route.reshape(1, NEL), within.reshape(1, NEL), xshift.reshape(1, NEL), reference_image, deformed_image
    )
    asks = (m0, m1, m2, m3)
    q = {kind: swap_y(asks[kind], kind) for kind in KINDS}
    d1, d0 = swap_x(thick, 1), swap_x(thick, 0)
    grad, packed, extra, portions = moments(reference_image, (d0, d1), (q[0], q[1]), fractions.reshape(NEL, 3))
    q[3], q[0], q[1], q[2], packed = lax.optimization_barrier((q[3], q[0], q[1], q[2], packed))
    *served, at_home = serve(deformed_image, d0, d1, [q[kind] for kind in KINDS] + [own], [8 * (k < 2) + k for k in KINDS] + [4])
    known = packed[None]
    bricks = [swap_y(block, kind) for kind, block in zip(KINDS, served)] + [at_home]
    steps = gather_steps(lax.axis_size("gx"), lax.axis_size("gy"))
    for k, step in enumerate(steps[:-3]):
        if k == 1:
            known, at_home = lax.optimization_barrier((known, at_home))
        known = doubled(known, step)
    bricks[-1] = at_home
    bricks, known = lax.optimization_barrier((bricks, known))
    mismatch, part = warp(place, bricks, reference_image, grad, portions, extra)
    beside, across = swapped(known, steps[-3]), swapped(known, steps[-2])
    known, beside, across, _ = lax.optimization_barrier((known, beside, across, part))
    load = lax.all_to_all(part, ("gx", "gy"), 0, 0)
    blocks = [known, beside, across, swapped(beside, steps[-2])]
    blocks = blocks + [swapped(block, steps[-1]) for block in blocks]
    return solve(jnp.concatenate(blocks, axis=0), load), mismatch


def solution(mesh):
    placed = (
        P(None, "gx", "gy"),
        P(None, "gx", "gy"),
        P("gx", "gy", None, None),
        P("gx", "gy", None),
        P("gx", "gy", None),
        P("gx", "gy", None, None),
    )
    return jax.shard_map(
        body,
        mesh=mesh,
        in_specs=placed,
        out_specs=(P(None, None, "gx", "gy"), P(None, "gx", "gy")),
        check_vma=False,
    )
```
